32 devices in a mesh: freq: 2 (over y), src: 4 (over z), rcv: 4 (over x, core).
Axes of the slice: x: 2, y: 2, z: 4, core: 2. Of those that a mesh axis runs over, the one named last changes fastest.
Arguments:
- primaries: bfloat16 [4, 2, 1024, 3072], P('freq', None, 'src', 'rcv'), parts along dimension 0, may hold values from -0.078125 to 0.078125
- data: bfloat16 [4, 2, 1024, 1024], P('freq', None, 'src', 'rcv'), parts along dimension 0, may hold values from -6 to 6
- aperture: int32 [4, 12], replicated, may hold values from 0 to 3, as said below
Outputs:
- multiples: float32 [4, 2, 1024, 1024], P('freq', None, 'src', 'rcv'), parts along dimension 0
The draws below stay inside these ranges and needn't reach their ends.
There are 2 independent parts, one for each index of `freq`. The reference program is written for one: setup_inputs(seed, part) draws one part's arguments, and reference() takes and returns one part's arrays. A program takes and returns all parts, laid end to end along the dimension named above; an argument that names none is the same for every part. Nothing has to cross between parts.
Inputs may be any that keep to these rules, and one draw needn't show every extreme that they name: aperture[b, a] lies within 6 blocks of b; entries of a row may repeat; in every draw some row names both b - 6 and b + 6, where these exist.
All inputs are finite; a program needn't handle non-finite values.
Results may differ from the reference program's by a relative error of at most 0.0003.
Values may be sent and summed in bfloat16 or wider, within the bound.
No kernel may reach another device: no remote copies, remote signals or barrier semaphores. Data moves between devices by JAX's collectives and lax.ppermute only.
A program may use at most 128 MiB of HBM per device.

```python
import jax
import jax.numpy as jnp
from jax import lax

BLK = 256
APER = 12
HW = 6
NS = 1024
NB = 4
RWIN = 1024


def draw_aperture(key, part):
    key = jax.random.fold_in(key, 11)
    key_one, key_two, key_three = jax.random.split(key, 3)
    offsets = jax.random.randint(key_one, (NB, APER), -HW, HW + 1)
    low_slot = jax.random.randint(key_two, (), 0, APER // 2)
    high_slot = jax.random.randint(key_three, (), APER // 2, APER)
    centre = NB // 2
    offsets = offsets.at[centre, low_slot].set(-HW)
    offsets = offsets.at[centre, high_slot].set(HW)
    blocks = jnp.arange(NB, dtype=jnp.int32)[:, None] + offsets
    return jnp.clip(blocks, 0, NB - 1).astype(jnp.int32)


def levels(key, extent, pieces, least, largest):
    level = 1.0
    for position, blocks in pieces:
        draws = jax.random.uniform(jax.random.fold_in(jax.random.fold_in(key, 6), position), (blocks,), jnp.float32, least / len(pieces), largest / len(pieces))
        level = level * jnp.repeat(jnp.exp(draws), extent[position] // blocks).reshape((-1,) + (1,) * (len(extent) - 1 - position))
    return level


def centred(own_key, dims, width, limit, shards=(), held_as=jnp.bfloat16):
    array = jax.random.normal(own_key, dims, jnp.float32) * width
    if len(shards) > 0:
        array = levels(own_key, dims, shards, -0.22, 0.18) * array
    return jnp.clip(array, min=-limit, max=limit).astype(held_as)


def setup_inputs(seed: int = 0, part: int = 0) -> dict:
    key_of = jax.random.split(jax.random.key(seed), 4)
    own_keys = jax.random.split(jax.random.fold_in(key_of[3], part), 4)
    return {
        "primaries": centred(own_keys[0], (2, 2, NS, APER * BLK), (2 * APER * BLK) ** -0.5, 0.078125, ((2, 4), (3, 4))),
        "data": centred(own_keys[1], (2, 2, NS, RWIN), 1.0, 6.0, ((2, 4), (3, 4))),
        "aperture": draw_aperture(jax.random.fold_in(key_of[3], 71), part),
    }


def reference(primaries, data, aperture):
    data_blocks = data.reshape(2, 2, NB, BLK, RWIN)
    panel_blocks = primaries.reshape(2, 2, NB, BLK, APER * BLK)

    def one_block(inputs):
        block_index, aperture_row = inputs
        panel = lax.dynamic_index_in_dim(panel_blocks, block_index, 2, keepdims=False).astype(jnp.float32)
        picked = jnp.take(data_blocks, aperture_row, axis=2).reshape(2, 2, APER * BLK, RWIN)
        picked = picked.astype(jnp.float32)
        real_part = jnp.einsum("sxc,scr->sxr", panel[:, 0], picked[:, 0], precision=lax.Precision.HIGHEST)
        real_part = real_part - jnp.einsum("sxc,scr->sxr", panel[:, 1], picked[:, 1], precision=lax.Precision.HIGHEST)
        imag_part = jnp.einsum("sxc,scr->sxr", panel[:, 0], picked[:, 1], precision=lax.Precision.HIGHEST)
        imag_part = imag_part + jnp.einsum("sxc,scr->sxr", panel[:, 1], picked[:, 0], precision=lax.Precision.HIGHEST)
        return jnp.stack([real_part, imag_part], axis=1)

    results = lax.map(one_block, (jnp.arange(NB, dtype=jnp.int32), aperture.astype(jnp.int32)))
    return results.transpose(1, 2, 0, 3, 4).reshape(2, 2, NS, RWIN)
```

```python
import functools

import jax
import jax.numpy as jnp
from jax import lax
from jax.experimental import pallas as pl
from jax.experimental.pallas import tpu as pltpu
from jax.sharding import PartitionSpec as P

BLK = 256
APER = 12
HW = 6


def from_behind(x, axis, by):
    peers = lax.axis_size(axis)
    pairs = [(i, i + by) for i in range(peers) if 0 <= i + by < peers]
    return lax.ppermute(x, axis, pairs)


def swap(x, axis, bit):
    peers = lax.axis_size(axis)
    return lax.ppermute(x, axis, [(i, i ^ bit) for i in range(peers)])


def gather_window(data):
    axis_count = lax.axis_size("src")
    if axis_count <= 2 * HW + 1:
        return lax.all_gather(data, "src", axis=0, tiled=False), False
    pieces = [data if off == 0 else from_behind(data, "src", -off) for off in range(-HW, HW + 1)]
    return jnp.stack(pieces, axis=0), True


def gather_panels(primaries):
    peers = lax.axis_size("rcv")
    panels = {0: primaries}
    bit = peers // 2
    while bit >= 1:
        for m in list(panels):
            panels[m ^ bit] = swap(panels[m], "rcv", bit)
        bit //= 2
    return [panels[m] for m in range(peers)]


def kernel(relative, per_shard, aperture_ref, *refs):
    *panel_refs, window_ref, out_ref = refs
    block = lax.axis_index("src")
    me = lax.axis_index("rcv")
    first = block - HW if relative else 0
    real = None
    imag = None
    for m, panel_ref in enumerate(panel_refs):
        shard = lax.bitwise_xor(me, m)
        rows = [aperture_ref[block, shard * per_shard + q] - first for q in range(per_shard)]
        data_re = jnp.concatenate([window_ref[row, 0, 0] for row in rows], axis=0)
        data_im = jnp.concatenate([window_ref[row, 0, 1] for row in rows], axis=0)
        panel_re = panel_ref[0, 0]
        panel_im = panel_ref[0, 1]
        dot = functools.partial(jnp.dot, preferred_element_type=jnp.float32)
        re = dot(panel_re, data_re) - dot(panel_im, data_im)
        im = dot(panel_re, data_im) + dot(panel_im, data_re)
        real = re if real is None else real + re
        imag = im if imag is None else imag + im
    out_ref[0, 0] = real
    out_ref[0, 1] = imag


def body(primaries, data, aperture):
    surveys = primaries.shape[0]
    columns = primaries.shape[3]
    width = data.shape[3]
    window, relative = gather_window(data)
    panels = gather_panels(primaries)
    depth = window.shape[0]
    return pl.pallas_call(
        functools.partial(kernel, relative, columns // BLK),
        grid=(surveys,),
        out_shape=jax.ShapeDtypeStruct((surveys, 2, BLK, width), jnp.float32),
        in_specs=[pl.BlockSpec(memory_space=pltpu.SMEM)]
        + [pl.BlockSpec((1, 2, BLK, columns), lambda v: (v, 0, 0, 0)) for _ in panels]
        + [pl.BlockSpec((depth, 1, 2, BLK, width), lambda v: (0, v, 0, 0, 0))],
        out_specs=pl.BlockSpec((1, 2, BLK, width), lambda v: (v, 0, 0, 0)),
        compiler_params=pltpu.CompilerParams(vmem_limit_bytes=40 * 1024 * 1024),
        cost_estimate=pl.CostEstimate(
            flops=8 * surveys * BLK * BLK * APER * width, bytes_accessed=9 << 20, transcendentals=0
        ),
    )(aperture, *panels, window)


def solution(mesh):
    placed = (P("freq", None, "src", "rcv"), P("freq", None, "src", "rcv"), P())
    return jax.shard_map(
        body, mesh=mesh, in_specs=placed, out_specs=P("freq", None, "src", "rcv"), check_vma=False
    )
```

```python
import functools

import jax
import jax.numpy as jnp
from jax import lax
from jax.experimental import pallas as pl
from jax.experimental.pallas import tpu as pltpu
from jax.sharding import PartitionSpec as P

BLK = 256
APER = 12
HW = 6


def from_behind(x, axis, by):
    peers = lax.axis_size(axis)
    pairs = [(i, i + by) for i in range(peers) if 0 <= i + by < peers]
    return lax.ppermute(x, axis, pairs)


def swap(x, axis, bit):
    peers = lax.axis_size(axis)
    return lax.ppermute(x, axis, [(i, i ^ bit) for i in range(peers)])


def gather_window(parts):
    reach = min(HW, lax.axis_size("src") - 1)
    windows = [{0: part} for part in parts]
    for hop in range(1, reach + 1):
        for window in windows:
            window[-hop] = from_behind(window[1 - hop], "src", 1)
            window[hop] = from_behind(window[hop - 1], "src", -1)
    return [[window[distance] for distance in range(-reach, reach + 1)] for window in windows]


def gather_panels(parts):
    peers = lax.axis_size("rcv")
    gathered = [{0: part} for part in parts]
    bit = peers // 2
    while bit >= 1:
        for panels in gathered:
            for m in list(panels):
                panels[m ^ bit] = swap(panels[m], "rcv", bit)
        bit //= 2
    return [[panels[m] for m in range(peers)] for panels in gathered]


def kernel(survey, panel_count, piece_count, aperture_ref, *refs):
    panel_refs = refs[:panel_count]
    piece_refs = refs[panel_count : panel_count + piece_count]
    out_ref, panels, window, result, panel_sems, piece_sems, out_sem = refs[-7:]
    reach = piece_count // 2
    block = lax.axis_index("src")
    me = lax.axis_index("rcv")
    per_shard = panels.shape[-1] // BLK
    piece_copies = [
        pltpu.make_async_copy(ref, window.at[k], piece_sems.at[k]) for k, ref in enumerate(piece_refs)
    ]
    panel_copies = [
        pltpu.make_async_copy(ref, panels.at[m], panel_sems.at[m]) for m, ref in enumerate(panel_refs)
    ]
    for copy in piece_copies:
        copy.start()
    for copy in panel_copies:
        copy.start()
    for copy in piece_copies:
        copy.wait()
    dot = functools.partial(jnp.dot, preferred_element_type=jnp.float32)
    real = None
    imag = None
    for m in range(panel_count):
        shard = lax.bitwise_xor(me, m)
        rows = [aperture_ref[block, shard * per_shard + q] - block + reach for q in range(per_shard)]
        data_re = jnp.concatenate([window[row, 0, 0] for row in rows], axis=0)
        data_im = jnp.concatenate([window[row, 0, 1] for row in rows], axis=0)
        panel_copies[m].wait()
        panel_re = panels[m, 0, 0]
        panel_im = panels[m, 0, 1]
        re = dot(panel_re, data_re) - dot(panel_im, data_im)
        im = dot(panel_re, data_im) + dot(panel_im, data_re)
        real = re if real is None else real + re
        imag = im if imag is None else imag + im
    result[0] = real
    result[1] = imag
    out_copy = pltpu.make_async_copy(result, out_ref.at[survey], out_sem)
    out_copy.start()
    out_copy.wait()


def products(survey, surveys, aperture, panels, pieces, out):
    columns = panels[0].shape[-1]
    width = pieces[0].shape[-1]
    anywhere = pl.BlockSpec(memory_space=pl.ANY)
    operands = [aperture, *panels, *pieces]
    in_specs = [pl.BlockSpec(memory_space=pltpu.SMEM)] + [anywhere] * (len(panels) + len(pieces))
    aliases = {}
    if out is not None:
        aliases = {len(operands): 0}
        operands.append(out)
        in_specs.append(anywhere)
    return pl.pallas_call(
        functools.partial(kernel, survey, len(panels), len(pieces)),
        out_shape=jax.ShapeDtypeStruct((surveys, 2, BLK, width), jnp.float32),
        in_specs=in_specs,
        out_specs=anywhere,
        scratch_shapes=[
            pltpu.VMEM((len(panels), 1, 2, BLK, columns), jnp.bfloat16),
            pltpu.VMEM((len(pieces), 1, 2, BLK, width), jnp.bfloat16),
            pltpu.VMEM((2, BLK, width), jnp.float32),
            pltpu.SemaphoreType.DMA((len(panels),)),
            pltpu.SemaphoreType.DMA((len(pieces),)),
            pltpu.SemaphoreType.DMA,
        ],
        input_output_aliases=aliases,
        compiler_params=pltpu.CompilerParams(vmem_limit_bytes=24 * 1024 * 1024),
        cost_estimate=pl.CostEstimate(
            flops=8 * BLK * BLK * APER * width, bytes_accessed=5 << 20, transcendentals=0
        ),
    )(*operands)


def body(primaries, data, aperture):
    surveys = primaries.shape[0]
    panels = gather_panels([primaries[v : v + 1] for v in range(surveys)])
    windows = gather_window([data[v : v + 1] for v in range(surveys)])
    out = None
    for v in range(surveys):
        out = products(v, surveys, aperture, panels[v], windows[v], out)
    return out


def solution(mesh):
    placed = (P("freq", None, "src", "rcv"), P("freq", None, "src", "rcv"), P())
    return jax.shard_map(
        body, mesh=mesh, in_specs=placed, out_specs=P("freq", None, "src", "rcv"), check_vma=False
    )
```

```python
import functools

import jax
import jax.numpy as jnp
from jax import lax
from jax.experimental import pallas as pl
from jax.experimental.pallas import tpu as pltpu
from jax.sharding import PartitionSpec as P

BLK = 256
APER = 12
HW = 6


def from_behind(x, axis, by):
    peers = lax.axis_size(axis)
    pairs = [(i, i + by) for i in range(peers) if 0 <= i + by < peers]
    return lax.ppermute(x, axis, pairs)


def swap(x, axis, bit):
    peers = lax.axis_size(axis)
    return lax.ppermute(x, axis, [(i, i ^ bit) for i in range(peers)])


def after(value, *earlier):
    return lax.optimization_barrier((value, *earlier))[0]


def line_window(data):
    peers = lax.axis_size("src")
    at_end = (lax.axis_index("src") + 1) % peers < 2
    far = lax.ppermute(data, "src", [(0, 3), (1, 2), (2, 1), (3, 0)])
    near = lax.ppermute(data, "src", [(0, 1), (1, 0), (2, 3), (3, 2)])
    onward = jnp.where(at_end, data, far)
    return [
        [(data, v), (near, v), (lax.ppermute(onward[v : v + 1], "src", [(0, 2), (2, 3), (3, 1), (1, 0)]), 0), (far, v)]
        for v in range(data.shape[0])
    ]


def hop_window(data):
    reach = min(HW, lax.axis_size("src") - 1)
    window = {0: data}
    for hop in range(1, reach + 1):
        window[-hop] = from_behind(window[1 - hop], "src", 1)
        window[hop] = from_behind(window[hop - 1], "src", -1)
    return [[(window[distance], v) for distance in range(-reach, reach + 1)] for v in range(data.shape[0])]


def gather_panels(primaries, windows):
    peers = lax.axis_size("rcv")
    whole = {0: primaries}
    bit = 1
    while bit < peers // 2:
        for m in list(whole):
            whole[m ^ bit] = swap(whole[m], "rcv", bit)
        bit *= 2
    panels = []
    for v in range(primaries.shape[0]):
        own = primaries[v : v + 1]
        if v > 0:
            own = after(primaries, whole[1])[v : v + 1]
        found = {bit: swap(own, "rcv", bit)}
        handed = found[bit]
        if v > 0:
            handed = after(handed, *[piece for window in windows for piece, _ in window])
        for lower in range(1, bit):
            last = lower & (lower - 1)
            found[bit ^ lower] = swap(found[bit ^ last] if last else handed, "rcv", lower & -lower)
        panels.append([(whole[m], v) for m in range(bit)] + [(found[m], 0) for m in range(bit, peers)])
    return panels


def window_slot(block, wanted, peers, reach):
    return lax.bitwise_xor(block, wanted) if peers == 4 else wanted - block + reach


def kernel(survey, panel_at, piece_at, aperture_ref, *refs):
    panel_count, piece_count = len(panel_at), len(piece_at)
    panel_refs = [ref.at[v] for ref, v in zip(refs, panel_at)]
    piece_refs = [ref.at[v] for ref, v in zip(refs[panel_count:], piece_at)]
    out_ref, window, result, piece_sems, out_sems = refs[-5:]
    block = lax.axis_index("src")
    me = lax.axis_index("rcv")
    per_shard = panel_refs[0].shape[-1] // BLK
    copies = [
        pltpu.make_async_copy(ref, window.at[k], piece_sems.at[k]) for k, ref in enumerate(piece_refs)
    ]
    for copy in copies:
        copy.start()
    slots = []
    for m in range(panel_count):
        shard = lax.bitwise_xor(me, m)
        wanted = [aperture_ref[block, shard * per_shard + q] for q in range(per_shard)]
        slots.append([window_slot(block, w, lax.axis_size("src"), piece_count // 2) for w in wanted])
    for copy in copies:
        copy.wait()
    dot = functools.partial(jnp.dot, preferred_element_type=jnp.float32)

    def total(panel_part, data_part):
        terms = [
            dot(ref[panel_part], jnp.concatenate([window[k, data_part] for k in rows], axis=0))
            for ref, rows in zip(panel_refs, slots)
        ]
        return sum(terms[1:], terms[0])

    outs = [pltpu.make_async_copy(result.at[part], out_ref.at[survey, part], out_sems.at[part]) for part in range(2)]
    result[0] = total(0, 0) - total(1, 1)
    outs[0].start()
    result[1] = total(0, 1) + total(1, 0)
    outs[1].start()
    for copy in outs:
        copy.wait()


def products(survey, surveys, aperture, panels, pieces, out):
    panels, panel_at = zip(*panels)
    pieces, piece_at = zip(*pieces)
    width = pieces[0].shape[-1]
    anywhere = pl.BlockSpec(memory_space=pl.ANY)
    operands = [aperture, *panels, *pieces]
    in_specs = [pl.BlockSpec(memory_space=pltpu.SMEM)]
    in_specs += [pl.BlockSpec(memory_space=pltpu.VMEM)] * len(panels) + [anywhere] * len(pieces)
    aliases = {}
    if out is not None:
        aliases = {len(operands): 0}
        operands.append(out)
        in_specs.append(anywhere)
    return pl.pallas_call(
        functools.partial(kernel, survey, panel_at, piece_at),
        out_shape=jax.ShapeDtypeStruct((surveys, 2, BLK, width), jnp.float32),
        in_specs=in_specs,
        out_specs=anywhere,
        scratch_shapes=[
            pltpu.VMEM((len(pieces), 2, BLK, width), jnp.bfloat16),
            pltpu.VMEM((2, BLK, width), jnp.float32),
            pltpu.SemaphoreType.DMA((len(pieces),)),
            pltpu.SemaphoreType.DMA((2,)),
        ],
        input_output_aliases=aliases,
        compiler_params=pltpu.CompilerParams(vmem_limit_bytes=24 * 1024 * 1024),
        cost_estimate=pl.CostEstimate(
            flops=8 * BLK * BLK * APER * width, bytes_accessed=5 << 20, transcendentals=0
        ),
    )(*operands)


def body(primaries, data, aperture):
    surveys = primaries.shape[0]
    windows = (line_window if lax.axis_size("src") == 4 else hop_window)(data)
    panels = gather_panels(primaries, windows)
    out = None
    for v in range(surveys):
        out = products(v, surveys, aperture, panels[v], windows[v], out)
    return out


def solution(mesh):
    placed = (P("freq", None, "src", "rcv"), P("freq", None, "src", "rcv"), P())
    return jax.shard_map(
        body, mesh=mesh, in_specs=placed, out_specs=P("freq", None, "src", "rcv"), check_vma=False
    )
```

```python
import functools

import jax
import jax.numpy as jnp
from jax import lax
from jax.experimental import pallas as pl
from jax.experimental.pallas import tpu as pltpu
from jax.sharding import PartitionSpec as P

BLK = 256
APER = 12
HW = 6


def from_behind(x, axis, by):
    peers = lax.axis_size(axis)
    pairs = [(i, i + by) for i in range(peers) if 0 <= i + by < peers]
    return lax.ppermute(x, axis, pairs)


def swap(x, axis, bit):
    peers = lax.axis_size(axis)
    return lax.ppermute(x, axis, [(i, i ^ bit) for i in range(peers)])


def after(value, *earlier):
    return lax.optimization_barrier((value, *earlier))[0]


def line_window(data):
    peers = lax.axis_size("src")
    at_end = (lax.axis_index("src") + 1) % peers < 2
    windows = []
    for v, own in enumerate(lax.optimization_barrier([data[v : v + 1] for v in range(data.shape[0])])):
        far = lax.ppermute(own, "src", [(0, 3), (1, 2), (2, 1), (3, 0)])
        near = lax.ppermute(own, "src", [(0, 1), (1, 0), (2, 3), (3, 2)])
        middle = lax.ppermute(jnp.where(at_end, own, far), "src", [(0, 2), (2, 3), (3, 1), (1, 0)])
        windows.append([(data, v), (near, 0), (middle, 0), (far, 0)])
    return windows


def hop_window(data):
    reach = min(HW, lax.axis_size("src") - 1)
    window = {0: data}
    for hop in range(1, reach + 1):
        window[-hop] = from_behind(window[1 - hop], "src", 1)
        window[hop] = from_behind(window[hop - 1], "src", -1)
    return [[(window[distance], v) for distance in range(-reach, reach + 1)] for v in range(data.shape[0])]


def gather_panels(first, primaries, windows):
    bit = lax.axis_size("rcv") // 2
    panels = []
    for v in range(primaries.shape[0]):
        own = first if v == 0 else after(primaries, windows[v - 1][1][0])[v : v + 1]
        found = {0: own, bit: swap(own, "rcv", bit)}
        ready = after((found[0], found[bit]), *[piece for piece, _ in windows[v]])
        for lower in range(1, bit):
            last = lower & (lower - 1)
            for half, first in zip((0, bit), ready):
                found[half ^ lower] = swap(found[half ^ last] if last else first, "rcv", lower & -lower)
        panels.append([(found[m], 0) for m in range(2 * bit)])
    return panels


def window_slot(block, wanted, peers, reach):
    return lax.bitwise_xor(block, wanted) if peers == 4 else wanted - block + reach


def kernel(survey, panel_at, piece_at, aperture_ref, *refs):
    panel_refs = [ref.at[v] for ref, v in zip(refs, panel_at)]
    piece_refs = [ref.at[v] for ref, v in zip(refs[len(panel_at) :], piece_at)]
    out_ref, window, result, out_sems = refs[-4:]
    block = lax.axis_index("src")
    me = lax.axis_index("rcv")
    columns = panel_refs[0].shape[-1]
    per_shard = columns // BLK
    width = result.shape[-1]
    for k, ref in enumerate(piece_refs):
        window[k, :, :width] = ref[0]
        window[k, :, width:] = ref[1]
    panels = []
    blocks = []
    for m, ref in enumerate(panel_refs):
        shard = lax.bitwise_xor(me, m)
        panels.append(ref[...].reshape(2 * BLK, columns))
        for q in range(per_shard):
            wanted = aperture_ref[block, shard * per_shard + q]
            blocks.append(window[window_slot(block, wanted, lax.axis_size("src"), len(piece_refs) // 2)])
    products = jnp.dot(
        jnp.concatenate(panels, axis=1), jnp.concatenate(blocks, axis=0), preferred_element_type=jnp.float32
    )
    outs = [pltpu.make_async_copy(result.at[part], out_ref.at[survey, part], out_sems.at[part]) for part in range(2)]
    result[0] = products[:BLK, :width] - products[BLK:, width:]
    outs[0].start()
    result[1] = products[:BLK, width:] + products[BLK:, :width]
    outs[1].start()
    for copy in outs:
        copy.wait()


def multiply(survey, surveys, aperture, panels, pieces, out):
    panels, panel_at = zip(*panels)
    pieces, piece_at = zip(*pieces)
    width = pieces[0].shape[-1]
    anywhere = pl.BlockSpec(memory_space=pl.ANY)
    operands = [aperture, *panels, *pieces]
    in_specs = [pl.BlockSpec(memory_space=pltpu.SMEM)]
    in_specs += [pl.BlockSpec(memory_space=pltpu.VMEM)] * (len(panels) + len(pieces))
    aliases = {}
    weight = 1 if survey + 1 == surveys else 2
    if out is not None:
        aliases = {len(operands): 0}
        operands.append(out)
        in_specs.append(anywhere)
    return pl.pallas_call(
        functools.partial(kernel, survey, panel_at, piece_at),
        out_shape=jax.ShapeDtypeStruct((surveys, 2, BLK, width), jnp.float32),
        in_specs=in_specs,
        out_specs=anywhere,
        scratch_shapes=[
            pltpu.VMEM((len(pieces), BLK, 2 * width), jnp.bfloat16),
            pltpu.VMEM((2, BLK, width), jnp.float32),
            pltpu.SemaphoreType.DMA((2,)),
        ],
        input_output_aliases=aliases,
        compiler_params=pltpu.CompilerParams(vmem_limit_bytes=24 * 1024 * 1024),
        cost_estimate=pl.CostEstimate(
            flops=int(weight * 8 * BLK * BLK * APER * width), bytes_accessed=5 << 20, transcendentals=0
        ),
    )(*operands)


def body(primaries, data, aperture):
    surveys = primaries.shape[0]
    first = primaries[:1]
    windows = (line_window if lax.axis_size("src") == 4 else hop_window)(after(data, first))
    panels = gather_panels(first, primaries, windows)
    out = None
    for v in range(surveys):
        out = multiply(v, surveys, aperture, panels[v], windows[v], out)
    return out


def solution(mesh):
    placed = (P("freq", None, "src", "rcv"), P("freq", None, "src", "rcv"), P())
    return jax.shard_map(
        body, mesh=mesh, in_specs=placed, out_specs=P("freq", None, "src", "rcv"), check_vma=False
    )
```

```python
import functools

import jax
import jax.numpy as jnp
from jax import lax
from jax.experimental import pallas as pl
from jax.experimental.pallas import tpu as pltpu
from jax.sharding import PartitionSpec as P

BLK = 256
APER = 12
HW = 6


def from_behind(x, axis, by):
    peers = lax.axis_size(axis)
    pairs = [(i, i + by) for i in range(peers) if 0 <= i + by < peers]
    return lax.ppermute(x, axis, pairs)


def swap(x, axis, bit):
    peers = lax.axis_size(axis)
    return lax.ppermute(x, axis, [(i, i ^ bit) for i in range(peers)])


def after(value, *earlier):
    return lax.optimization_barrier((value, *earlier))[0]


def line_window(data):
    peers = lax.axis_size("src")
    at_end = (lax.axis_index("src") + 1) % peers < 2
    windows = []
    for v, own in enumerate(lax.optimization_barrier([data[v : v + 1] for v in range(data.shape[0])])):
        far = lax.ppermute(own, "src", [(0, 3), (1, 2), (2, 1), (3, 0)])
        near = lax.ppermute(own, "src", [(0, 1), (1, 0), (2, 3), (3, 2)])
        onward = jnp.where(at_end, own, far)
        middle = lax.ppermute(onward, "src", [(0, 2), (2, 3), (3, 1), (1, 0)])
        windows.append([(own, 0), (near, 0), (middle, 0), (far, 0)])
    return windows


def hop_window(data):
    reach = min(HW, lax.axis_size("src") - 1)
    window = {0: data}
    for hop in range(1, reach + 1):
        window[-hop] = from_behind(window[1 - hop], "src", 1)
        window[hop] = from_behind(window[hop - 1], "src", -1)
    return [[(window[distance], v) for distance in range(-reach, reach + 1)] for v in range(data.shape[0])]


def gather_panels(primaries, windows):
    bit = lax.axis_size("rcv") // 2
    awaited = [piece for piece, _ in windows[0]] + [piece for window in windows[1:] for piece, _ in (window[1], window[-1])]
    panels = []
    for v in range(primaries.shape[0]):
        own = primaries[v : v + 1]
        found = {0: own, bit: swap(own, "rcv", bit)}
        ready = after((own, found[bit]), *awaited) if v == 0 else (own, found[bit])
        for half, origin in zip((0, bit), ready):
            for lower in range(1, bit):
                last = lower & (lower - 1)
                found[half ^ lower] = swap(found[half ^ last] if last else origin, "rcv", lower & -lower)
        panels.append([(found[m], 0) for m in range(2 * bit)])
    return panels


def window_slot(block, wanted, peers, reach):
    return lax.bitwise_xor(block, wanted) if peers == 4 else wanted - block + reach


def window_kernel(piece_at, *refs):
    window = refs[-1]
    width = window.shape[-1] // 2
    for k, (ref, v) in enumerate(zip(refs, piece_at)):
        window[k, :, :width] = ref[v, 0]
        window[k, :, width:] = ref[v, 1]


def assemble(pieces, weight):
    pieces, piece_at = zip(*pieces)
    width = pieces[0].shape[-1]
    return pl.pallas_call(
        functools.partial(window_kernel, piece_at),
        out_shape=jax.ShapeDtypeStruct((len(pieces), BLK, 2 * width), jnp.bfloat16),
        in_specs=[pl.BlockSpec(memory_space=pltpu.VMEM)] * len(pieces),
        out_specs=pl.BlockSpec(memory_space=pltpu.VMEM),
        compiler_params=pltpu.CompilerParams(vmem_limit_bytes=16 * 1024 * 1024),
        cost_estimate=pl.CostEstimate(
            flops=int(weight * 8 * BLK * BLK * APER * width), bytes_accessed=1 << 20, transcendentals=0
        ),
    )(*pieces)


def kernel(survey, panel_at, aperture_ref, *refs):
    panel_refs = [ref.at[v] for ref, v in zip(refs, panel_at)]
    window = refs[len(panel_at)]
    out_ref, result, out_sems = refs[-3:]
    block = lax.axis_index("src")
    me = lax.axis_index("rcv")
    columns = panel_refs[0].shape[-1]
    per_shard = columns // BLK
    width = result.shape[-1]
    panels = []
    blocks = []
    for m, ref in enumerate(panel_refs):
        shard = lax.bitwise_xor(me, m)
        panels.append(ref[...].reshape(2 * BLK, columns))
        for q in range(per_shard):
            wanted = aperture_ref[block, shard * per_shard + q]
            blocks.append(window[window_slot(block, wanted, lax.axis_size("src"), window.shape[0] // 2)])
    products = jnp.dot(
        jnp.concatenate(panels, axis=1), jnp.concatenate(blocks, axis=0), preferred_element_type=jnp.float32
    )
    outs = [pltpu.make_async_copy(result.at[part], out_ref.at[survey, part], out_sems.at[part]) for part in range(2)]
    result[0] = products[:BLK, :width] - products[BLK:, width:]
    outs[0].start()
    result[1] = products[:BLK, width:] + products[BLK:, :width]
    outs[1].start()
    for copy in outs:
        copy.wait()


def multiply(survey, surveys, aperture, panels, window, out, weight):
    panels, panel_at = zip(*panels)
    width = window.shape[-1] // 2
    anywhere = pl.BlockSpec(memory_space=pl.ANY)
    operands = [aperture, *panels, window]
    in_specs = [pl.BlockSpec(memory_space=pltpu.SMEM)]
    in_specs += [pl.BlockSpec(memory_space=pltpu.VMEM)] * (len(panels) + 1)
    aliases = {}
    if out is not None:
        aliases = {len(operands): 0}
        operands.append(out)
        in_specs.append(anywhere)
    return pl.pallas_call(
        functools.partial(kernel, survey, panel_at),
        out_shape=jax.ShapeDtypeStruct((surveys, 2, BLK, width), jnp.float32),
        in_specs=in_specs,
        out_specs=anywhere,
        scratch_shapes=[pltpu.VMEM((2, BLK, width), jnp.float32), pltpu.SemaphoreType.DMA((2,))],
        input_output_aliases=aliases,
        compiler_params=pltpu.CompilerParams(vmem_limit_bytes=24 * 1024 * 1024),
        cost_estimate=pl.CostEstimate(
            flops=int(weight * 8 * BLK * BLK * APER * width), bytes_accessed=1 << 20, transcendentals=0
        ),
    )(*operands)


def body(primaries, data, aperture):
    surveys = primaries.shape[0]
    windows = (line_window if lax.axis_size("src") == 4 else hop_window)(data)
    panels = gather_panels(primaries, windows)
    out = None
    for v in range(surveys):
        pieces = windows[v]
        if out is not None:
            pieces = [(after(piece, out), at) for piece, at in pieces]
        window = assemble(pieces, 4 if v else 0.1)
        out = multiply(v, surveys, aperture, panels[v], window, out, 1 if v else 0.3)
    return out


def solution(mesh):
    placed = (P("freq", None, "src", "rcv"), P("freq", None, "src", "rcv"), P())
    return jax.shard_map(
        body, mesh=mesh, in_specs=placed, out_specs=P("freq", None, "src", "rcv"), check_vma=False
    )
```

```python
import functools

import jax
import jax.numpy as jnp
from jax import lax
from jax.experimental import pallas as pl
from jax.experimental.pallas import tpu as pltpu
from jax.sharding import PartitionSpec as P

BLK = 256
APER = 12
HW = 6


def from_behind(x, axis, by):
    peers = lax.axis_size(axis)
    pairs = [(i, i + by) for i in range(peers) if 0 <= i + by < peers]
    return lax.ppermute(x, axis, pairs)


def swap(x, axis, bit):
    peers = lax.axis_size(axis)
    return lax.ppermute(x, axis, [(i, i ^ bit) for i in range(peers)])


def after(value, *earlier):
    return lax.optimization_barrier((value, *earlier))[0]


def line_window(data):
    peers = lax.axis_size("src")
    at_end = (lax.axis_index("src") + 1) % peers < 2
    near = lax.ppermute(data, "src", [(0, 1), (1, 0), (2, 3), (3, 2)])
    windows = []
    for v, own in enumerate(lax.optimization_barrier([data[v : v + 1] for v in range(data.shape[0])])):
        far = lax.ppermute(own, "src", [(0, 3), (1, 2), (2, 1), (3, 0)])
        onward = jnp.where(at_end, own, far)
        middle = lax.ppermute(onward, "src", [(0, 2), (2, 3), (3, 1), (1, 0)])
        windows.append([(data, v), (near, v), (middle, 0), (far, 0)])
    return windows


def hop_window(data):
    reach = min(HW, lax.axis_size("src") - 1)
    window = {0: data}
    for hop in range(1, reach + 1):
        window[-hop] = from_behind(window[1 - hop], "src", 1)
        window[hop] = from_behind(window[hop - 1], "src", -1)
    return [[(window[distance], v) for distance in range(-reach, reach + 1)] for v in range(data.shape[0])]


def exchange(primaries):
    bit = lax.axis_size("rcv") // 2
    halves = []
    for v in range(primaries.shape[0]):
        own = primaries[v : v + 1]
        primaries = after(primaries, own)
        halves.append((own, swap(own, "rcv", bit)))
    return halves


def hand_on(halves):
    bit = lax.axis_size("rcv") // 2
    panels = list(halves)
    for lower in range(1, bit):
        panels += [swap(panels[2 * (lower & (lower - 1)) + half], "rcv", lower & -lower) for half in range(2)]
    return panels[::2] + panels[1::2]


def window_slot(block, wanted, peers, reach):
    return lax.bitwise_xor(block, wanted) if peers == 4 else wanted - block + reach


def kernel(survey, panel_at, piece_at, aperture_ref, *refs):
    panel_refs = [ref.at[v] for ref, v in zip(refs, panel_at)]
    piece_refs = [ref.at[v] for ref, v in zip(refs[len(panel_at) :], piece_at)]
    out_ref, window, result, out_sems = refs[-4:]
    block = lax.axis_index("src")
    me = lax.axis_index("rcv")
    columns = panel_refs[0].shape[-1]
    per_shard = columns // BLK
    width = result.shape[-1]
    for k, ref in enumerate(piece_refs):
        window[k, :, :width] = ref[0]
        window[k, :, width:] = ref[1]
    panels = []
    blocks = []
    for m, ref in enumerate(panel_refs):
        shard = lax.bitwise_xor(me, m)
        panels.append(ref[...].reshape(2 * BLK, columns))
        for q in range(per_shard):
            wanted = aperture_ref[block, shard * per_shard + q]
            blocks.append(window[window_slot(block, wanted, lax.axis_size("src"), len(piece_refs) // 2)])
    products = jnp.dot(
        jnp.concatenate(panels, axis=1), jnp.concatenate(blocks, axis=0), preferred_element_type=jnp.float32
    )
    outs = [pltpu.make_async_copy(result.at[part], out_ref.at[survey, part], out_sems.at[part]) for part in range(2)]
    result[0] = products[:BLK, :width] - products[BLK:, width:]
    outs[0].start()
    result[1] = products[:BLK, width:] + products[BLK:, :width]
    outs[1].start()
    for copy in outs:
        copy.wait()


def multiply(survey, surveys, aperture, panels, pieces, out):
    panels, panel_at = zip(*panels)
    pieces, piece_at = zip(*pieces)
    width = pieces[0].shape[-1]
    anywhere = pl.BlockSpec(memory_space=pl.ANY)
    operands = [aperture, *panels, *pieces]
    in_specs = [pl.BlockSpec(memory_space=pltpu.SMEM)]
    in_specs += [pl.BlockSpec(memory_space=pltpu.VMEM)] * (len(panels) + len(pieces))
    aliases = {}
    weight = 1 if survey + 1 == surveys else 1.6
    if out is not None:
        aliases = {len(operands): 0}
        operands.append(out)
        in_specs.append(anywhere)
    return pl.pallas_call(
        functools.partial(kernel, survey, panel_at, piece_at),
        out_shape=jax.ShapeDtypeStruct((surveys, 2, BLK, width), jnp.float32),
        in_specs=in_specs,
        out_specs=anywhere,
        scratch_shapes=[
            pltpu.VMEM((len(pieces), BLK, 2 * width), jnp.bfloat16),
            pltpu.VMEM((2, BLK, width), jnp.float32),
            pltpu.SemaphoreType.DMA((2,)),
        ],
        input_output_aliases=aliases,
        compiler_params=pltpu.CompilerParams(vmem_limit_bytes=24 * 1024 * 1024),
        cost_estimate=pl.CostEstimate(
            flops=int(weight * 8 * BLK * BLK * APER * width), bytes_accessed=5 << 20, transcendentals=0
        ),
    )(*operands)


def body(primaries, data, aperture):
    surveys = primaries.shape[0]
    halves = exchange(primaries)
    windows = (line_window if lax.axis_size("src") == 4 else hop_window)(after(data, halves[0][0]))
    under_way = [window[k][0] for window in windows[1:] for k in (1, -1)]
    out = None
    for v in range(surveys):
        ready = after(halves[v], [piece for piece, _ in windows[v]], under_way)
        out = multiply(v, surveys, aperture, [(panel, 0) for panel in hand_on(ready)], windows[v], out)
    return out


def solution(mesh):
    placed = (P("freq", None, "src", "rcv"), P("freq", None, "src", "rcv"), P())
    return jax.shard_map(
        body, mesh=mesh, in_specs=placed, out_specs=P("freq", None, "src", "rcv"), check_vma=False
    )
```

```python
import functools

import jax
import jax.numpy as jnp
from jax import lax
from jax.experimental import pallas as pl
from jax.experimental.pallas import tpu as pltpu
from jax.sharding import PartitionSpec as P

BLK = 256
APER = 12
HW = 6
LANES = 128


def after(value, *earlier):
    return lax.optimization_barrier((value, *earlier))[0]


def from_behind(x, axis, by):
    peers = lax.axis_size(axis)
    pairs = [(i, i + by) for i in range(peers) if 0 <= i + by < peers]
    return lax.ppermute(x, axis, pairs)


def swap(x, axis, bit):
    peers = lax.axis_size(axis)
    return lax.ppermute(x, axis, [(i, i ^ bit) for i in range(peers)])


def at_end():
    return (lax.axis_index("src") + 1) % lax.axis_size("src") < 2


def line_window(data):
    middle = lax.ppermute(data, "src", [(1, 2), (2, 1)])
    near = lax.ppermute(data, "src", [(0, 1), (1, 0), (2, 3), (3, 2)])
    ends = lax.ppermute(data, "src", [(0, 3), (3, 0)])
    onward = jnp.where(at_end(), data, middle)
    windows = []
    for v in range(data.shape[0]):
        onward = onward if v == 0 else after(onward, near)
        across = lax.ppermute(onward[v : v + 1], "src", [(0, 2), (2, 3), (3, 1), (1, 0)])
        windows.append([(data, v), (near, v), (middle, v), (ends, v), (across, 0)])
    return windows


def hop_window(data):
    reach = min(HW, lax.axis_size("src") - 1)
    window = {0: data}
    for hop in range(1, reach + 1):
        window[-hop] = from_behind(window[1 - hop], "src", 1)
        window[hop] = from_behind(window[hop - 1], "src", -1)
    return [[(window[distance], v) for distance in range(-reach, reach + 1)] for v in range(data.shape[0])]


def gather_panels(primaries):
    bit = lax.axis_size("rcv") // 2
    panels = {0: primaries, bit: swap(primaries, "rcv", bit)}
    for lower in range(1, bit):
        for half in (0, bit):
            panels[half ^ lower] = swap(panels[half ^ (lower & (lower - 1))], "rcv", lower & -lower)
    return [panels[m] for m in range(2 * bit)]


def fill_window(window, refs, piece_at):
    pieces = [ref.at[v] for ref, v in zip(refs, piece_at)]
    line = lax.axis_size("src") == 4
    for h in range(window.shape[0]):
        lanes = pl.ds(h * LANES, LANES)
        for part in range(2):
            blocks = [piece[part, :, lanes] for piece in pieces]
            if line:
                own, near, middle, ends, across = blocks
                blocks = [own, near, across, jnp.where(at_end(), ends, middle)]
            for k, block in enumerate(blocks):
                window[h, k, :, pl.ds(part * LANES, LANES)] = block


def product(window, h, aperture_ref, panels):
    src = lax.axis_index("src")
    me = lax.axis_index("rcv")
    blocks = []
    for m, panel in panels:
        shard = lax.bitwise_xor(me, m)
        per_shard = panel.shape[-1] // BLK
        for q in range(per_shard):
            wanted = aperture_ref[src, shard * per_shard + q]
            k = lax.bitwise_xor(src, wanted) if lax.axis_size("src") == 4 else wanted - src + window.shape[1] // 2
            blocks.append(window[h, k])
    values = jnp.concatenate([panel[...].reshape(2 * BLK, panel.shape[-1]) for _, panel in panels], axis=1)
    both = jnp.dot(values, jnp.concatenate(blocks, axis=0), preferred_element_type=jnp.float32)
    return both[:BLK, :LANES] - both[BLK:, LANES:], both[:BLK, LANES:] + both[BLK:, :LANES]


def first_kernel(split, piece_at, aperture_ref, *refs):
    panel_refs = refs[:split]
    window, partial = refs[-2:]
    fill_window(window, refs[split:-2], piece_at)

    @pl.loop(0, window.shape[0])
    def _(h):
        partial[h, 0], partial[h, 1] = product(
            window, h, aperture_ref, [(m, ref.at[0]) for m, ref in enumerate(panel_refs)]
        )


def last_kernel(split, piece_at, aperture_ref, first_window, partial, *refs):
    panel_count = len(refs) - len(piece_at) - 4
    panel_refs = refs[:panel_count]
    out_ref, window, result, sems = refs[-4:]
    fill_window(window, refs[panel_count:-4], piece_at)
    halves = window.shape[0]

    def copies(h):
        return [
            pltpu.make_async_copy(
                result.at[h, v, part], out_ref.at[v, part, :, pl.ds(h * LANES, LANES)], sems.at[h, v, part]
            )
            for v in range(2)
            for part in range(2)
        ]

    @pl.loop(0, halves)
    def _(h):
        panels = [(m, ref.at[0]) for m, ref in enumerate(panel_refs)]
        real, imag = product(window=first_window, h=h, aperture_ref=aperture_ref, panels=panels[split:])
        result[h, 0, 0] = partial[h, 0] + real
        result[h, 0, 1] = partial[h, 1] + imag
        panels = [(m, ref.at[1]) for m, ref in enumerate(panel_refs)]
        result[h, 1, 0], result[h, 1, 1] = product(window, h, aperture_ref, panels)
        for copy in copies(h):
            copy.start()

    for h in range(halves):
        for copy in copies(h):
            copy.wait()


def spec(space):
    return pl.BlockSpec(memory_space=space)


def cost(share):
    return pl.CostEstimate(flops=int(share * (8 * BLK * BLK * APER * BLK)), bytes_accessed=1 << 20, transcendentals=0)


def held(piece, token):
    return pl.pallas_call(
        lambda piece_ref, token_ref, out_ref: None,
        out_shape=jax.ShapeDtypeStruct(piece.shape, piece.dtype),
        in_specs=[spec(pl.ANY)] * 2,
        out_specs=spec(pl.ANY),
        input_output_aliases={0: 0},
        cost_estimate=cost(12),
    )(piece, token)


def body(primaries, data, aperture):
    width = data.shape[3]
    halves = width // LANES
    first, last = (line_window if lax.axis_size("src") == 4 else hop_window)(data)
    panels = gather_panels(primaries)
    depth = 4 if lax.axis_size("src") == 4 else len(first)
    split = len(panels) - 1
    window_shape = (halves, depth, BLK, 2 * LANES)
    params = pltpu.CompilerParams(vmem_limit_bytes=24 * 1024 * 1024)

    pieces, piece_at = zip(*first)
    window, partial = pl.pallas_call(
        functools.partial(first_kernel, split, piece_at),
        out_shape=[
            jax.ShapeDtypeStruct(window_shape, jnp.bfloat16),
            jax.ShapeDtypeStruct((halves, 2, BLK, LANES), jnp.float32),
        ],
        in_specs=[spec(pltpu.SMEM)] + [spec(pltpu.VMEM)] * (split + len(pieces)),
        out_specs=[spec(pltpu.VMEM)] * 2,
        compiler_params=params,
        cost_estimate=cost(0.3),
    )(aperture, *panels[:split], *pieces)

    pieces, piece_at = zip(*last)
    pieces = [*pieces[:-1], held(pieces[-1], partial)]
    return pl.pallas_call(
        functools.partial(last_kernel, split, piece_at),
        out_shape=jax.ShapeDtypeStruct((2, 2, BLK, width), jnp.float32),
        in_specs=[spec(pltpu.SMEM)] + [spec(pltpu.VMEM)] * (2 + len(panels) + len(pieces)),
        out_specs=spec(pl.ANY),
        scratch_shapes=[
            pltpu.VMEM(window_shape, jnp.bfloat16),
            pltpu.VMEM((halves, 2, 2, BLK, LANES), jnp.float32),
            pltpu.SemaphoreType.DMA((halves, 2, 2)),
        ],
        compiler_params=params,
        cost_estimate=cost(1.25),
    )(aperture, window, partial, *panels, *pieces)


def solution(mesh):
    placed = (P("freq", None, "src", "rcv"), P("freq", None, "src", "rcv"), P())
    return jax.shard_map(
        body, mesh=mesh, in_specs=placed, out_specs=P("freq", None, "src", "rcv"), check_vma=False
    )
```

```python
import functools

import jax
import jax.numpy as jnp
from jax import lax
from jax.experimental import pallas as pl
from jax.experimental.pallas import tpu as pltpu
from jax.sharding import PartitionSpec as P

BLK = 256
APER = 12
HW = 6


def after(value, *earlier):
    return lax.optimization_barrier((value, *earlier))[0]


def from_behind(x, axis, by):
    peers = lax.axis_size(axis)
    pairs = [(i, i + by) for i in range(peers) if 0 <= i + by < peers]
    return lax.ppermute(x, axis, pairs)


def swap(x, axis, bit):
    peers = lax.axis_size(axis)
    return lax.ppermute(x, axis, [(i, i ^ bit) for i in range(peers)])


def at_end():
    return (lax.axis_index("src") + 1) % lax.axis_size("src") < 2


def line_window(data):
    near = lax.ppermute(data, "src", [(0, 1), (1, 0), (2, 3), (3, 2)])
    windows = []
    for v, own in enumerate(lax.optimization_barrier([data[v : v + 1] for v in range(data.shape[0])])):
        far = lax.ppermute(own, "src", [(0, 3), (1, 2), (2, 1), (3, 0)])
        onward = jnp.where(at_end(), own, far if v == 0 else after(far, near))
        across = lax.ppermute(onward, "src", [(0, 2), (2, 3), (3, 1), (1, 0)])
        windows.append([(data, v), (near, v), (across, 0), (far, 0)])
    return windows


def hop_window(data):
    reach = min(HW, lax.axis_size("src") - 1)
    window = {0: data}
    for hop in range(1, reach + 1):
        window[-hop] = from_behind(window[1 - hop], "src", 1)
        window[hop] = from_behind(window[hop - 1], "src", -1)
    return [[(window[distance], v) for distance in range(-reach, reach + 1)] for v in range(data.shape[0])]


def gather_panels(primaries):
    bit = lax.axis_size("rcv") // 2
    panels = {0: primaries, bit: swap(primaries, "rcv", bit)}
    for lower in range(1, bit):
        for half in (0, bit):
            panels[half ^ lower] = swap(panels[half ^ (lower & (lower - 1))], "rcv", lower & -lower)
    return [panels[m] for m in range(2 * bit)]


def fill_window(window, pieces):
    width = window.shape[-1] // 2
    for k, piece in pieces.items():
        window[k, :, :width] = piece[0]
        window[k, :, width:] = piece[1]


def product(window, aperture_ref, panels):
    src = lax.axis_index("src")
    me = lax.axis_index("rcv")
    width = window.shape[-1] // 2
    blocks = []
    for m, panel in panels.items():
        shard = lax.bitwise_xor(me, m)
        per_shard = panel.shape[-1] // BLK
        for q in range(per_shard):
            wanted = aperture_ref[src, shard * per_shard + q]
            blocks.append(window[lax.bitwise_xor(src, wanted) if lax.axis_size("src") == 4 else wanted - src + window.shape[0] // 2])
    values = jnp.concatenate([panel[...].reshape(2 * BLK, panel.shape[-1]) for panel in panels.values()], axis=1)
    both = jnp.dot(values, jnp.concatenate(blocks, axis=0), preferred_element_type=jnp.float32)
    return both[:BLK, :width] - both[BLK:, width:], both[:BLK, width:] + both[BLK:, :width]


def first_kernel(split, first_at, last_at, aperture_ref, *refs):
    panel_refs = refs[:split]
    first_refs = refs[split : split + len(first_at)]
    last_refs = refs[split + len(first_at) : -3]
    first_window, last_window, partial = refs[-3:]
    fill_window(first_window, {k: ref.at[v] for k, (ref, v) in enumerate(zip(first_refs, first_at))})
    fill_window(last_window, {k: ref.at[v] for ref, (k, v) in zip(last_refs, last_at.items())})
    partial[0], partial[1] = product(first_window, aperture_ref, {m: ref.at[0] for m, ref in enumerate(panel_refs)})


def last_kernel(split, late, aperture_ref, partial, first_window, _, late_ref, *refs):
    panel_refs = refs[:-4]
    out_ref, window, result, sems = refs[-4:]

    def finish(v, real, imag):
        result[v, 0] = real
        result[v, 1] = imag
        copies = [pltpu.make_async_copy(result.at[v, part], out_ref.at[v, part], sems.at[v, part]) for part in range(2)]
        for copy in copies:
            copy.start()
        return copies

    real, imag = product(first_window, aperture_ref, {m: ref.at[0] for m, ref in enumerate(panel_refs) if m >= split})
    copies = finish(0, partial[0] + real, partial[1] + imag)
    fill_window(window, {late: late_ref.at[0]})
    copies += finish(1, *product(window, aperture_ref, {m: ref.at[1] for m, ref in enumerate(panel_refs)}))
    for copy in copies:
        copy.wait()


def spec(space):
    return pl.BlockSpec(memory_space=space)


def cost(share):
    return pl.CostEstimate(flops=int(share * (8 * BLK * BLK * APER * BLK)), bytes_accessed=1 << 20, transcendentals=0)


def limit(megabytes):
    return pltpu.CompilerParams(vmem_limit_bytes=megabytes << 20)


def held(piece, token):
    return pl.pallas_call(
        lambda piece_ref, token_ref, out_ref: None,
        out_shape=jax.ShapeDtypeStruct(piece.shape, piece.dtype),
        in_specs=[spec(pl.ANY)] * 2,
        out_specs=spec(pl.ANY),
        input_output_aliases={0: 0},
        compiler_params=limit(1),
        cost_estimate=cost(12),
    )(piece, token)


def body(primaries, data, aperture):
    width = data.shape[3]
    line = lax.axis_size("src") == 4
    first, last = (line_window if line else hop_window)(data)
    panels = gather_panels(primaries)
    split = len(panels) - 1
    late = 2 if line else len(last) - 1
    late_piece, late_at = last[late]
    late_piece = late_piece[late_at : late_at + 1]
    window_shape = (len(first), BLK, 2 * width)
    early = {k: piece for k, piece in enumerate(last) if k != late}

    first_window, window, partial = pl.pallas_call(
        functools.partial(first_kernel, split, [v for _, v in first], {k: v for k, (_, v) in early.items()}),
        out_shape=[jax.ShapeDtypeStruct(window_shape, jnp.bfloat16)] * 2
        + [jax.ShapeDtypeStruct((2, BLK, width), jnp.float32)],
        in_specs=[spec(pltpu.SMEM)] + [spec(pltpu.VMEM)] * (split + len(first) + len(early)),
        out_specs=[spec(pltpu.VMEM)] * 3,
        compiler_params=limit(16),
        cost_estimate=cost(0.3),
    )(aperture, *panels[:split], *[piece for piece, _ in first], *[piece for piece, _ in early.values()])

    return pl.pallas_call(
        functools.partial(last_kernel, split, late),
        out_shape=[
            jax.ShapeDtypeStruct((2, 2, BLK, width), jnp.float32),
            jax.ShapeDtypeStruct(window_shape, jnp.bfloat16),
        ],
        in_specs=[spec(pltpu.SMEM)] + [spec(pltpu.VMEM)] * (4 + len(panels)),
        out_specs=[spec(pl.ANY), spec(pltpu.VMEM)],
        scratch_shapes=[pltpu.VMEM((2, 2, BLK, width), jnp.float32), pltpu.SemaphoreType.DMA((2, 2))],
        input_output_aliases={3: 1},
        compiler_params=limit(16),
        cost_estimate=cost(1.25),
    )(aperture, partial, first_window, window, held(late_piece, partial), *panels)[0]


def solution(mesh):
    placed = (P("freq", None, "src", "rcv"), P("freq", None, "src", "rcv"), P())
    return jax.shard_map(
        body, mesh=mesh, in_specs=placed, out_specs=P("freq", None, "src", "rcv"), check_vma=False
    )
```

```python
import functools

import jax
import jax.numpy as jnp
from jax import lax
from jax.experimental import pallas as pl
from jax.experimental.pallas import tpu as pltpu
from jax.sharding import PartitionSpec as P

BLK = 256
APER = 12
HW = 6


def after(value, *earlier):
    return lax.optimization_barrier((value, *earlier))[0]


def from_behind(x, axis, by):
    peers = lax.axis_size(axis)
    pairs = [(i, i + by) for i in range(peers) if 0 <= i + by < peers]
    return lax.ppermute(x, axis, pairs)


def swap(x, axis, bit):
    peers = lax.axis_size(axis)
    return lax.ppermute(x, axis, [(i, i ^ bit) for i in range(peers)])


def at_end():
    return (lax.axis_index("src") + 1) % lax.axis_size("src") < 2


def split_kernel(data_ref, *refs):
    *part_refs, sems = refs
    copies = [pltpu.make_async_copy(data_ref.at[pl.ds(v, 1)], ref, sems.at[v]) for v, ref in enumerate(part_refs)]
    for copy in copies:
        copy.start()
    for copy in copies:
        copy.wait()


def split_surveys(data):
    surveys, *shape = data.shape
    return pl.pallas_call(
        split_kernel,
        out_shape=[jax.ShapeDtypeStruct((1, *shape), data.dtype)] * surveys,
        in_specs=[spec(pl.ANY)],
        out_specs=[spec(pltpu.VMEM)] * surveys,
        scratch_shapes=[pltpu.SemaphoreType.DMA((surveys,))],
        compiler_params=limit(1),
        cost_estimate=cost(0.1),
    )(data)


def line_window(data):
    near = lax.ppermute(data, "src", [(0, 1), (1, 0), (2, 3), (3, 2)])
    windows = []
    for v, own in enumerate(split_surveys(data)):
        far = lax.ppermute(own, "src", [(0, 3), (1, 2), (2, 1), (3, 0)])
        onward = jnp.where(at_end(), own, far)
        across = lax.ppermute(onward, "src", [(0, 2), (2, 3), (3, 1), (1, 0)])
        windows.append([(data, v), (near, v), (across, 0), (far, 0)])
    return windows


def hop_window(data):
    reach = min(HW, lax.axis_size("src") - 1)
    window = {0: data}
    for hop in range(1, reach + 1):
        window[-hop] = from_behind(window[1 - hop], "src", 1)
        window[hop] = from_behind(window[hop - 1], "src", -1)
    return [[(window[distance], v) for distance in range(-reach, reach + 1)] for v in range(data.shape[0])]


def gather_panels(primaries):
    bit = lax.axis_size("rcv") // 2
    panels = {0: primaries, bit: swap(primaries, "rcv", bit)}
    for lower in range(1, bit):
        for half in (0, bit):
            panels[half ^ lower] = swap(panels[half ^ (lower & (lower - 1))], "rcv", lower & -lower)
    return [panels[m] for m in range(2 * bit)]


def fill_window(window, pieces):
    width = window.shape[-1] // 2
    for k, piece in pieces.items():
        window[k, :, :width] = piece[0]
        window[k, :, width:] = piece[1]


def product(window, aperture_ref, panels):
    src = lax.axis_index("src")
    me = lax.axis_index("rcv")
    width = window.shape[-1] // 2
    blocks = []
    for m, panel in panels.items():
        shard = lax.bitwise_xor(me, m)
        per_shard = panel.shape[-1] // BLK
        for q in range(per_shard):
            wanted = aperture_ref[src, shard * per_shard + q]
            blocks.append(window[lax.bitwise_xor(src, wanted) if lax.axis_size("src") == 4 else wanted - src + window.shape[0] // 2])
    values = jnp.concatenate([panel[...].reshape(2 * BLK, panel.shape[-1]) for panel in panels.values()], axis=1)
    both = jnp.dot(values, jnp.concatenate(blocks, axis=0), preferred_element_type=jnp.float32)
    return both[:BLK, :width] - both[BLK:, width:], both[:BLK, width:] + both[BLK:, :width]


def first_kernel(split, first_at, last_at, aperture_ref, *refs):
    panel_refs = refs[:split]
    first_refs = refs[split : split + len(first_at)]
    last_refs = refs[split + len(first_at) : -3]
    first_window, last_window, partial = refs[-3:]
    fill_window(first_window, {k: ref.at[v] for k, (ref, v) in enumerate(zip(first_refs, first_at))})
    fill_window(last_window, {k: ref.at[v] for ref, (k, v) in zip(last_refs, last_at.items())})
    partial[0], partial[1] = product(first_window, aperture_ref, {m: ref.at[0] for m, ref in enumerate(panel_refs)})


def last_kernel(split, late, aperture_ref, partial, first_window, _, late_ref, *refs):
    panel_refs = refs[:-4]
    out_ref, window, result, sems = refs[-4:]

    def finish(v, real, imag):
        result[v, 0] = real
        result[v, 1] = imag
        copies = [pltpu.make_async_copy(result.at[v, part], out_ref.at[v, part], sems.at[v, part]) for part in range(2)]
        for copy in copies:
            copy.start()
        return copies

    real, imag = product(first_window, aperture_ref, {m: ref.at[0] for m, ref in enumerate(panel_refs) if m >= split})
    copies = finish(0, partial[0] + real, partial[1] + imag)
    fill_window(window, {late: late_ref.at[0]})
    copies += finish(1, *product(window, aperture_ref, {m: ref.at[1] for m, ref in enumerate(panel_refs)}))
    for copy in copies:
        copy.wait()


def spec(space):
    return pl.BlockSpec(memory_space=space)


def cost(share):
    return pl.CostEstimate(flops=int(share * (8 * BLK * BLK * APER * BLK)), bytes_accessed=1 << 20, transcendentals=0)


def limit(megabytes):
    return pltpu.CompilerParams(vmem_limit_bytes=megabytes << 20)


def held(piece, token):
    return pl.pallas_call(
        lambda piece_ref, token_ref, out_ref: None,
        out_shape=jax.ShapeDtypeStruct(piece.shape, piece.dtype),
        in_specs=[spec(pl.ANY)] * 2,
        out_specs=spec(pl.ANY),
        input_output_aliases={0: 0},
        compiler_params=limit(1),
        cost_estimate=cost(12),
    )(piece, token)


def body(primaries, data, aperture):
    width = data.shape[3]
    line = lax.axis_size("src") == 4
    first, last = (line_window if line else hop_window)(data)
    panels = gather_panels(primaries)
    split = len(panels) - 1
    late = 2 if line else len(last) - 1
    late_piece, late_at = last[late]
    late_piece = late_piece[late_at : late_at + 1]
    window_shape = (len(first), BLK, 2 * width)
    early = {k: piece for k, piece in enumerate(last) if k != late}

    first_window, window, partial = pl.pallas_call(
        functools.partial(first_kernel, split, [v for _, v in first], {k: v for k, (_, v) in early.items()}),
        out_shape=[jax.ShapeDtypeStruct(window_shape, jnp.bfloat16)] * 2
        + [jax.ShapeDtypeStruct((2, BLK, width), jnp.float32)],
        in_specs=[spec(pltpu.SMEM)] + [spec(pltpu.VMEM)] * (split + len(first) + len(early)),
        out_specs=[spec(pltpu.VMEM)] * 3,
        compiler_params=limit(16),
        cost_estimate=cost(0.3),
    )(aperture, *panels[:split], *[piece for piece, _ in first], *[piece for piece, _ in early.values()])

    return pl.pallas_call(
        functools.partial(last_kernel, split, late),
        out_shape=[
            jax.ShapeDtypeStruct((2, 2, BLK, width), jnp.float32),
            jax.ShapeDtypeStruct(window_shape, jnp.bfloat16),
        ],
        in_specs=[spec(pltpu.SMEM)] + [spec(pltpu.VMEM)] * (4 + len(panels)),
        out_specs=[spec(pl.ANY), spec(pltpu.VMEM)],
        scratch_shapes=[pltpu.VMEM((2, 2, BLK, width), jnp.float32), pltpu.SemaphoreType.DMA((2, 2))],
        input_output_aliases={3: 1},
        compiler_params=limit(16),
        cost_estimate=cost(1.25),
    )(aperture, partial, first_window, window, held(late_piece, partial), *panels)[0]


def solution(mesh):
    placed = (P("freq", None, "src", "rcv"), P("freq", None, "src", "rcv"), P())
    return jax.shard_map(
        body, mesh=mesh, in_specs=placed, out_specs=P("freq", None, "src", "rcv"), check_vma=False
    )
```

```python
import functools

import jax
import jax.numpy as jnp
from jax import lax
from jax.experimental import pallas as pl
from jax.experimental.pallas import tpu as pltpu
from jax.sharding import PartitionSpec as P

BLK = 256
APER = 12
HW = 6


def after(value, *earlier):
    return lax.optimization_barrier((value, *earlier))[0]


def from_behind(x, axis, by):
    peers = lax.axis_size(axis)
    pairs = [(i, i + by) for i in range(peers) if 0 <= i + by < peers]
    return lax.ppermute(x, axis, pairs)


def swap(x, axis, bit):
    peers = lax.axis_size(axis)
    return lax.ppermute(x, axis, [(i, i ^ bit) for i in range(peers)])


def at_end():
    return (lax.axis_index("src") + 1) % lax.axis_size("src") < 2


def line_window(data):
    near = lax.ppermute(data, "src", [(0, 1), (1, 0), (2, 3), (3, 2)])
    windows = []
    for v, own in enumerate(lax.optimization_barrier([data[v : v + 1] for v in range(data.shape[0])])):
        far = lax.ppermute(own, "src", [(0, 3), (1, 2), (2, 1), (3, 0)])
        onward = jnp.where(at_end(), own, far)
        across = lax.ppermute(onward, "src", [(0, 2), (2, 3), (3, 1), (1, 0)])
        windows.append([(own, 0), (near, v), (across, 0), (far, 0)])
    return windows


def hop_window(data):
    reach = min(HW, lax.axis_size("src") - 1)
    window = {0: data}
    for hop in range(1, reach + 1):
        window[-hop] = from_behind(window[1 - hop], "src", 1)
        window[hop] = from_behind(window[hop - 1], "src", -1)
    return [[(window[distance], v) for distance in range(-reach, reach + 1)] for v in range(data.shape[0])]


def gather_panels(primaries):
    bit = lax.axis_size("rcv") // 2
    panels = [primaries]
    for lower in range(1, bit):
        panels.append(swap(panels[lower & (lower - 1)], "rcv", lower & -lower))
    return panels, swap(primaries, "rcv", bit)


def hand_on(panel, token):
    bit = lax.axis_size("rcv") // 2
    panels = [after(panel, token)]
    for lower in range(1, bit):
        panels.append(swap(panels[lower & (lower - 1)], "rcv", lower & -lower))
    return panels[1:]


def fill_window(window, pieces):
    width = window.shape[-1] // 2
    for k, piece in pieces.items():
        window[k, :, :width] = piece[0]
        window[k, :, width:] = piece[1]


def slot_entries(aperture_ref, m, per_shard, depth):
    src = lax.axis_index("src")
    shard = lax.bitwise_xor(lax.axis_index("rcv"), m)
    wanted = [aperture_ref[src, shard * per_shard + q] for q in range(per_shard)]
    if lax.axis_size("src") == 4:
        return [lax.bitwise_xor(src, block) for block in wanted]
    return [block - src + depth // 2 for block in wanted]


def times(values, blocks):
    both = jnp.dot(values, blocks, preferred_element_type=jnp.float32)
    rows, width = both.shape[0] // 2, both.shape[1] // 2
    return both[:rows, :width] - both[rows:, width:], both[:rows, width:] + both[rows:, :width]


def rows_of(panel):
    return panel[...].reshape(2 * panel.shape[1], panel.shape[2])


def product(window, aperture_ref, panels):
    blocks = []
    for m, panel in panels.items():
        entries = slot_entries(aperture_ref, m, panel.shape[-1] // BLK, window.shape[0])
        blocks += [window[k] for k in entries]
    values = jnp.concatenate([rows_of(panel) for panel in panels.values()], axis=1)
    return times(values, jnp.concatenate(blocks, axis=0))


def sum_of_late(aperture_ref, panels, late, depth):
    total = None
    for m, panel in panels.items():
        values = rows_of(panel)
        for q, k in enumerate(slot_entries(aperture_ref, m, panel.shape[-1] // BLK, depth)):
            term = values[:, q * BLK : (q + 1) * BLK].astype(jnp.float32) * jnp.where(k == late, 1.0, 0.0)
            total = term if total is None else total + term
    return total


def in_two(total):
    high = total.astype(jnp.bfloat16)
    low = (total - high.astype(jnp.float32)).astype(jnp.bfloat16)
    return jnp.concatenate([high, low], axis=1)


def add_late(total_in_two, window, late):
    block = window[late]
    return times(total_in_two, jnp.concatenate([block, block], axis=0))


def kernel_a(near_half, ats, late, aperture_ref, *refs):
    panel_refs = refs[:near_half]
    piece_refs = list(refs[near_half:-6])
    windows, sums, parts = refs[-6:-4], refs[-4:-2], refs[-2:]
    for v, (window, at) in enumerate(zip(windows, ats)):
        window[late] = jnp.zeros(window.shape[1:], window.dtype)
        fill_window(window, {k: piece_refs.pop(0).at[index] for k, index in at.items()})
        panels = {m: ref.at[v] for m, ref in enumerate(panel_refs)}
        parts[v][0], parts[v][1] = product(window, aperture_ref, panels)
        sums[v][...] = sum_of_late(aperture_ref, panels, late, window.shape[0])


def kernel_b(m, late, aperture_ref, late_ref, _, last_window, first_sum, last_sum, first_in, last_in, panel_ref, *refs):
    window, two, first_part, last_part = refs
    fill_window(window, {late: late_ref.at[0]})
    real, imag = product(window, aperture_ref, {m: panel_ref.at[0]})
    late_real, late_imag = add_late(in_two(first_sum[...]), window, late)
    first_part[0] = first_in[0] + (real + late_real)
    first_part[1] = first_in[1] + (imag + late_imag)
    panels = {m: panel_ref.at[1]}
    real, imag = product(last_window, aperture_ref, panels)
    last_part[0] = last_in[0] + real
    last_part[1] = last_in[1] + imag
    two[...] = in_two(last_sum[...] + sum_of_late(aperture_ref, panels, late, last_window.shape[0]))


def last_kernel(far_half, late, aperture_ref, late_ref, first_window, _, two, first_part, last_part, *refs):
    *panel_refs, out_ref, window, result, sems = refs

    def finish(v, part, real, imag):
        copies = [pltpu.make_async_copy(result.at[v, p], out_ref.at[v, p], sems.at[v, p]) for p in range(2)]
        for p, value in enumerate((real, imag)):
            result[v, p] = part[p] + value
            copies[p].start()
        return copies

    panels = [{far_half + m: ref.at[v] for m, ref in enumerate(panel_refs)} for v in range(2)]
    copies = finish(0, first_part, *product(first_window, aperture_ref, panels[0]))
    fill_window(window, {late: late_ref.at[0]})
    real, imag = product(window, aperture_ref, panels[1])
    late_real, late_imag = add_late(two[...], window, late)
    copies += finish(1, last_part, real + late_real, imag + late_imag)
    for copy in copies:
        copy.wait()


def spec(space):
    return pl.BlockSpec(memory_space=space)


def cost(share):
    return pl.CostEstimate(flops=int(share * (8 * BLK * BLK * APER * BLK)), bytes_accessed=1 << 20, transcendentals=0)


def limit(megabytes):
    return pltpu.CompilerParams(vmem_limit_bytes=megabytes << 20)


def held(piece, token):
    return pl.pallas_call(
        lambda piece_ref, token_ref, out_ref: None,
        out_shape=jax.ShapeDtypeStruct(piece.shape, piece.dtype),
        in_specs=[spec(pl.ANY)] * 2,
        out_specs=spec(pl.ANY),
        input_output_aliases={0: 0},
        compiler_params=limit(1),
        cost_estimate=cost(12),
    )(piece, token)


def body(primaries, data, aperture):
    width = data.shape[3]
    line = lax.axis_size("src") == 4
    windows = (line_window if line else hop_window)(data)
    panels, far_panel = gather_panels(primaries)
    half = len(panels)
    late = 2 if line else len(windows[0]) - 1
    late_pieces = [piece[at : at + 1] for piece, at in (window[late] for window in windows)]
    early = [{k: piece for k, piece in enumerate(window) if k != late} for window in windows]
    vmem, smem, anywhere = spec(pltpu.VMEM), spec(pltpu.SMEM), spec(pl.ANY)
    window = jax.ShapeDtypeStruct((len(windows[0]), BLK, 2 * width), jnp.bfloat16)
    total = jax.ShapeDtypeStruct((2 * BLK, BLK), jnp.float32)
    part = jax.ShapeDtypeStruct((2, BLK, width), jnp.float32)

    pieces = [piece for window_pieces in early for piece, _ in window_pieces.values()]
    first, last, first_sum, last_sum, first_part, last_part = pl.pallas_call(
        functools.partial(kernel_a, half, [{k: at for k, (_, at) in pieces.items()} for pieces in early], late),
        out_shape=[window] * 2 + [total] * 2 + [part] * 2,
        in_specs=[smem] + [vmem] * (half + len(pieces)),
        out_specs=[vmem] * 6,
        compiler_params=limit(16),
        cost_estimate=cost(0.1),
    )(aperture, *panels, *pieces)

    handed_on = hand_on(far_panel, first_part)
    first, two, first_part, last_part = pl.pallas_call(
        functools.partial(kernel_b, half, late),
        out_shape=[window, jax.ShapeDtypeStruct((2 * BLK, 2 * BLK), jnp.bfloat16), part, part],
        in_specs=[smem] + [vmem] * 8,
        out_specs=[vmem] * 4,
        input_output_aliases={2: 0, 6: 2, 7: 3},
        compiler_params=limit(16),
        cost_estimate=cost(0.1),
    )(aperture, late_pieces[0], first, last, first_sum, last_sum, first_part, last_part, far_panel)

    return pl.pallas_call(
        functools.partial(last_kernel, half + 1, late),
        out_shape=[jax.ShapeDtypeStruct((2, 2, BLK, width), jnp.float32), window],
        in_specs=[smem] + [vmem] * (6 + len(handed_on)),
        out_specs=[anywhere, vmem],
        scratch_shapes=[pltpu.VMEM((2, 2, BLK, width), jnp.float32), pltpu.SemaphoreType.DMA((2, 2))],
        input_output_aliases={3: 1},
        compiler_params=limit(16),
        cost_estimate=cost(1),
    )(aperture, held(late_pieces[1], two), first, last, two, first_part, last_part, *handed_on)[0]


def solution(mesh):
    placed = (P("freq", None, "src", "rcv"), P("freq", None, "src", "rcv"), P())
    return jax.shard_map(
        body, mesh=mesh, in_specs=placed, out_specs=P("freq", None, "src", "rcv"), check_vma=False
    )
```

```python
import functools

import jax
import jax.numpy as jnp
from jax import lax
from jax.experimental import pallas as pl
from jax.experimental.pallas import tpu as pltpu
from jax.sharding import PartitionSpec as P

BLK = 256
APER = 12
HW = 6


def after(value, *earlier):
    return lax.optimization_barrier((value, *earlier))[0]


def from_behind(x, axis, by):
    peers = lax.axis_size(axis)
    pairs = [(i, i + by) for i in range(peers) if 0 <= i + by < peers]
    return lax.ppermute(x, axis, pairs)


def swap(x, axis, bit):
    peers = lax.axis_size(axis)
    return lax.ppermute(x, axis, [(i, i ^ bit) for i in range(peers)])


def at_end():
    return (lax.axis_index("src") + 1) % lax.axis_size("src") < 2


def line_window(data, others):
    windows = []
    for v, own in enumerate(lax.optimization_barrier([data[v : v + 1] for v in range(data.shape[0])])):
        begun = own if v == 0 else after(own, *others)
        near = lax.ppermute(begun, "src", [(0, 1), (1, 0), (2, 3), (3, 2)])
        far = lax.ppermute(begun, "src", [(0, 3), (1, 2), (2, 1), (3, 0)])
        onward = jnp.where(at_end(), after(own, near), far)
        across = lax.ppermute(onward, "src", [(0, 2), (2, 3), (3, 1), (1, 0)])
        windows.append([(own, 0), (near, 0), (across, 0), (far, 0)])
    return windows


def hop_window(data, others):
    reach = min(HW, lax.axis_size("src") - 1)
    window = {0: data}
    for hop in range(1, reach + 1):
        window[-hop] = from_behind(window[1 - hop], "src", 1)
        window[hop] = from_behind(window[hop - 1], "src", -1)
    return [[(window[distance], v) for distance in range(-reach, reach + 1)] for v in range(data.shape[0])]


def gather_panels(primaries):
    bit = lax.axis_size("rcv") // 2
    panels = [primaries]
    for lower in range(1, bit):
        panels.append(swap(panels[lower & (lower - 1)], "rcv", lower & -lower))
    return panels, swap(primaries, "rcv", bit)


def hand_on(panel, token):
    bit = lax.axis_size("rcv") // 2
    panels = [after(panel, token)]
    for lower in range(1, bit):
        panels.append(swap(panels[lower & (lower - 1)], "rcv", lower & -lower))
    return panels[1:]


def fill_window(window, pieces):
    width = window.shape[-1] // 2
    for k, piece in pieces.items():
        window[k, :, :width] = piece[0]
        window[k, :, width:] = piece[1]


def slot_entries(aperture_ref, m, per_shard, depth):
    src = lax.axis_index("src")
    shard = lax.bitwise_xor(lax.axis_index("rcv"), m)
    wanted = [aperture_ref[src, shard * per_shard + q] for q in range(per_shard)]
    if lax.axis_size("src") == 4:
        return [lax.bitwise_xor(src, block) for block in wanted]
    return [block - src + depth // 2 for block in wanted]


def times(values, blocks):
    both = jnp.dot(values, blocks, preferred_element_type=jnp.float32)
    rows, width = both.shape[0] // 2, both.shape[1] // 2
    return both[:rows, :width] - both[rows:, width:], both[:rows, width:] + both[rows:, :width]


def rows_of(panel):
    return panel[...].reshape(2 * panel.shape[1], panel.shape[2])


def product(window, aperture_ref, panels):
    blocks = []
    for m, panel in panels.items():
        entries = slot_entries(aperture_ref, m, panel.shape[-1] // BLK, window.shape[0])
        blocks += [window[k] for k in entries]
    values = jnp.concatenate([rows_of(panel) for panel in panels.values()], axis=1)
    return times(values, jnp.concatenate(blocks, axis=0))


def sum_of_late(aperture_ref, panels, late, depth):
    total = None
    for m, panel in panels.items():
        values = rows_of(panel)
        for q, k in enumerate(slot_entries(aperture_ref, m, panel.shape[-1] // BLK, depth)):
            term = values[:, q * BLK : (q + 1) * BLK].astype(jnp.float32) * jnp.where(k == late, 1.0, 0.0)
            total = term if total is None else total + term
    return total


def in_two(total):
    high = total.astype(jnp.bfloat16)
    low = (total - high.astype(jnp.float32)).astype(jnp.bfloat16)
    return jnp.concatenate([high, low], axis=1)


def add_late(total_in_two, window, late):
    block = window[late]
    return times(total_in_two, jnp.concatenate([block, block], axis=0))


def kernel_a(near_half, ats, late, aperture_ref, *refs):
    panel_refs = refs[:near_half]
    piece_refs = list(refs[near_half:-6])
    windows, sums, parts = refs[-6:-4], refs[-4:-2], refs[-2:]
    for v, (window, at) in enumerate(zip(windows, ats)):
        window[late] = jnp.zeros(window.shape[1:], window.dtype)
        fill_window(window, {k: piece_refs.pop(0).at[index] for k, index in at.items()})
        panels = {m: ref.at[v] for m, ref in enumerate(panel_refs)}
        parts[v][0], parts[v][1] = product(window, aperture_ref, panels)
        sums[v][...] = sum_of_late(aperture_ref, panels, late, window.shape[0])


def kernel_b(late, late_ref, _, first_sum, first_in, window, first_part):
    fill_window(window, {late: late_ref.at[0]})
    real, imag = add_late(in_two(first_sum[...]), window, late)
    first_part[0] = first_in[0] + real
    first_part[1] = first_in[1] + imag


def kernel_c(m, late, aperture_ref, first_window, last_window, last_sum, first_in, last_in, panel_ref, *refs):
    two, *parts = refs
    for v, (window, part_in, part) in enumerate(zip((first_window, last_window), (first_in, last_in), parts)):
        real, imag = product(window, aperture_ref, {m: panel_ref.at[v]})
        part[0] = part_in[0] + real
        part[1] = part_in[1] + imag
    panels = {m: panel_ref.at[1]}
    two[...] = in_two(last_sum[...] + sum_of_late(aperture_ref, panels, late, last_window.shape[0]))


def last_kernel(far_half, late, aperture_ref, late_ref, first_window, _, two, first_part, last_part, *refs):
    *panel_refs, out_ref, window, result, sems = refs

    def finish(v, part, real, imag):
        copies = [pltpu.make_async_copy(result.at[v, p], out_ref.at[v, p], sems.at[v, p]) for p in range(2)]
        for p, value in enumerate((real, imag)):
            result[v, p] = part[p] + value
            copies[p].start()
        return copies

    panels = [{far_half + m: ref.at[v] for m, ref in enumerate(panel_refs)} for v in range(2)]
    copies = finish(0, first_part, *product(first_window, aperture_ref, panels[0]))
    fill_window(window, {late: late_ref.at[0]})
    real, imag = product(window, aperture_ref, panels[1])
    late_real, late_imag = add_late(two[...], window, late)
    copies += finish(1, last_part, real + late_real, imag + late_imag)
    for copy in copies:
        copy.wait()


def spec(space):
    return pl.BlockSpec(memory_space=space)


def cost(share):
    return pl.CostEstimate(flops=int(share * (8 * BLK * BLK * APER * BLK)), bytes_accessed=1 << 20, transcendentals=0)


def limit(megabytes):
    return pltpu.CompilerParams(vmem_limit_bytes=megabytes << 20)


def held(piece, token):
    return pl.pallas_call(
        lambda piece_ref, token_ref, out_ref: None,
        out_shape=jax.ShapeDtypeStruct(piece.shape, piece.dtype),
        in_specs=[spec(pl.ANY)] * 2,
        out_specs=spec(pl.ANY),
        input_output_aliases={0: 0},
        compiler_params=limit(1),
        cost_estimate=cost(12),
    )(piece, token)


def body(primaries, data, aperture):
    width = data.shape[3]
    line = lax.axis_size("src") == 4
    panels, far_panel = gather_panels(primaries)
    half = len(panels)
    windows = (line_window if line else hop_window)(data, panels[1:])
    late = 2 if line else len(windows[0]) - 1
    late_pieces = [piece[at : at + 1] for piece, at in (window[late] for window in windows)]
    early = [{k: piece for k, piece in enumerate(window) if k != late} for window in windows]
    vmem, smem, anywhere = spec(pltpu.VMEM), spec(pltpu.SMEM), spec(pl.ANY)
    window = jax.ShapeDtypeStruct((len(windows[0]), BLK, 2 * width), jnp.bfloat16)
    total = jax.ShapeDtypeStruct((2 * BLK, BLK), jnp.float32)
    part = jax.ShapeDtypeStruct((2, BLK, width), jnp.float32)

    pieces = [piece for window_pieces in early for piece, _ in window_pieces.values()]
    first, last, first_sum, last_sum, first_part, last_part = pl.pallas_call(
        functools.partial(kernel_a, half, [{k: at for k, (_, at) in pieces.items()} for pieces in early], late),
        out_shape=[window] * 2 + [total] * 2 + [part] * 2,
        in_specs=[smem] + [vmem] * (half + len(pieces)),
        out_specs=[vmem] * 6,
        compiler_params=limit(16),
        cost_estimate=cost(0.1),
    )(aperture, *panels, *pieces)

    first, first_part = pl.pallas_call(
        functools.partial(kernel_b, late),
        out_shape=[window, part],
        in_specs=[vmem] * 4,
        out_specs=[vmem] * 2,
        input_output_aliases={1: 0, 3: 1},
        compiler_params=limit(16),
        cost_estimate=cost(0.1),
    )(late_pieces[0], first, first_sum, first_part)

    handed_on = hand_on(far_panel, first_part)
    two, first_part, last_part = pl.pallas_call(
        functools.partial(kernel_c, half, late),
        out_shape=[jax.ShapeDtypeStruct((2 * BLK, 2 * BLK), jnp.bfloat16), part, part],
        in_specs=[smem] + [vmem] * 6,
        out_specs=[vmem] * 3,
        input_output_aliases={4: 1, 5: 2},
        compiler_params=limit(16),
        cost_estimate=cost(0.1),
    )(aperture, first, last, last_sum, first_part, last_part, far_panel)

    return pl.pallas_call(
        functools.partial(last_kernel, half + 1, late),
        out_shape=[jax.ShapeDtypeStruct((2, 2, BLK, width), jnp.float32), window],
        in_specs=[smem] + [vmem] * (6 + len(handed_on)),
        out_specs=[anywhere, vmem],
        scratch_shapes=[pltpu.VMEM((2, 2, BLK, width), jnp.float32), pltpu.SemaphoreType.DMA((2, 2))],
        input_output_aliases={3: 1},
        compiler_params=limit(16),
        cost_estimate=cost(1),
    )(aperture, held(late_pieces[1], two), first, last, two, first_part, last_part, *handed_on)[0]


def solution(mesh):
    placed = (P("freq", None, "src", "rcv"), P("freq", None, "src", "rcv"), P())
    return jax.shard_map(
        body, mesh=mesh, in_specs=placed, out_specs=P("freq", None, "src", "rcv"), check_vma=False
    )
```

```python
import functools

import jax
import jax.numpy as jnp
from jax import lax
from jax.experimental import pallas as pl
from jax.experimental.pallas import tpu as pltpu
from jax.sharding import PartitionSpec as P

BLK = 256
APER = 12
HW = 6
PIECES = 4


def after(value, *earlier):
    return lax.optimization_barrier((value, *earlier))[0]


def from_behind(x, axis, by):
    peers = lax.axis_size(axis)
    pairs = [(i, i + by) for i in range(peers) if 0 <= i + by < peers]
    return lax.ppermute(x, axis, pairs)


def swap(x, axis, bit):
    peers = lax.axis_size(axis)
    return lax.ppermute(x, axis, [(i, i ^ bit) for i in range(peers)])


def at_end():
    return (lax.axis_index("src") + 1) % lax.axis_size("src") < 2


def line_window(data):
    middle = lax.ppermute(data, "src", [(0, 0), (1, 2), (2, 1), (3, 3)])
    near = lax.ppermute(data, "src", [(0, 1), (1, 0), (2, 3), (3, 2)])
    ends = lax.ppermute(data, "src", [(0, 3), (1, 1), (2, 2), (3, 0)])
    windows = []
    for v in range(data.shape[0]):
        onward = middle
        across = lax.ppermute(onward[v : v + 1], "src", [(0, 2), (2, 3), (3, 1), (1, 0)])
        windows.append([(data, v), (near, v), (across, 0), (middle, v), (ends, v)])
    return windows


def hop_window(data):
    reach = min(HW, lax.axis_size("src") - 1)
    window = {0: data}
    for hop in range(1, reach + 1):
        window[-hop] = from_behind(window[1 - hop], "src", 1)
        window[hop] = from_behind(window[hop - 1], "src", -1)
    return [[(window[distance], v) for distance in range(-reach, reach + 1)] for v in range(data.shape[0])]


def gather_panels(primaries):
    bit = lax.axis_size("rcv") // 2
    panels = [primaries]
    for lower in range(1, bit):
        panels.append(swap(panels[lower & (lower - 1)], "rcv", lower & -lower))
    return panels, swap(primaries, "rcv", bit)


def hand_on(panel, token):
    bit = lax.axis_size("rcv") // 2
    panels = [after(panel, token)]
    for lower in range(1, bit):
        panels.append(swap(panels[lower & (lower - 1)], "rcv", lower & -lower))
    return panels[1:]


def fill_window(window, pieces):
    width = window.shape[-1] // 2
    for k, piece in pieces.items():
        if k < window.shape[0]:
            for part in range(2):
                block = piece[part]
                if k + 1 == window.shape[0] and k + 1 in pieces:
                    block = jnp.where(at_end(), pieces[k + 1][part], block)
                window[k, :, part * width : (part + 1) * width] = block


def slot_entries(aperture_ref, m, per_shard, depth):
    src = lax.axis_index("src")
    shard = lax.bitwise_xor(lax.axis_index("rcv"), m)
    wanted = [aperture_ref[src, shard * per_shard + q] for q in range(per_shard)]
    if lax.axis_size("src") == 4:
        return [lax.bitwise_xor(src, block) for block in wanted]
    return [block - src + depth // 2 for block in wanted]


def times(values, blocks):
    both = jnp.dot(values, blocks, preferred_element_type=jnp.float32)
    rows, width = both.shape[0] // 2, both.shape[1] // 2
    return both[:rows, :width] - both[rows:, width:], both[:rows, width:] + both[rows:, :width]


def rows_of(panel):
    return panel[...].reshape(2 * panel.shape[1], panel.shape[2])


def product(window, aperture_ref, panels, late_in_two=None, late=None):
    blocks = []
    for m, panel in panels.items():
        entries = slot_entries(aperture_ref, m, panel.shape[-1] // BLK, window.shape[0])
        blocks += [window[k] for k in entries]
    values = [rows_of(panel) for panel in panels.values()]
    if late_in_two is not None:
        values.append(late_in_two)
        blocks += [window[late]] * 2
    return times(jnp.concatenate(values, axis=1), jnp.concatenate(blocks, axis=0))


def sum_of_late(aperture_ref, panels, late, depth):
    total = None
    for m, panel in panels.items():
        values = rows_of(panel)
        for q, k in enumerate(slot_entries(aperture_ref, m, panel.shape[-1] // BLK, depth)):
            term = values[:, q * BLK : (q + 1) * BLK].astype(jnp.float32) * jnp.where(k == late, 1.0, 0.0)
            total = term if total is None else total + term
    return total


def in_two(total):
    high = total.astype(jnp.bfloat16)
    low = (total - high.astype(jnp.float32)).astype(jnp.bfloat16)
    return jnp.concatenate([high, low], axis=1)


def kernel_a(near_half, ats, late, aperture_ref, *refs):
    panel_refs = refs[:near_half]
    piece_refs = list(refs[near_half:-6])
    windows, sums, parts = refs[-6:-4], refs[-4:-2], refs[-2:]
    for v, (window, at) in enumerate(zip(windows, ats)):
        window[late] = jnp.zeros(window.shape[1:], window.dtype)
        fill_window(window, {k: piece_refs.pop(0).at[index] for k, index in at.items()})
        panels = {m: ref.at[v] for m, ref in enumerate(panel_refs)}
        parts[v][0], parts[v][1] = product(window, aperture_ref, panels)
        sums[v][...] = sum_of_late(aperture_ref, panels, late, window.shape[0])


def kernel_b(m, late, aperture_ref, late_ref, _, last_window, first_sum, last_sum, first_in, last_in, panel_ref, *refs):
    window, two, first_part, last_part = refs
    fill_window(window, {late: late_ref.at[0]})
    real, imag = product(window, aperture_ref, {m: panel_ref.at[0]}, in_two(first_sum[...]), late)
    first_part[0] = first_in[0] + real
    first_part[1] = first_in[1] + imag
    panels = {m: panel_ref.at[1]}
    real, imag = product(last_window, aperture_ref, panels)
    last_part[0] = last_in[0] + real
    last_part[1] = last_in[1] + imag
    two[...] = in_two(last_sum[...] + sum_of_late(aperture_ref, panels, late, last_window.shape[0]))


def last_kernel(far_half, late, aperture_ref, late_ref, first_window, _, two, first_part, last_part, *refs):
    *panel_refs, out_ref, window, result, sems = refs

    def finish(v, part, real, imag):
        copies = []
        for p, value in enumerate((real, imag)):
            result[v, p] = part[p] + value
            for chunk in range(PIECES):
                rows = pl.ds(chunk * (BLK // PIECES), BLK // PIECES)
                copies.append(
                    pltpu.make_async_copy(result.at[v, p, rows], out_ref.at[v, p, rows], sems.at[v, p, chunk])
                )
                copies[-1].start()
        return copies

    panels = [{far_half + m: ref.at[v] for m, ref in enumerate(panel_refs)} for v in range(2)]
    copies = finish(0, first_part, *product(first_window, aperture_ref, panels[0]))
    fill_window(window, {late: late_ref.at[0]})
    copies += finish(1, last_part, *product(window, aperture_ref, panels[1], two[...], late))
    for copy in copies:
        copy.wait()


def spec(space):
    return pl.BlockSpec(memory_space=space)


def cost(share):
    return pl.CostEstimate(flops=int(share * (8 * BLK * BLK * APER * BLK)), bytes_accessed=1 << 20, transcendentals=0)


def limit(megabytes):
    return pltpu.CompilerParams(vmem_limit_bytes=megabytes << 20)


def held(piece, token):
    return pl.pallas_call(
        lambda piece_ref, token_ref, out_ref: None,
        out_shape=jax.ShapeDtypeStruct(piece.shape, piece.dtype),
        in_specs=[spec(pl.ANY)] * 2,
        out_specs=spec(pl.ANY),
        input_output_aliases={0: 0},
        compiler_params=limit(1),
        cost_estimate=cost(12),
    )(piece, token)


def body(primaries, data, aperture):
    width = data.shape[3]
    line = lax.axis_size("src") == 4
    windows = (line_window if line else hop_window)(data)
    panels, far_panel = gather_panels(primaries)
    half = len(panels)
    late = 2 if line else len(windows[0]) - 1
    late_pieces = [piece[at : at + 1] for piece, at in (window[late] for window in windows)]
    early = [{k: piece for k, piece in enumerate(window) if k != late} for window in windows]
    vmem, smem, anywhere = spec(pltpu.VMEM), spec(pltpu.SMEM), spec(pl.ANY)
    window = jax.ShapeDtypeStruct((4 if line else len(windows[0]), BLK, 2 * width), jnp.bfloat16)
    total = jax.ShapeDtypeStruct((2 * BLK, BLK), jnp.float32)
    part = jax.ShapeDtypeStruct((2, BLK, width), jnp.float32)

    pieces = [piece for window_pieces in early for piece, _ in window_pieces.values()]
    first, last, first_sum, last_sum, first_part, last_part = pl.pallas_call(
        functools.partial(kernel_a, half, [{k: at for k, (_, at) in pieces.items()} for pieces in early], late),
        out_shape=[window] * 2 + [total] * 2 + [part] * 2,
        in_specs=[smem] + [vmem] * (half + len(pieces)),
        out_specs=[vmem] * 6,
        compiler_params=limit(16),
        cost_estimate=cost(0.1),
    )(aperture, *panels, *pieces)

    handed_on = hand_on(far_panel, first_part)
    first, two, first_part, last_part = pl.pallas_call(
        functools.partial(kernel_b, half, late),
        out_shape=[window, jax.ShapeDtypeStruct((2 * BLK, 2 * BLK), jnp.bfloat16), part, part],
        in_specs=[smem] + [vmem] * 8,
        out_specs=[vmem] * 4,
        input_output_aliases={2: 0, 6: 2, 7: 3},
        compiler_params=limit(16),
        cost_estimate=cost(0.1),
    )(aperture, late_pieces[0], first, last, first_sum, last_sum, first_part, last_part, far_panel)

    return pl.pallas_call(
        functools.partial(last_kernel, half + 1, late),
        out_shape=[jax.ShapeDtypeStruct((2, 2, BLK, width), jnp.float32), window],
        in_specs=[smem] + [vmem] * (6 + len(handed_on)),
        out_specs=[anywhere, vmem],
        scratch_shapes=[pltpu.VMEM((2, 2, BLK, width), jnp.float32), pltpu.SemaphoreType.DMA((2, 2, PIECES))],
        input_output_aliases={3: 1},
        compiler_params=limit(16),
        cost_estimate=cost(1),
    )(aperture, held(late_pieces[1], two), first, last, two, first_part, last_part, *handed_on)[0]


def solution(mesh):
    placed = (P("freq", None, "src", "rcv"), P("freq", None, "src", "rcv"), P())
    return jax.shard_map(
        body, mesh=mesh, in_specs=placed, out_specs=P("freq", None, "src", "rcv"), check_vma=False
    )
```

```python
import functools

import jax
import jax.numpy as jnp
from jax import lax
from jax.experimental import pallas as pl
from jax.experimental.pallas import tpu as pltpu
from jax.sharding import PartitionSpec as P

BLK = 256
APER = 12
HW = 6
PIECES = 1


def after(value, *earlier):
    return lax.optimization_barrier((value, *earlier))[0]


def from_behind(x, axis, by):
    peers = lax.axis_size(axis)
    pairs = [(i, i + by) for i in range(peers) if 0 <= i + by < peers]
    return lax.ppermute(x, axis, pairs)


def swap(x, axis, bit):
    peers = lax.axis_size(axis)
    return lax.ppermute(x, axis, [(i, i ^ bit) for i in range(peers)])


def at_end():
    return (lax.axis_index("src") + 1) % lax.axis_size("src") < 2


def line_window(data):
    near = lax.ppermute(data, "src", [(0, 1), (1, 0), (2, 3), (3, 2)])
    windows = []
    for v in range(data.shape[0]):
        own = (after(data, windows[-1][0][0]) if windows else data)[v : v + 1]
        far = lax.ppermute(own, "src", [(0, 3), (1, 2), (2, 1), (3, 0)])
        onward = jnp.where(at_end(), own, far)
        across = lax.ppermute(onward, "src", [(0, 2), (2, 3), (3, 1), (1, 0)])
        windows.append([(own, 0), (near, v), (across, 0), (far, 0)])
    return windows


def hop_window(data):
    reach = min(HW, lax.axis_size("src") - 1)
    window = {0: data}
    for hop in range(1, reach + 1):
        window[-hop] = from_behind(window[1 - hop], "src", 1)
        window[hop] = from_behind(window[hop - 1], "src", -1)
    return [[(window[distance], v) for distance in range(-reach, reach + 1)] for v in range(data.shape[0])]


def gather_panels(primaries):
    bit = lax.axis_size("rcv") // 2
    panels = [primaries]
    for lower in range(1, bit):
        panels.append(swap(panels[lower & (lower - 1)], "rcv", lower & -lower))
    return panels, swap(primaries, "rcv", bit)


def hand_on(panel, token):
    bit = lax.axis_size("rcv") // 2
    panels = [after(panel, token)]
    for lower in range(1, bit):
        panels.append(swap(panels[lower & (lower - 1)], "rcv", lower & -lower))
    return panels[1:]


def fill_window(window, pieces):
    width = window.shape[-1] // 2
    for k, piece in pieces.items():
        window[k, :, :width] = piece[0]
        window[k, :, width:] = piece[1]


def slot_entries(aperture_ref, m, per_shard, depth):
    src = lax.axis_index("src")
    shard = lax.bitwise_xor(lax.axis_index("rcv"), m)
    wanted = [aperture_ref[src, shard * per_shard + q] for q in range(per_shard)]
    if lax.axis_size("src") == 4:
        return [lax.bitwise_xor(src, block) for block in wanted]
    return [block - src + depth // 2 for block in wanted]


def times(values, blocks):
    both = jnp.dot(values, blocks, preferred_element_type=jnp.float32)
    rows, width = both.shape[0] // 2, both.shape[1] // 2
    return both[:rows, :width] - both[rows:, width:], both[:rows, width:] + both[rows:, :width]


def rows_of(panel):
    return panel[...].reshape(2 * panel.shape[1], panel.shape[2])


def product(window, aperture_ref, panels, late_in_two=None, late=None):
    blocks = []
    for m, panel in panels.items():
        entries = slot_entries(aperture_ref, m, panel.shape[-1] // BLK, window.shape[0])
        blocks += [window[k] for k in entries]
    values = [rows_of(panel) for panel in panels.values()]
    if late_in_two is not None:
        values.append(late_in_two)
        blocks += [window[late]] * 2
    return times(jnp.concatenate(values, axis=1), jnp.concatenate(blocks, axis=0))


def sum_of_late(aperture_ref, panels, late, depth):
    total = None
    for m, panel in panels.items():
        values = rows_of(panel)
        for q, k in enumerate(slot_entries(aperture_ref, m, panel.shape[-1] // BLK, depth)):
            term = values[:, q * BLK : (q + 1) * BLK].astype(jnp.float32) * jnp.where(k == late, 1.0, 0.0)
            total = term if total is None else total + term
    return total


def in_two(total):
    high = total.astype(jnp.bfloat16)
    low = (total - high.astype(jnp.float32)).astype(jnp.bfloat16)
    return jnp.concatenate([high, low], axis=1)


def kernel_a(near_half, ats, late, aperture_ref, *refs):
    panel_refs = refs[:near_half]
    piece_refs = list(refs[near_half:-6])
    windows, sums, parts = refs[-6:-4], refs[-4:-2], refs[-2:]
    for v, (window, at) in enumerate(zip(windows, ats)):
        window[late] = jnp.zeros(window.shape[1:], window.dtype)
        fill_window(window, {k: piece_refs.pop(0).at[index] for k, index in at.items()})
        panels = {m: ref.at[v] for m, ref in enumerate(panel_refs)}
        parts[v][0], parts[v][1] = product(window, aperture_ref, panels)
        sums[v][...] = sum_of_late(aperture_ref, panels, late, window.shape[0])


def kernel_b(m, late, aperture_ref, late_ref, _, last_window, first_sum, last_sum, first_in, last_in, panel_ref, *refs):
    window, two, first_part, last_part = refs
    fill_window(window, {late: late_ref.at[0]})
    real, imag = product(window, aperture_ref, {m: panel_ref.at[0]}, in_two(first_sum[...]), late)
    first_part[0] = first_in[0] + real
    first_part[1] = first_in[1] + imag
    panels = {m: panel_ref.at[1]}
    real, imag = product(last_window, aperture_ref, panels)
    last_part[0] = last_in[0] + real
    last_part[1] = last_in[1] + imag
    two[...] = in_two(last_sum[...] + sum_of_late(aperture_ref, panels, late, last_window.shape[0]))


def last_kernel(far_half, late, aperture_ref, late_ref, first_window, _, two, first_part, last_part, *refs):
    *panel_refs, out_ref, window, result, sems = refs

    def finish(v, part, real, imag):
        copies = []
        for p, value in enumerate((real, imag)):
            result[v, p] = part[p] + value
            for chunk in range(PIECES):
                rows = pl.ds(chunk * (BLK // PIECES), BLK // PIECES)
                copies.append(
                    pltpu.make_async_copy(result.at[v, p, rows], out_ref.at[v, p, rows], sems.at[v, p, chunk])
                )
                copies[-1].start()
        return copies

    panels = [{far_half + m: ref.at[v] for m, ref in enumerate(panel_refs)} for v in range(2)]
    copies = finish(0, first_part, *product(first_window, aperture_ref, panels[0]))
    fill_window(window, {late: late_ref.at[0]})
    copies += finish(1, last_part, *product(window, aperture_ref, panels[1], two[...], late))
    for copy in copies:
        copy.wait()


def spec(space):
    return pl.BlockSpec(memory_space=space)


def cost(share):
    return pl.CostEstimate(flops=int(share * (8 * BLK * BLK * APER * BLK)), bytes_accessed=1 << 20, transcendentals=0)


def limit(megabytes):
    return pltpu.CompilerParams(vmem_limit_bytes=megabytes << 20)


def held(piece, token):
    return pl.pallas_call(
        lambda piece_ref, token_ref, out_ref: None,
        out_shape=jax.ShapeDtypeStruct(piece.shape, piece.dtype),
        in_specs=[spec(pl.ANY)] * 2,
        out_specs=spec(pl.ANY),
        input_output_aliases={0: 0},
        compiler_params=limit(1),
        cost_estimate=cost(12),
    )(piece, token)


def body(primaries, data, aperture):
    width = data.shape[3]
    line = lax.axis_size("src") == 4
    windows = (line_window if line else hop_window)(data)
    panels, far_panel = gather_panels(primaries)
    half = len(panels)
    late = 2 if line else len(windows[0]) - 1
    late_pieces = [piece[at : at + 1] for piece, at in (window[late] for window in windows)]
    early = [{k: piece for k, piece in enumerate(window) if k != late} for window in windows]
    vmem, smem, anywhere = spec(pltpu.VMEM), spec(pltpu.SMEM), spec(pl.ANY)
    window = jax.ShapeDtypeStruct((len(windows[0]), BLK, 2 * width), jnp.bfloat16)
    total = jax.ShapeDtypeStruct((2 * BLK, BLK), jnp.float32)
    part = jax.ShapeDtypeStruct((2, BLK, width), jnp.float32)

    pieces = [piece for window_pieces in early for piece, _ in window_pieces.values()]
    first, last, first_sum, last_sum, first_part, last_part = pl.pallas_call(
        functools.partial(kernel_a, half, [{k: at for k, (_, at) in pieces.items()} for pieces in early], late),
        out_shape=[window] * 2 + [total] * 2 + [part] * 2,
        in_specs=[smem] + [vmem] * (half + len(pieces)),
        out_specs=[vmem] * 6,
        compiler_params=limit(16),
        cost_estimate=cost(0.1),
    )(aperture, *panels, *pieces)

    handed_on = hand_on(far_panel, first_part)
    first, two, first_part, last_part = pl.pallas_call(
        functools.partial(kernel_b, half, late),
        out_shape=[window, jax.ShapeDtypeStruct((2 * BLK, 2 * BLK), jnp.bfloat16), part, part],
        in_specs=[smem] + [vmem] * 8,
        out_specs=[vmem] * 4,
        input_output_aliases={2: 0, 6: 2, 7: 3},
        compiler_params=limit(16),
        cost_estimate=cost(0.1),
    )(aperture, late_pieces[0], first, last, first_sum, last_sum, first_part, last_part, far_panel)

    return pl.pallas_call(
        functools.partial(last_kernel, half + 1, late),
        out_shape=[jax.ShapeDtypeStruct((2, 2, BLK, width), jnp.float32), window],
        in_specs=[smem] + [vmem] * (6 + len(handed_on)),
        out_specs=[anywhere, vmem],
        scratch_shapes=[pltpu.VMEM((2, 2, BLK, width), jnp.float32), pltpu.SemaphoreType.DMA((2, 2, PIECES))],
        input_output_aliases={3: 1},
        compiler_params=limit(16),
        cost_estimate=cost(1),
    )(aperture, held(late_pieces[1], two), first, last, two, first_part, last_part, *handed_on)[0]


def solution(mesh):
    placed = (P("freq", None, "src", "rcv"), P("freq", None, "src", "rcv"), P())
    return jax.shard_map(
        body, mesh=mesh, in_specs=placed, out_specs=P("freq", None, "src", "rcv"), check_vma=False
    )
```

```python
import functools

import jax
import jax.numpy as jnp
from jax import lax
from jax.experimental import pallas as pl
from jax.experimental.pallas import tpu as pltpu
from jax.sharding import PartitionSpec as P

BLK = 256
APER = 12
HW = 6
PIECES = 1


def after(value, *earlier):
    return lax.optimization_barrier((value, *earlier))[0]


def from_behind(x, axis, by):
    peers = lax.axis_size(axis)
    pairs = [(i, i + by) for i in range(peers) if 0 <= i + by < peers]
    return lax.ppermute(x, axis, pairs)


def swap(x, axis, bit):
    peers = lax.axis_size(axis)
    return lax.ppermute(x, axis, [(i, i ^ bit) for i in range(peers)])


def at_end():
    return (lax.axis_index("src") + 1) % lax.axis_size("src") < 2


def line_window(data):
    near_pairs = [(0, 1), (1, 0), (2, 3), (3, 2)]
    far = lax.ppermute(data, "src", [(0, 3), (1, 2), (2, 1), (3, 0)])
    near = lax.ppermute(data, "src", near_pairs)
    windows = []
    for v in range(data.shape[0]):
        across = lax.ppermute(far[v : v + 1], "src", near_pairs)
        windows.append([(data, v), (near, v), (across, 0), (far, v)])
    return windows


def hop_window(data):
    reach = min(HW, lax.axis_size("src") - 1)
    window = {0: data}
    for hop in range(1, reach + 1):
        window[-hop] = from_behind(window[1 - hop], "src", 1)
        window[hop] = from_behind(window[hop - 1], "src", -1)
    return [[(window[distance], v) for distance in range(-reach, reach + 1)] for v in range(data.shape[0])]


def gather_panels(primaries):
    bit = lax.axis_size("rcv") // 2
    panels = [primaries]
    for lower in range(1, bit):
        panels.append(swap(panels[lower & (lower - 1)], "rcv", lower & -lower))
    return panels, swap(primaries, "rcv", bit)


def hand_on(panel, token):
    bit = lax.axis_size("rcv") // 2
    panels = [after(panel, token)]
    for lower in range(1, bit):
        panels.append(swap(panels[lower & (lower - 1)], "rcv", lower & -lower))
    return panels[1:]


def fill_window(window, pieces):
    width = window.shape[-1] // 2
    for k, piece in pieces.items():
        window[k, :, :width] = piece[0]
        window[k, :, width:] = piece[1]


def slot_entries(aperture_ref, m, per_shard, depth):
    src = lax.axis_index("src")
    shard = lax.bitwise_xor(lax.axis_index("rcv"), m)
    wanted = [aperture_ref[src, shard * per_shard + q] for q in range(per_shard)]
    if lax.axis_size("src") == 4:
        return [lax.bitwise_xor(src, block) for block in wanted]
    return [block - src + depth // 2 for block in wanted]


def times(values, blocks):
    both = jnp.dot(values, blocks, preferred_element_type=jnp.float32)
    rows, width = both.shape[0] // 2, both.shape[1] // 2
    return both[:rows, :width] - both[rows:, width:], both[:rows, width:] + both[rows:, :width]


def rows_of(panel):
    return panel[...].reshape(2 * panel.shape[1], panel.shape[2])


def product(window, aperture_ref, panels, late_in_two=None, late=None):
    blocks = []
    for m, panel in panels.items():
        entries = slot_entries(aperture_ref, m, panel.shape[-1] // BLK, window.shape[0])
        blocks += [window[k] for k in entries]
    values = [rows_of(panel) for panel in panels.values()]
    if late_in_two is not None:
        values.append(late_in_two)
        blocks += [window[late]] * 2
    return times(jnp.concatenate(values, axis=1), jnp.concatenate(blocks, axis=0))


def sum_of_late(aperture_ref, panels, late, depth):
    total = None
    for m, panel in panels.items():
        values = rows_of(panel)
        for q, k in enumerate(slot_entries(aperture_ref, m, panel.shape[-1] // BLK, depth)):
            term = values[:, q * BLK : (q + 1) * BLK].astype(jnp.float32) * jnp.where(k == late, 1.0, 0.0)
            total = term if total is None else total + term
    return total


def in_two(total):
    high = total.astype(jnp.bfloat16)
    low = (total - high.astype(jnp.float32)).astype(jnp.bfloat16)
    return jnp.concatenate([high, low], axis=1)


def kernel_a(near_half, ats, late, aperture_ref, *refs):
    panel_refs = refs[:near_half]
    piece_refs = list(refs[near_half:-6])
    windows, sums, parts = refs[-6:-4], refs[-4:-2], refs[-2:]
    for v, (window, at) in enumerate(zip(windows, ats)):
        window[late] = jnp.zeros(window.shape[1:], window.dtype)
        fill_window(window, {k: piece_refs.pop(0).at[index] for k, index in at.items()})
        panels = {m: ref.at[v] for m, ref in enumerate(panel_refs)}
        parts[v][0], parts[v][1] = product(window, aperture_ref, panels)
        sums[v][...] = sum_of_late(aperture_ref, panels, late, window.shape[0])


def kernel_b(m, late, aperture_ref, late_ref, _, last_window, first_sum, last_sum, first_in, last_in, panel_ref, *refs):
    window, two, first_part, last_part = refs
    fill_window(window, {late: late_ref.at[0]})
    real, imag = product(window, aperture_ref, {m: panel_ref.at[0]}, in_two(first_sum[...]), late)
    first_part[0] = first_in[0] + real
    first_part[1] = first_in[1] + imag
    panels = {m: panel_ref.at[1]}
    real, imag = product(last_window, aperture_ref, panels)
    last_part[0] = last_in[0] + real
    last_part[1] = last_in[1] + imag
    two[...] = in_two(last_sum[...] + sum_of_late(aperture_ref, panels, late, last_window.shape[0]))


def last_kernel(far_half, late, aperture_ref, late_ref, first_window, _, two, first_part, last_part, *refs):
    *panel_refs, out_ref, window, result, sems = refs

    def finish(v, part, real, imag):
        copies = []
        for p, value in enumerate((real, imag)):
            result[v, p] = part[p] + value
            for chunk in range(PIECES):
                rows = pl.ds(chunk * (BLK // PIECES), BLK // PIECES)
                copies.append(
                    pltpu.make_async_copy(result.at[v, p, rows], out_ref.at[v, p, rows], sems.at[v, p, chunk])
                )
                copies[-1].start()
        return copies

    panels = [{far_half + m: ref.at[v] for m, ref in enumerate(panel_refs)} for v in range(2)]
    copies = finish(0, first_part, *product(first_window, aperture_ref, panels[0]))
    fill_window(window, {late: late_ref.at[0]})
    copies += finish(1, last_part, *product(window, aperture_ref, panels[1], two[...], late))
    for copy in copies:
        copy.wait()


def spec(space):
    return pl.BlockSpec(memory_space=space)


def cost(share):
    return pl.CostEstimate(flops=int(share * (8 * BLK * BLK * APER * BLK)), bytes_accessed=1 << 20, transcendentals=0)


def limit(megabytes):
    return pltpu.CompilerParams(vmem_limit_bytes=megabytes << 20)


def held(piece, token):
    return pl.pallas_call(
        lambda piece_ref, token_ref, out_ref: None,
        out_shape=jax.ShapeDtypeStruct(piece.shape, piece.dtype),
        in_specs=[spec(pl.ANY)] * 2,
        out_specs=spec(pl.ANY),
        input_output_aliases={0: 0},
        compiler_params=limit(1),
        cost_estimate=cost(12),
    )(piece, token)


def body(primaries, data, aperture):
    width = data.shape[3]
    line = lax.axis_size("src") == 4
    windows = (line_window if line else hop_window)(data)
    panels, far_panel = gather_panels(primaries)
    half = len(panels)
    late = 2 if line else len(windows[0]) - 1
    late_pieces = [piece[at : at + 1] for piece, at in (window[late] for window in windows)]
    early = [{k: piece for k, piece in enumerate(window) if k != late} for window in windows]
    vmem, smem, anywhere = spec(pltpu.VMEM), spec(pltpu.SMEM), spec(pl.ANY)
    window = jax.ShapeDtypeStruct((len(windows[0]), BLK, 2 * width), jnp.bfloat16)
    total = jax.ShapeDtypeStruct((2 * BLK, BLK), jnp.float32)
    part = jax.ShapeDtypeStruct((2, BLK, width), jnp.float32)

    pieces = [piece for window_pieces in early for piece, _ in window_pieces.values()]
    first, last, first_sum, last_sum, first_part, last_part = pl.pallas_call(
        functools.partial(kernel_a, half, [{k: at for k, (_, at) in pieces.items()} for pieces in early], late),
        out_shape=[window] * 2 + [total] * 2 + [part] * 2,
        in_specs=[smem] + [vmem] * (half + len(pieces)),
        out_specs=[vmem] * 6,
        compiler_params=limit(16),
        cost_estimate=cost(0.1),
    )(aperture, *panels, *pieces)

    handed_on = hand_on(far_panel, first_part)
    first, two, first_part, last_part = pl.pallas_call(
        functools.partial(kernel_b, half, late),
        out_shape=[window, jax.ShapeDtypeStruct((2 * BLK, 2 * BLK), jnp.bfloat16), part, part],
        in_specs=[smem] + [vmem] * 8,
        out_specs=[vmem] * 4,
        input_output_aliases={2: 0, 6: 2, 7: 3},
        compiler_params=limit(16),
        cost_estimate=cost(0.1),
    )(aperture, late_pieces[0], first, last, first_sum, last_sum, first_part, last_part, far_panel)

    return pl.pallas_call(
        functools.partial(last_kernel, half + 1, late),
        out_shape=[jax.ShapeDtypeStruct((2, 2, BLK, width), jnp.float32), window],
        in_specs=[smem] + [vmem] * (6 + len(handed_on)),
        out_specs=[anywhere, vmem],
        scratch_shapes=[pltpu.VMEM((2, 2, BLK, width), jnp.float32), pltpu.SemaphoreType.DMA((2, 2, PIECES))],
        input_output_aliases={3: 1},
        compiler_params=limit(16),
        cost_estimate=cost(1),
    )(aperture, held(late_pieces[1], two), first, last, two, first_part, last_part, *handed_on)[0]


def solution(mesh):
    placed = (P("freq", None, "src", "rcv"), P("freq", None, "src", "rcv"), P())
    return jax.shard_map(
        body, mesh=mesh, in_specs=placed, out_specs=P("freq", None, "src", "rcv"), check_vma=False
    )
```

```python
import functools

import jax
import jax.numpy as jnp
from jax import lax
from jax.experimental import pallas as pl
from jax.experimental.pallas import tpu as pltpu
from jax.sharding import PartitionSpec as P

BLK = 256
APER = 12
HW = 6
PIECES = 1


def after(value, *earlier):
    return lax.optimization_barrier((value, *earlier))[0]


def from_behind(x, axis, by):
    peers = lax.axis_size(axis)
    pairs = [(i, i + by) for i in range(peers) if 0 <= i + by < peers]
    return lax.ppermute(x, axis, pairs)


def swap(x, axis, bit):
    peers = lax.axis_size(axis)
    return lax.ppermute(x, axis, [(i, i ^ bit) for i in range(peers)])


def at_end():
    return (lax.axis_index("src") + 1) % lax.axis_size("src") < 2


def line_window(data):
    near_pairs = [(0, 1), (1, 0), (2, 3), (3, 2)]
    near = lax.ppermute(data, "src", near_pairs)
    windows = []
    for own in lax.optimization_barrier([data[v : v + 1] for v in range(data.shape[0])]):
        far = lax.ppermute(own, "src", [(0, 3), (1, 2), (2, 1), (3, 0)])
        across = lax.ppermute(far, "src", near_pairs)
        windows.append([(own, 0), (near, len(windows)), (across, 0), (far, 0)])
    return windows


def hop_window(data):
    reach = min(HW, lax.axis_size("src") - 1)
    window = {0: data}
    for hop in range(1, reach + 1):
        window[-hop] = from_behind(window[1 - hop], "src", 1)
        window[hop] = from_behind(window[hop - 1], "src", -1)
    return [[(window[distance], v) for distance in range(-reach, reach + 1)] for v in range(data.shape[0])]


def gather_panels(primaries):
    bit = lax.axis_size("rcv") // 2
    panels = [primaries]
    for lower in range(1, bit):
        panels.append(swap(panels[lower & (lower - 1)], "rcv", lower & -lower))
    return panels, swap(primaries, "rcv", bit)


def hand_on(panel, token):
    bit = lax.axis_size("rcv") // 2
    panels = [after(panel, token)]
    for lower in range(1, bit):
        panels.append(swap(panels[lower & (lower - 1)], "rcv", lower & -lower))
    return panels[1:]


def fill_window(window, pieces):
    width = window.shape[-1] // 2
    for k, piece in pieces.items():
        window[k, :, :width] = piece[0]
        window[k, :, width:] = piece[1]


def slot_entries(aperture_ref, m, per_shard, depth):
    src = lax.axis_index("src")
    shard = lax.bitwise_xor(lax.axis_index("rcv"), m)
    wanted = [aperture_ref[src, shard * per_shard + q] for q in range(per_shard)]
    if lax.axis_size("src") == 4:
        return [lax.bitwise_xor(src, block) for block in wanted]
    return [block - src + depth // 2 for block in wanted]


def times(values, blocks):
    both = jnp.dot(values, blocks, preferred_element_type=jnp.float32)
    rows, width = both.shape[0] // 2, both.shape[1] // 2
    return both[:rows, :width] - both[rows:, width:], both[:rows, width:] + both[rows:, :width]


def rows_of(panel):
    return panel[...].reshape(2 * panel.shape[1], panel.shape[2])


def product(window, aperture_ref, panels, late_in_two=None, late=None):
    blocks = []
    for m, panel in panels.items():
        entries = slot_entries(aperture_ref, m, panel.shape[-1] // BLK, window.shape[0])
        blocks += [window[k] for k in entries]
    values = [rows_of(panel) for panel in panels.values()]
    if late_in_two is not None:
        values.append(late_in_two)
        blocks += [window[late]] * 2
    return times(jnp.concatenate(values, axis=1), jnp.concatenate(blocks, axis=0))


def sum_of_late(aperture_ref, panels, late, depth):
    total = None
    for m, panel in panels.items():
        values = rows_of(panel)
        for q, k in enumerate(slot_entries(aperture_ref, m, panel.shape[-1] // BLK, depth)):
            term = values[:, q * BLK : (q + 1) * BLK].astype(jnp.float32) * jnp.where(k == late, 1.0, 0.0)
            total = term if total is None else total + term
    return total


def in_two(total):
    high = total.astype(jnp.bfloat16)
    low = (total - high.astype(jnp.float32)).astype(jnp.bfloat16)
    return jnp.concatenate([high, low], axis=1)


def kernel_a(near_half, ats, late, aperture_ref, *refs):
    panel_refs = refs[:near_half]
    piece_refs = list(refs[near_half:-6])
    windows, sums, parts = refs[-6:-4], refs[-4:-2], refs[-2:]
    for v, (window, at) in enumerate(zip(windows, ats)):
        window[late] = jnp.zeros(window.shape[1:], window.dtype)
        fill_window(window, {k: piece_refs.pop(0).at[index] for k, index in at.items()})
        panels = {m: ref.at[v] for m, ref in enumerate(panel_refs)}
        parts[v][0], parts[v][1] = product(window, aperture_ref, panels)
        sums[v][...] = sum_of_late(aperture_ref, panels, late, window.shape[0])


def kernel_b(m, late, aperture_ref, late_ref, _, last_window, first_sum, last_sum, first_in, last_in, panel_ref, *refs):
    window, two, first_part, last_part = refs
    fill_window(window, {late: late_ref.at[0]})
    real, imag = product(window, aperture_ref, {m: panel_ref.at[0]}, in_two(first_sum[...]), late)
    first_part[0] = first_in[0] + real
    first_part[1] = first_in[1] + imag
    panels = {m: panel_ref.at[1]}
    real, imag = product(last_window, aperture_ref, panels)
    last_part[0] = last_in[0] + real
    last_part[1] = last_in[1] + imag
    two[...] = in_two(last_sum[...] + sum_of_late(aperture_ref, panels, late, last_window.shape[0]))


def last_kernel(far_half, late, aperture_ref, late_ref, first_window, _, two, first_part, last_part, *refs):
    *panel_refs, out_ref, window, result, sems = refs

    def finish(v, part, real, imag):
        copies = []
        for p, value in enumerate((real, imag)):
            result[v, p] = part[p] + value
            for chunk in range(PIECES):
                rows = pl.ds(chunk * (BLK // PIECES), BLK // PIECES)
                copies.append(
                    pltpu.make_async_copy(result.at[v, p, rows], out_ref.at[v, p, rows], sems.at[v, p, chunk])
                )
                copies[-1].start()
        return copies

    each = len(panel_refs) // 2
    panels = [{far_half + m: panel_refs[v * each + m].at[0] for m in range(each)} for v in range(2)]
    copies = finish(0, first_part, *product(first_window, aperture_ref, panels[0]))
    fill_window(window, {late: late_ref.at[0]})
    copies += finish(1, last_part, *product(window, aperture_ref, panels[1], two[...], late))
    for copy in copies:
        copy.wait()


def spec(space):
    return pl.BlockSpec(memory_space=space)


def cost(share):
    return pl.CostEstimate(flops=int(share * (8 * BLK * BLK * APER * BLK)), bytes_accessed=1 << 20, transcendentals=0)


def limit(megabytes):
    return pltpu.CompilerParams(vmem_limit_bytes=megabytes << 20)


def held(piece, token):
    return pl.pallas_call(
        lambda piece_ref, token_ref, out_ref: None,
        out_shape=jax.ShapeDtypeStruct(piece.shape, piece.dtype),
        in_specs=[spec(pl.ANY)] * 2,
        out_specs=spec(pl.ANY),
        input_output_aliases={0: 0},
        compiler_params=limit(1),
        cost_estimate=cost(12),
    )(piece, token)


def body(primaries, data, aperture):
    width = data.shape[3]
    line = lax.axis_size("src") == 4
    windows = (line_window if line else hop_window)(data)
    panels, far_panel = gather_panels(primaries)
    half = len(panels)
    late = 2 if line else len(windows[0]) - 1
    late_pieces = [piece[at : at + 1] for piece, at in (window[late] for window in windows)]
    early = [{k: piece for k, piece in enumerate(window) if k != late} for window in windows]
    vmem, smem, anywhere = spec(pltpu.VMEM), spec(pltpu.SMEM), spec(pl.ANY)
    window = jax.ShapeDtypeStruct((len(windows[0]), BLK, 2 * width), jnp.bfloat16)
    total = jax.ShapeDtypeStruct((2 * BLK, BLK), jnp.float32)
    part = jax.ShapeDtypeStruct((2, BLK, width), jnp.float32)

    pieces = [piece for window_pieces in early for piece, _ in window_pieces.values()]
    first, last, first_sum, last_sum, first_part, last_part = pl.pallas_call(
        functools.partial(kernel_a, half, [{k: at for k, (_, at) in pieces.items()} for pieces in early], late),
        out_shape=[window] * 2 + [total] * 2 + [part] * 2,
        in_specs=[smem] + [vmem] * (half + len(pieces)),
        out_specs=[vmem] * 6,
        compiler_params=limit(16),
        cost_estimate=cost(0.1),
    )(aperture, *panels, *pieces)

    handed_on = [hand_on(half_panel, first_part) for half_panel in (far_panel[:1], far_panel[1:])]
    first, two, first_part, last_part = pl.pallas_call(
        functools.partial(kernel_b, half, late),
        out_shape=[window, jax.ShapeDtypeStruct((2 * BLK, 2 * BLK), jnp.bfloat16), part, part],
        in_specs=[smem] + [vmem] * 8,
        out_specs=[vmem] * 4,
        input_output_aliases={2: 0, 6: 2, 7: 3},
        compiler_params=limit(16),
        cost_estimate=cost(0.1),
    )(aperture, late_pieces[0], first, last, first_sum, last_sum, first_part, last_part, far_panel)

    return pl.pallas_call(
        functools.partial(last_kernel, half + 1, late),
        out_shape=[jax.ShapeDtypeStruct((2, 2, BLK, width), jnp.float32), window],
        in_specs=[smem] + [vmem] * (6 + 2 * len(handed_on[0])),
        out_specs=[anywhere, vmem],
        scratch_shapes=[pltpu.VMEM((2, 2, BLK, width), jnp.float32), pltpu.SemaphoreType.DMA((2, 2, PIECES))],
        input_output_aliases={3: 1},
        compiler_params=limit(16),
        cost_estimate=cost(1),
    )(aperture, held(late_pieces[1], two), first, last, two, first_part, last_part, *handed_on[0], *handed_on[1])[0]


def solution(mesh):
    placed = (P("freq", None, "src", "rcv"), P("freq", None, "src", "rcv"), P())
    return jax.shard_map(
        body, mesh=mesh, in_specs=placed, out_specs=P("freq", None, "src", "rcv"), check_vma=False
    )
```

```python
import functools

import jax
import jax.numpy as jnp
from jax import lax
from jax.experimental import pallas as pl
from jax.experimental.pallas import tpu as pltpu
from jax.sharding import PartitionSpec as P

BLK = 256
APER = 12
HW = 6
PIECES = 1


def after(value, *earlier):
    return lax.optimization_barrier((value, *earlier))[0]


def from_behind(x, axis, by):
    peers = lax.axis_size(axis)
    pairs = [(i, i + by) for i in range(peers) if 0 <= i + by < peers]
    return lax.ppermute(x, axis, pairs)


def swap(x, axis, bit):
    peers = lax.axis_size(axis)
    return lax.ppermute(x, axis, [(i, i ^ bit) for i in range(peers)])


def at_end():
    return (lax.axis_index("src") + 1) % lax.axis_size("src") < 2


def line_window(data):
    near_pairs = [(0, 1), (1, 0), (2, 3), (3, 2)]
    far = lax.ppermute(data, "src", [(0, 3), (1, 2), (2, 1), (3, 0)])
    near = lax.ppermute(data, "src", near_pairs)
    windows = []
    for v in range(data.shape[0]):
        across = lax.ppermute(far[v : v + 1], "src", near_pairs)
        windows.append([(data, v), (near, v), (across, 0), (far, v)])
    return windows


def hop_window(data):
    reach = min(HW, lax.axis_size("src") - 1)
    window = {0: data}
    for hop in range(1, reach + 1):
        window[-hop] = from_behind(window[1 - hop], "src", 1)
        window[hop] = from_behind(window[hop - 1], "src", -1)
    return [[(window[distance], v) for distance in range(-reach, reach + 1)] for v in range(data.shape[0])]


def gather_panels(primaries):
    bit = lax.axis_size("rcv") // 2
    panels = [primaries]
    for lower in range(1, bit):
        panels.append(swap(panels[lower & (lower - 1)], "rcv", lower & -lower))
    return panels, swap(primaries, "rcv", bit)


def hand_on(panel, token):
    bit = lax.axis_size("rcv") // 2
    panels = [after(panel, token)]
    for lower in range(1, bit):
        panels.append(swap(panels[lower & (lower - 1)], "rcv", lower & -lower))
    return panels[1:]


def fill_window(window, pieces):
    width = window.shape[-1] // 2
    for k, piece in pieces.items():
        window[k, :, :width] = piece[0]
        window[k, :, width:] = piece[1]


def slot_entries(aperture_ref, m, per_shard, depth):
    src = lax.axis_index("src")
    shard = lax.bitwise_xor(lax.axis_index("rcv"), m)
    wanted = [aperture_ref[src, shard * per_shard + q] for q in range(per_shard)]
    if lax.axis_size("src") == 4:
        return [lax.bitwise_xor(src, block) for block in wanted]
    return [block - src + depth // 2 for block in wanted]


def rows_of(panel):
    return panel[...].reshape(2 * panel.shape[1], panel.shape[2])


def product(window, aperture_ref, panels, late_in_two=None, late=None):
    terms = []
    for m, panel in panels.items():
        values = rows_of(panel)
        entries = slot_entries(aperture_ref, m, panel.shape[-1] // BLK, window.shape[0])
        terms += [(values[:, q * BLK : (q + 1) * BLK], window[k]) for q, k in enumerate(entries)]
    if late_in_two is not None:
        terms += [(late_in_two[:, q * BLK : (q + 1) * BLK], window[late]) for q in range(2)]
    both = None
    for values, block in terms:
        term = jnp.dot(values, block, preferred_element_type=jnp.float32)
        both = term if both is None else both + term
    rows, width = both.shape[0] // 2, both.shape[1] // 2
    return both[:rows, :width] - both[rows:, width:], both[:rows, width:] + both[rows:, :width]


def sum_of_late(aperture_ref, panels, late, depth):
    total = None
    for m, panel in panels.items():
        values = rows_of(panel)
        for q, k in enumerate(slot_entries(aperture_ref, m, panel.shape[-1] // BLK, depth)):
            term = values[:, q * BLK : (q + 1) * BLK].astype(jnp.float32) * jnp.where(k == late, 1.0, 0.0)
            total = term if total is None else total + term
    return total


def in_two(total):
    high = total.astype(jnp.bfloat16)
    low = (total - high.astype(jnp.float32)).astype(jnp.bfloat16)
    return jnp.concatenate([high, low], axis=1)


def kernel_a(near_half, ats, late, aperture_ref, *refs):
    panel_refs = refs[:near_half]
    piece_refs = list(refs[near_half:-6])
    windows, sums, parts = refs[-6:-4], refs[-4:-2], refs[-2:]
    for v, (window, at) in enumerate(zip(windows, ats)):
        window[late] = jnp.zeros(window.shape[1:], window.dtype)
        fill_window(window, {k: piece_refs.pop(0).at[index] for k, index in at.items()})
        panels = {m: ref.at[v] for m, ref in enumerate(panel_refs)}
        parts[v][0], parts[v][1] = product(window, aperture_ref, panels)
        sums[v][...] = sum_of_late(aperture_ref, panels, late, window.shape[0])


def kernel_b(m, late, aperture_ref, late_ref, _, last_window, first_sum, last_sum, first_in, last_in, panel_ref, *refs):
    window, two, first_part, last_part = refs
    fill_window(window, {late: late_ref.at[0]})
    real, imag = product(window, aperture_ref, {m: panel_ref.at[0]}, in_two(first_sum[...]), late)
    first_part[0] = first_in[0] + real
    first_part[1] = first_in[1] + imag
    panels = {m: panel_ref.at[1]}
    real, imag = product(last_window, aperture_ref, panels)
    last_part[0] = last_in[0] + real
    last_part[1] = last_in[1] + imag
    two[...] = in_two(last_sum[...] + sum_of_late(aperture_ref, panels, late, last_window.shape[0]))


def last_kernel(far_half, late, aperture_ref, late_ref, first_window, _, two, first_part, last_part, *refs):
    *panel_refs, out_ref, window, result, sems = refs

    def finish(v, part, real, imag):
        copies = []
        for p, value in enumerate((real, imag)):
            result[v, p] = part[p] + value
            for chunk in range(PIECES):
                rows = pl.ds(chunk * (BLK // PIECES), BLK // PIECES)
                copies.append(
                    pltpu.make_async_copy(result.at[v, p, rows], out_ref.at[v, p, rows], sems.at[v, p, chunk])
                )
                copies[-1].start()
        return copies

    panels = [{far_half + m: ref.at[v] for m, ref in enumerate(panel_refs)} for v in range(2)]
    copies = finish(0, first_part, *product(first_window, aperture_ref, panels[0]))
    fill_window(window, {late: late_ref.at[0]})
    copies += finish(1, last_part, *product(window, aperture_ref, panels[1], two[...], late))
    for copy in copies:
        copy.wait()


def spec(space):
    return pl.BlockSpec(memory_space=space)


def cost(share):
    return pl.CostEstimate(flops=int(share * (8 * BLK * BLK * APER * BLK)), bytes_accessed=1 << 20, transcendentals=0)


def limit(megabytes):
    return pltpu.CompilerParams(vmem_limit_bytes=megabytes << 20)


def held(piece, token):
    return pl.pallas_call(
        lambda piece_ref, token_ref, out_ref: None,
        out_shape=jax.ShapeDtypeStruct(piece.shape, piece.dtype),
        in_specs=[spec(pl.ANY)] * 2,
        out_specs=spec(pl.ANY),
        input_output_aliases={0: 0},
        compiler_params=limit(1),
        cost_estimate=cost(12),
    )(piece, token)


def body(primaries, data, aperture):
    width = data.shape[3]
    line = lax.axis_size("src") == 4
    windows = (line_window if line else hop_window)(data)
    panels, far_panel = gather_panels(primaries)
    half = len(panels)
    late = 2 if line else len(windows[0]) - 1
    late_pieces = [piece[at : at + 1] for piece, at in (window[late] for window in windows)]
    early = [{k: piece for k, piece in enumerate(window) if k != late} for window in windows]
    vmem, smem, anywhere = spec(pltpu.VMEM), spec(pltpu.SMEM), spec(pl.ANY)
    window = jax.ShapeDtypeStruct((len(windows[0]), BLK, 2 * width), jnp.bfloat16)
    total = jax.ShapeDtypeStruct((2 * BLK, BLK), jnp.float32)
    part = jax.ShapeDtypeStruct((2, BLK, width), jnp.float32)

    pieces = [piece for window_pieces in early for piece, _ in window_pieces.values()]
    first, last, first_sum, last_sum, first_part, last_part = pl.pallas_call(
        functools.partial(kernel_a, half, [{k: at for k, (_, at) in pieces.items()} for pieces in early], late),
        out_shape=[window] * 2 + [total] * 2 + [part] * 2,
        in_specs=[smem] + [vmem] * (half + len(pieces)),
        out_specs=[vmem] * 6,
        compiler_params=limit(16),
        cost_estimate=cost(0.1),
    )(aperture, *panels, *pieces)

    handed_on = hand_on(far_panel, first_part)
    first, two, first_part, last_part = pl.pallas_call(
        functools.partial(kernel_b, half, late),
        out_shape=[window, jax.ShapeDtypeStruct((2 * BLK, 2 * BLK), jnp.bfloat16), part, part],
        in_specs=[smem] + [vmem] * 8,
        out_specs=[vmem] * 4,
        input_output_aliases={2: 0, 6: 2, 7: 3},
        compiler_params=limit(16),
        cost_estimate=cost(0.1),
    )(aperture, late_pieces[0], first, last, first_sum, last_sum, first_part, last_part, far_panel)

    return pl.pallas_call(
        functools.partial(last_kernel, half + 1, late),
        out_shape=[jax.ShapeDtypeStruct((2, 2, BLK, width), jnp.float32), window],
        in_specs=[smem] + [vmem] * (6 + len(handed_on)),
        out_specs=[anywhere, vmem],
        scratch_shapes=[pltpu.VMEM((2, 2, BLK, width), jnp.float32), pltpu.SemaphoreType.DMA((2, 2, PIECES))],
        input_output_aliases={3: 1},
        compiler_params=limit(16),
        cost_estimate=cost(1),
    )(aperture, held(late_pieces[1], two), first, last, two, first_part, last_part, *handed_on)[0]


def solution(mesh):
    placed = (P("freq", None, "src", "rcv"), P("freq", None, "src", "rcv"), P())
    return jax.shard_map(
        body, mesh=mesh, in_specs=placed, out_specs=P("freq", None, "src", "rcv"), check_vma=False
    )
```

```python
import functools

import jax
import jax.numpy as jnp
from jax import lax
from jax.experimental import pallas as pl
from jax.experimental.pallas import tpu as pltpu
from jax.sharding import PartitionSpec as P

BLK = 256
APER = 12
HW = 6
PIECES = 1


def after(value, *earlier):
    return lax.optimization_barrier((value, *earlier))[0]


def from_behind(x, axis, by):
    peers = lax.axis_size(axis)
    pairs = [(i, i + by) for i in range(peers) if 0 <= i + by < peers]
    return lax.ppermute(x, axis, pairs)


def swap(x, axis, bit):
    peers = lax.axis_size(axis)
    return lax.ppermute(x, axis, [(i, i ^ bit) for i in range(peers)])


def at_end():
    return (lax.axis_index("src") + 1) % lax.axis_size("src") < 2


def line_window(data):
    near_pairs = [(0, 1), (1, 0), (2, 3), (3, 2)]
    far = lax.ppermute(data, "src", [(0, 3), (1, 2), (2, 1), (3, 0)])
    near = lax.ppermute(data, "src", near_pairs)
    windows = []
    for v in range(data.shape[0]):
        across = lax.ppermute(far[v : v + 1], "src", near_pairs)
        windows.append([(data, v), (near, v), (across, 0), (far, v)])
    return windows


def hop_window(data):
    reach = min(HW, lax.axis_size("src") - 1)
    window = {0: data}
    for hop in range(1, reach + 1):
        window[-hop] = from_behind(window[1 - hop], "src", 1)
        window[hop] = from_behind(window[hop - 1], "src", -1)
    return [[(window[distance], v) for distance in range(-reach, reach + 1)] for v in range(data.shape[0])]


def gather_panels(primaries):
    bit = lax.axis_size("rcv") // 2
    panels = [primaries]
    for lower in range(1, bit):
        panels.append(swap(panels[lower & (lower - 1)], "rcv", lower & -lower))
    return panels, swap(primaries, "rcv", bit)


def hand_on(panel, token):
    bit = lax.axis_size("rcv") // 2
    panels = [after(panel, token)]
    for lower in range(1, bit):
        panels.append(swap(panels[lower & (lower - 1)], "rcv", lower & -lower))
    return panels[1:]


def fill_window(window, pieces):
    width = window.shape[-1] // 2
    for k, piece in pieces.items():
        window[k, :, :width] = piece[0]
        window[k, :, width:] = piece[1]


def slot_entries(aperture_ref, m, per_shard, depth):
    src = lax.axis_index("src")
    first_slot = lax.bitwise_xor(lax.axis_index("rcv"), m) * per_shard
    blocks = aperture_ref[...]
    at_row = lax.broadcasted_iota(jnp.int32, blocks.shape, 0) == src
    at_slot = lax.broadcasted_iota(jnp.int32, blocks.shape, 1)
    wanted = [jnp.sum(jnp.where(at_row & (at_slot == first_slot + q), blocks, 0)) for q in range(per_shard)]
    if lax.axis_size("src") == 4:
        return [lax.bitwise_xor(src, block) for block in wanted]
    return [block - src + depth // 2 for block in wanted]


def times(values, blocks):
    both = jnp.dot(values, blocks, preferred_element_type=jnp.float32)
    rows, width = both.shape[0] // 2, both.shape[1] // 2
    return both[:rows, :width] - both[rows:, width:], both[:rows, width:] + both[rows:, :width]


def rows_of(panel):
    return panel[...].reshape(2 * panel.shape[1], panel.shape[2])


def product(window, aperture_ref, panels, late_in_two=None, late=None):
    blocks = []
    for m, panel in panels.items():
        entries = slot_entries(aperture_ref, m, panel.shape[-1] // BLK, window.shape[0])
        blocks += [window[k] for k in entries]
    values = [rows_of(panel) for panel in panels.values()]
    if late_in_two is not None:
        values.append(late_in_two)
        blocks += [window[late]] * 2
    return times(jnp.concatenate(values, axis=1), jnp.concatenate(blocks, axis=0))


def sum_of_late(aperture_ref, panels, late, depth):
    total = None
    for m, panel in panels.items():
        values = rows_of(panel)
        for q, k in enumerate(slot_entries(aperture_ref, m, panel.shape[-1] // BLK, depth)):
            term = values[:, q * BLK : (q + 1) * BLK].astype(jnp.float32) * jnp.where(k == late, 1.0, 0.0)
            total = term if total is None else total + term
    return total


def in_two(total):
    high = total.astype(jnp.bfloat16)
    low = (total - high.astype(jnp.float32)).astype(jnp.bfloat16)
    return jnp.concatenate([high, low], axis=1)


def kernel_a(near_half, ats, late, aperture_ref, *refs):
    panel_refs = refs[:near_half]
    piece_refs = list(refs[near_half:-6])
    windows, sums, parts = refs[-6:-4], refs[-4:-2], refs[-2:]
    for v, (window, at) in enumerate(zip(windows, ats)):
        window[late] = jnp.zeros(window.shape[1:], window.dtype)
        fill_window(window, {k: piece_refs.pop(0).at[index] for k, index in at.items()})
        panels = {m: ref.at[v] for m, ref in enumerate(panel_refs)}
        parts[v][0], parts[v][1] = product(window, aperture_ref, panels)
        sums[v][...] = sum_of_late(aperture_ref, panels, late, window.shape[0])


def kernel_b(m, late, aperture_ref, late_ref, _, last_window, first_sum, last_sum, first_in, last_in, panel_ref, *refs):
    window, two, first_part, last_part = refs
    fill_window(window, {late: late_ref.at[0]})
    real, imag = product(window, aperture_ref, {m: panel_ref.at[0]}, in_two(first_sum[...]), late)
    first_part[0] = first_in[0] + real
    first_part[1] = first_in[1] + imag
    panels = {m: panel_ref.at[1]}
    real, imag = product(last_window, aperture_ref, panels)
    last_part[0] = last_in[0] + real
    last_part[1] = last_in[1] + imag
    two[...] = in_two(last_sum[...] + sum_of_late(aperture_ref, panels, late, last_window.shape[0]))


def last_kernel(far_half, late, aperture_ref, late_ref, first_window, _, two, first_part, last_part, *refs):
    *panel_refs, out_ref, window, result, sems = refs

    def finish(v, part, real, imag):
        copies = []
        for p, value in enumerate((real, imag)):
            result[v, p] = part[p] + value
            for chunk in range(PIECES):
                rows = pl.ds(chunk * (BLK // PIECES), BLK // PIECES)
                copies.append(
                    pltpu.make_async_copy(result.at[v, p, rows], out_ref.at[v, p, rows], sems.at[v, p, chunk])
                )
                copies[-1].start()
        return copies

    panels = [{far_half + m: ref.at[v] for m, ref in enumerate(panel_refs)} for v in range(2)]
    copies = finish(0, first_part, *product(first_window, aperture_ref, panels[0]))
    fill_window(window, {late: late_ref.at[0]})
    copies += finish(1, last_part, *product(window, aperture_ref, panels[1], two[...], late))
    for copy in copies:
        copy.wait()


def spec(space):
    return pl.BlockSpec(memory_space=space)


def cost(share):
    return pl.CostEstimate(flops=int(share * (8 * BLK * BLK * APER * BLK)), bytes_accessed=1 << 20, transcendentals=0)


def limit(megabytes):
    return pltpu.CompilerParams(vmem_limit_bytes=megabytes << 20)


def held(piece, token):
    return pl.pallas_call(
        lambda piece_ref, token_ref, out_ref: None,
        out_shape=jax.ShapeDtypeStruct(piece.shape, piece.dtype),
        in_specs=[spec(pl.ANY)] * 2,
        out_specs=spec(pl.ANY),
        input_output_aliases={0: 0},
        compiler_params=limit(1),
        cost_estimate=cost(12),
    )(piece, token)


def body(primaries, data, aperture):
    width = data.shape[3]
    line = lax.axis_size("src") == 4
    windows = (line_window if line else hop_window)(data)
    panels, far_panel = gather_panels(primaries)
    half = len(panels)
    late = 2 if line else len(windows[0]) - 1
    late_pieces = [piece[at : at + 1] for piece, at in (window[late] for window in windows)]
    early = [{k: piece for k, piece in enumerate(window) if k != late} for window in windows]
    vmem, anywhere = spec(pltpu.VMEM), spec(pl.ANY)
    window = jax.ShapeDtypeStruct((len(windows[0]), BLK, 2 * width), jnp.bfloat16)
    total = jax.ShapeDtypeStruct((2 * BLK, BLK), jnp.float32)
    part = jax.ShapeDtypeStruct((2, BLK, width), jnp.float32)

    pieces = [piece for window_pieces in early for piece, _ in window_pieces.values()]
    first, last, first_sum, last_sum, first_part, last_part = pl.pallas_call(
        functools.partial(kernel_a, half, [{k: at for k, (_, at) in pieces.items()} for pieces in early], late),
        out_shape=[window] * 2 + [total] * 2 + [part] * 2,
        in_specs=[vmem] + [vmem] * (half + len(pieces)),
        out_specs=[vmem] * 6,
        compiler_params=limit(16),
        cost_estimate=cost(0.1),
    )(aperture, *panels, *pieces)

    handed_on = hand_on(far_panel, first_part)
    first, two, first_part, last_part = pl.pallas_call(
        functools.partial(kernel_b, half, late),
        out_shape=[window, jax.ShapeDtypeStruct((2 * BLK, 2 * BLK), jnp.bfloat16), part, part],
        in_specs=[vmem] + [vmem] * 8,
        out_specs=[vmem] * 4,
        input_output_aliases={2: 0, 6: 2, 7: 3},
        compiler_params=limit(16),
        cost_estimate=cost(0.1),
    )(aperture, late_pieces[0], first, last, first_sum, last_sum, first_part, last_part, far_panel)

    return pl.pallas_call(
        functools.partial(last_kernel, half + 1, late),
        out_shape=[jax.ShapeDtypeStruct((2, 2, BLK, width), jnp.float32), window],
        in_specs=[vmem] + [vmem] * (6 + len(handed_on)),
        out_specs=[anywhere, vmem],
        scratch_shapes=[pltpu.VMEM((2, 2, BLK, width), jnp.float32), pltpu.SemaphoreType.DMA((2, 2, PIECES))],
        input_output_aliases={3: 1},
        compiler_params=limit(16),
        cost_estimate=cost(1),
    )(aperture, held(late_pieces[1], two), first, last, two, first_part, last_part, *handed_on)[0]


def solution(mesh):
    placed = (P("freq", None, "src", "rcv"), P("freq", None, "src", "rcv"), P())
    return jax.shard_map(
        body, mesh=mesh, in_specs=placed, out_specs=P("freq", None, "src", "rcv"), check_vma=False
    )
```

```python
import functools

import jax
import jax.numpy as jnp
from jax import lax
from jax.experimental import pallas as pl
from jax.experimental.pallas import tpu as pltpu
from jax.sharding import PartitionSpec as P

BLK = 256
APER = 12
HW = 6
PIECES = 1


def after(value, *earlier):
    return lax.optimization_barrier((value, *earlier))[0]


def from_behind(x, axis, by):
    peers = lax.axis_size(axis)
    pairs = [(i, i + by) for i in range(peers) if 0 <= i + by < peers]
    return lax.ppermute(x, axis, pairs)


def swap(x, axis, bit):
    peers = lax.axis_size(axis)
    return lax.ppermute(x, axis, [(i, i ^ bit) for i in range(peers)])


def at_end():
    return (lax.axis_index("src") + 1) % lax.axis_size("src") < 2


def line_window(data):
    near_pairs = [(0, 1), (1, 0), (2, 3), (3, 2)]
    near = lax.ppermute(data, "src", near_pairs)
    far = lax.ppermute(data, "src", [(0, 3), (1, 2), (2, 1), (3, 0)])
    near, far = lax.optimization_barrier((near, far))
    windows = []
    for v in range(data.shape[0]):
        across = lax.ppermute(far[v : v + 1], "src", near_pairs)
        windows.append([(data, v), (near, v), (across, 0), (far, v)])
    return windows


def hop_window(data):
    reach = min(HW, lax.axis_size("src") - 1)
    window = {0: data}
    for hop in range(1, reach + 1):
        window[-hop] = from_behind(window[1 - hop], "src", 1)
        window[hop] = from_behind(window[hop - 1], "src", -1)
    return [[(window[distance], v) for distance in range(-reach, reach + 1)] for v in range(data.shape[0])]


def gather_panels(primaries):
    bit = lax.axis_size("rcv") // 2
    panels = [primaries]
    for lower in range(1, bit):
        panels.append(swap(panels[lower & (lower - 1)], "rcv", lower & -lower))
    return panels, swap(primaries, "rcv", bit)


def hand_on(panel, token):
    bit = lax.axis_size("rcv") // 2
    panels = [after(panel, token)]
    for lower in range(1, bit):
        panels.append(swap(panels[lower & (lower - 1)], "rcv", lower & -lower))
    return panels[1:]


def fill_window(window, pieces):
    width = window.shape[-1] // 2
    for k, piece in pieces.items():
        window[k, :, :width] = piece[0]
        window[k, :, width:] = piece[1]


def slot_entries(aperture_ref, m, per_shard, depth):
    src = lax.axis_index("src")
    first_slot = lax.bitwise_xor(lax.axis_index("rcv"), m) * per_shard
    blocks = aperture_ref[...]
    at_row = lax.broadcasted_iota(jnp.int32, blocks.shape, 0) == src
    at_slot = lax.broadcasted_iota(jnp.int32, blocks.shape, 1)
    wanted = [jnp.sum(jnp.where(at_row & (at_slot == first_slot + q), blocks, 0)) for q in range(per_shard)]
    if lax.axis_size("src") == 4:
        return [lax.bitwise_xor(src, block) for block in wanted]
    return [block - src + depth // 2 for block in wanted]


def times(values, blocks):
    both = jnp.dot(values, blocks, preferred_element_type=jnp.float32)
    rows, width = both.shape[0] // 2, both.shape[1] // 2
    return both[:rows, :width] - both[rows:, width:], both[:rows, width:] + both[rows:, :width]


def rows_of(panel):
    return panel[...].reshape(2 * panel.shape[1], panel.shape[2])


def product(window, aperture_ref, panels, late_in_two=None, late=None):
    blocks = []
    for m, panel in panels.items():
        entries = slot_entries(aperture_ref, m, panel.shape[-1] // BLK, window.shape[0])
        blocks += [window[k] for k in entries]
    values = [rows_of(panel) for panel in panels.values()]
    if late_in_two is not None:
        values.append(late_in_two)
        blocks += [window[late]] * 2
    return times(jnp.concatenate(values, axis=1), jnp.concatenate(blocks, axis=0))


def sum_of_late(aperture_ref, panels, late, depth):
    total = None
    for m, panel in panels.items():
        values = rows_of(panel)
        for q, k in enumerate(slot_entries(aperture_ref, m, panel.shape[-1] // BLK, depth)):
            term = values[:, q * BLK : (q + 1) * BLK].astype(jnp.float32) * jnp.where(k == late, 1.0, 0.0)
            total = term if total is None else total + term
    return total


def in_two(total):
    high = total.astype(jnp.bfloat16)
    low = (total - high.astype(jnp.float32)).astype(jnp.bfloat16)
    return jnp.concatenate([high, low], axis=1)


def kernel_a(near_half, ats, late, aperture_ref, *refs):
    panel_refs = refs[:near_half]
    piece_refs = list(refs[near_half:-6])
    windows, sums, parts = refs[-6:-4], refs[-4:-2], refs[-2:]
    for v, (window, at) in enumerate(zip(windows, ats)):
        window[late] = jnp.zeros(window.shape[1:], window.dtype)
        fill_window(window, {k: piece_refs.pop(0).at[index] for k, index in at.items()})
        panels = {m: ref.at[v] for m, ref in enumerate(panel_refs)}
        parts[v][0], parts[v][1] = product(window, aperture_ref, panels)
        sums[v][...] = sum_of_late(aperture_ref, panels, late, window.shape[0])


def kernel_b(m, late, aperture_ref, late_ref, _, last_window, first_sum, last_sum, first_in, last_in, panel_ref, *refs):
    window, two, first_part, last_part = refs
    fill_window(window, {late: late_ref.at[0]})
    real, imag = product(window, aperture_ref, {m: panel_ref.at[0]}, in_two(first_sum[...]), late)
    first_part[0] = first_in[0] + real
    first_part[1] = first_in[1] + imag
    panels = {m: panel_ref.at[1]}
    real, imag = product(last_window, aperture_ref, panels)
    last_part[0] = last_in[0] + real
    last_part[1] = last_in[1] + imag
    two[...] = in_two(last_sum[...] + sum_of_late(aperture_ref, panels, late, last_window.shape[0]))


def last_kernel(far_half, late, aperture_ref, late_ref, first_window, _, two, first_part, last_part, *refs):
    *panel_refs, out_ref, window, result, sems = refs

    def finish(v, part, real, imag):
        copies = []
        for p, value in enumerate((real, imag)):
            result[v, p] = part[p] + value
            for chunk in range(PIECES):
                rows = pl.ds(chunk * (BLK // PIECES), BLK // PIECES)
                copies.append(
                    pltpu.make_async_copy(result.at[v, p, rows], out_ref.at[v, p, rows], sems.at[v, p, chunk])
                )
                copies[-1].start()
        return copies

    panels = [{far_half + m: ref.at[v] for m, ref in enumerate(panel_refs)} for v in range(2)]
    copies = finish(0, first_part, *product(first_window, aperture_ref, panels[0]))
    fill_window(window, {late: late_ref.at[0]})
    copies += finish(1, last_part, *product(window, aperture_ref, panels[1], two[...], late))
    for copy in copies:
        copy.wait()


def spec(space):
    return pl.BlockSpec(memory_space=space)


def cost(share):
    return pl.CostEstimate(flops=int(share * (8 * BLK * BLK * APER * BLK)), bytes_accessed=1 << 20, transcendentals=0)


def limit(megabytes):
    return pltpu.CompilerParams(vmem_limit_bytes=megabytes << 20)


def held(piece, token):
    return pl.pallas_call(
        lambda piece_ref, token_ref, out_ref: None,
        out_shape=jax.ShapeDtypeStruct(piece.shape, piece.dtype),
        in_specs=[spec(pl.ANY)] * 2,
        out_specs=spec(pl.ANY),
        input_output_aliases={0: 0},
        compiler_params=limit(1),
        cost_estimate=cost(12),
    )(piece, token)


def body(primaries, data, aperture):
    width = data.shape[3]
    line = lax.axis_size("src") == 4
    windows = (line_window if line else hop_window)(data)
    panels, far_panel = gather_panels(primaries)
    half = len(panels)
    late = 2 if line else len(windows[0]) - 1
    late_pieces = [piece[at : at + 1] for piece, at in (window[late] for window in windows)]
    early = [{k: piece for k, piece in enumerate(window) if k != late} for window in windows]
    vmem, anywhere = spec(pltpu.VMEM), spec(pl.ANY)
    window = jax.ShapeDtypeStruct((len(windows[0]), BLK, 2 * width), jnp.bfloat16)
    total = jax.ShapeDtypeStruct((2 * BLK, BLK), jnp.float32)
    part = jax.ShapeDtypeStruct((2, BLK, width), jnp.float32)

    pieces = [piece for window_pieces in early for piece, _ in window_pieces.values()]
    first, last, first_sum, last_sum, first_part, last_part = pl.pallas_call(
        functools.partial(kernel_a, half, [{k: at for k, (_, at) in pieces.items()} for pieces in early], late),
        out_shape=[window] * 2 + [total] * 2 + [part] * 2,
        in_specs=[vmem] + [vmem] * (half + len(pieces)),
        out_specs=[vmem] * 6,
        compiler_params=limit(16),
        cost_estimate=cost(0.1),
    )(aperture, *panels, *pieces)

    handed_on = hand_on(far_panel, first_part)
    first, two, first_part, last_part = pl.pallas_call(
        functools.partial(kernel_b, half, late),
        out_shape=[window, jax.ShapeDtypeStruct((2 * BLK, 2 * BLK), jnp.bfloat16), part, part],
        in_specs=[vmem] + [vmem] * 8,
        out_specs=[vmem] * 4,
        input_output_aliases={2: 0, 6: 2, 7: 3},
        compiler_params=limit(16),
        cost_estimate=cost(0.1),
    )(aperture, late_pieces[0], first, last, first_sum, last_sum, first_part, last_part, far_panel)

    return pl.pallas_call(
        functools.partial(last_kernel, half + 1, late),
        out_shape=[jax.ShapeDtypeStruct((2, 2, BLK, width), jnp.float32), window],
        in_specs=[vmem] + [vmem] * (6 + len(handed_on)),
        out_specs=[anywhere, vmem],
        scratch_shapes=[pltpu.VMEM((2, 2, BLK, width), jnp.float32), pltpu.SemaphoreType.DMA((2, 2, PIECES))],
        input_output_aliases={3: 1},
        compiler_params=limit(16),
        cost_estimate=cost(1),
    )(aperture, held(late_pieces[1], two), first, last, two, first_part, last_part, *handed_on)[0]


def solution(mesh):
    placed = (P("freq", None, "src", "rcv"), P("freq", None, "src", "rcv"), P())
    return jax.shard_map(
        body, mesh=mesh, in_specs=placed, out_specs=P("freq", None, "src", "rcv"), check_vma=False
    )
```

```python
import functools

import jax
import jax.numpy as jnp
from jax import lax
from jax.experimental import pallas as pl
from jax.experimental.pallas import tpu as pltpu
from jax.sharding import PartitionSpec as P

BLK = 256
APER = 12
HW = 6


def after(value, *earlier):
    return lax.optimization_barrier((value, *earlier))[0]


def from_behind(x, axis, by):
    peers = lax.axis_size(axis)
    pairs = [(i, i + by) for i in range(peers) if 0 <= i + by < peers]
    return lax.ppermute(x, axis, pairs)


def swap(x, axis, bit):
    peers = lax.axis_size(axis)
    return lax.ppermute(x, axis, [(i, i ^ bit) for i in range(peers)])


def at_end():
    return (lax.axis_index("src") + 1) % lax.axis_size("src") < 2


def line_window(data):
    near_pairs = [(0, 1), (1, 0), (2, 3), (3, 2)]
    far = lax.ppermute(data, "src", [(0, 3), (1, 2), (2, 1), (3, 0)])
    near = lax.ppermute(data, "src", near_pairs)
    windows = []
    for v in range(data.shape[0]):
        across = lax.ppermute(far[v : v + 1], "src", near_pairs)
        windows.append([(data, v), (near, v), (across, 0), (far, v)])
    return windows


def hop_window(data):
    reach = min(HW, lax.axis_size("src") - 1)
    window = {0: data}
    for hop in range(1, reach + 1):
        window[-hop] = from_behind(window[1 - hop], "src", 1)
        window[hop] = from_behind(window[hop - 1], "src", -1)
    return [[(window[distance], v) for distance in range(-reach, reach + 1)] for v in range(data.shape[0])]


def gather_panels(primaries):
    bit = lax.axis_size("rcv") // 2
    panels = [primaries]
    for lower in range(1, bit):
        panels.append(swap(panels[lower & (lower - 1)], "rcv", lower & -lower))
    return panels, swap(primaries, "rcv", bit)


def hand_on(panel, token):
    bit = lax.axis_size("rcv") // 2
    panels = [after(panel, token)]
    for lower in range(1, bit):
        panels.append(swap(panels[lower & (lower - 1)], "rcv", lower & -lower))
    return panels[1:]


def fill_window(window, pieces):
    width = window.shape[-1] // 2
    for k, piece in pieces.items():
        window[k, :, :width] = piece[0]
        window[k, :, width:] = piece[1]


def slot_entries(aperture_ref, m, per_shard, depth):
    src = lax.axis_index("src")
    first_slot = lax.bitwise_xor(lax.axis_index("rcv"), m) * per_shard
    blocks = aperture_ref[...]
    at_row = lax.broadcasted_iota(jnp.int32, blocks.shape, 0) == src
    at_slot = lax.broadcasted_iota(jnp.int32, blocks.shape, 1)
    wanted = [jnp.sum(jnp.where(at_row & (at_slot == first_slot + q), blocks, 0)) for q in range(per_shard)]
    if lax.axis_size("src") == 4:
        return [lax.bitwise_xor(src, block) for block in wanted]
    return [block - src + depth // 2 for block in wanted]


def times(values, blocks):
    both = jnp.dot(values, blocks, preferred_element_type=jnp.float32)
    rows, width = both.shape[0] // 2, both.shape[1] // 2
    return both[:rows, :width] - both[rows:, width:], both[:rows, width:] + both[rows:, :width]


def rows_of(panel):
    return panel[...].reshape(2 * panel.shape[1], panel.shape[2])


def product(window, aperture_ref, panels, late_in_two=None, late=None, late_block=None):
    blocks = []
    for m, panel in panels.items():
        entries = slot_entries(aperture_ref, m, panel.shape[-1] // BLK, window.shape[0])
        picked = [window[k] for k in entries]
        if late_block is not None:
            picked = [jnp.where(k == late, late_block, block) for k, block in zip(entries, picked)]
        blocks += picked
    values = [rows_of(panel) for panel in panels.values()]
    if late_in_two is not None:
        values.append(late_in_two)
        blocks += [window[late] if late_block is None else late_block] * 2
    return times(jnp.concatenate(values, axis=1), jnp.concatenate(blocks, axis=0))


def sum_of_late(aperture_ref, panels, late, depth):
    total = None
    for m, panel in panels.items():
        values = rows_of(panel)
        for q, k in enumerate(slot_entries(aperture_ref, m, panel.shape[-1] // BLK, depth)):
            term = values[:, q * BLK : (q + 1) * BLK].astype(jnp.float32) * jnp.where(k == late, 1.0, 0.0)
            total = term if total is None else total + term
    return total


def in_two(total):
    high = total.astype(jnp.bfloat16)
    low = (total - high.astype(jnp.float32)).astype(jnp.bfloat16)
    return jnp.concatenate([high, low], axis=1)


def kernel_a(near_half, ats, late, aperture_ref, *refs):
    panel_refs = refs[:near_half]
    piece_refs = list(refs[near_half:-6])
    windows, sums, parts = refs[-6:-4], refs[-4:-2], refs[-2:]
    for v, (window, at) in enumerate(zip(windows, ats)):
        window[late] = jnp.zeros(window.shape[1:], window.dtype)
        fill_window(window, {k: piece_refs.pop(0).at[index] for k, index in at.items()})
        panels = {m: ref.at[v] for m, ref in enumerate(panel_refs)}
        parts[v][0], parts[v][1] = product(window, aperture_ref, panels)
        sums[v][...] = sum_of_late(aperture_ref, panels, late, window.shape[0])


def kernel_b(m, late, aperture_ref, late_ref, _, last_window, first_sum, last_sum, first_in, last_in, panel_ref, *refs):
    window, two, first_part, last_part = refs
    fill_window(window, {late: late_ref.at[0]})
    real, imag = product(window, aperture_ref, {m: panel_ref.at[0]}, in_two(first_sum[...]), late)
    first_part[0] = first_in[0] + real
    first_part[1] = first_in[1] + imag
    panels = {m: panel_ref.at[1]}
    real, imag = product(last_window, aperture_ref, panels)
    last_part[0] = last_in[0] + real
    last_part[1] = last_in[1] + imag
    two[...] = in_two(last_sum[...] + sum_of_late(aperture_ref, panels, late, last_window.shape[0]))


def last_kernel(far_half, late, aperture_ref, late_ref, first_window, window, two, first_part, last_part, *refs):
    *panel_refs, out_ref, result, sems = refs

    def finish(v, part, real, imag):
        copies = []
        for p, value in enumerate((real, imag)):
            result[v, p] = part[p] + value
            copies.append(pltpu.make_async_copy(result.at[v, p], out_ref.at[v, p], sems.at[v, p]))
            copies[-1].start()
        return copies

    panels = [{far_half + m: ref.at[v] for m, ref in enumerate(panel_refs)} for v in range(2)]
    copies = finish(0, first_part, *product(first_window, aperture_ref, panels[0]))
    late_block = jnp.concatenate([late_ref[0, 0], late_ref[0, 1]], axis=1)
    copies += finish(1, last_part, *product(window, aperture_ref, panels[1], two[...], late, late_block))
    for copy in copies:
        copy.wait()


def spec(space):
    return pl.BlockSpec(memory_space=space)


def cost(share):
    return pl.CostEstimate(flops=int(share * (8 * BLK * BLK * APER * BLK)), bytes_accessed=1 << 20, transcendentals=0)


def limit(megabytes):
    return pltpu.CompilerParams(vmem_limit_bytes=megabytes << 20)


def held(piece, token):
    return pl.pallas_call(
        lambda piece_ref, token_ref, out_ref: None,
        out_shape=jax.ShapeDtypeStruct(piece.shape, piece.dtype),
        in_specs=[spec(pl.ANY)] * 2,
        out_specs=spec(pl.ANY),
        input_output_aliases={0: 0},
        compiler_params=limit(1),
        cost_estimate=cost(12),
    )(piece, token)


def body(primaries, data, aperture):
    width = data.shape[3]
    line = lax.axis_size("src") == 4
    windows = (line_window if line else hop_window)(data)
    panels, far_panel = gather_panels(primaries)
    half = len(panels)
    late = 2 if line else len(windows[0]) - 1
    late_pieces = [piece[at : at + 1] for piece, at in (window[late] for window in windows)]
    early = [{k: piece for k, piece in enumerate(window) if k != late} for window in windows]
    vmem, anywhere = spec(pltpu.VMEM), spec(pl.ANY)
    window = jax.ShapeDtypeStruct((len(windows[0]), BLK, 2 * width), jnp.bfloat16)
    total = jax.ShapeDtypeStruct((2 * BLK, BLK), jnp.float32)
    part = jax.ShapeDtypeStruct((2, BLK, width), jnp.float32)

    pieces = [piece for window_pieces in early for piece, _ in window_pieces.values()]
    first, last, first_sum, last_sum, first_part, last_part = pl.pallas_call(
        functools.partial(kernel_a, half, [{k: at for k, (_, at) in pieces.items()} for pieces in early], late),
        out_shape=[window] * 2 + [total] * 2 + [part] * 2,
        in_specs=[vmem] + [vmem] * (half + len(pieces)),
        out_specs=[vmem] * 6,
        compiler_params=limit(16),
        cost_estimate=cost(0.1),
    )(aperture, *panels, *pieces)

    handed_on = hand_on(far_panel, first_part)
    first, two, first_part, last_part = pl.pallas_call(
        functools.partial(kernel_b, half, late),
        out_shape=[window, jax.ShapeDtypeStruct((2 * BLK, 2 * BLK), jnp.bfloat16), part, part],
        in_specs=[vmem] + [vmem] * 8,
        out_specs=[vmem] * 4,
        input_output_aliases={2: 0, 6: 2, 7: 3},
        compiler_params=limit(16),
        cost_estimate=cost(0.1),
    )(aperture, late_pieces[0], first, last, first_sum, last_sum, first_part, last_part, far_panel)

    return pl.pallas_call(
        functools.partial(last_kernel, half + 1, late),
        out_shape=jax.ShapeDtypeStruct((2, 2, BLK, width), jnp.float32),
        in_specs=[vmem] * (7 + len(handed_on)),
        out_specs=anywhere,
        scratch_shapes=[pltpu.VMEM((2, 2, BLK, width), jnp.float32), pltpu.SemaphoreType.DMA((2, 2))],
        compiler_params=limit(16),
        cost_estimate=cost(1),
    )(aperture, held(late_pieces[1], two), first, last, two, first_part, last_part, *handed_on)


def solution(mesh):
    placed = (P("freq", None, "src", "rcv"), P("freq", None, "src", "rcv"), P())
    return jax.shard_map(
        body, mesh=mesh, in_specs=placed, out_specs=P("freq", None, "src", "rcv"), check_vma=False
    )
```

```python
import functools

import jax
import jax.numpy as jnp
from jax import lax
from jax.experimental import pallas as pl
from jax.experimental.pallas import tpu as pltpu
from jax.sharding import PartitionSpec as P

BLK = 256
APER = 12
HW = 6
PIECES = 1


def after(value, *earlier):
    return lax.optimization_barrier((value, *earlier))[0]


def from_behind(x, axis, by):
    peers = lax.axis_size(axis)
    pairs = [(i, i + by) for i in range(peers) if 0 <= i + by < peers]
    return lax.ppermute(x, axis, pairs)


def swap(x, axis, bit):
    peers = lax.axis_size(axis)
    return lax.ppermute(x, axis, [(i, i ^ bit) for i in range(peers)])


def at_end():
    return (lax.axis_index("src") + 1) % lax.axis_size("src") < 2


def line_window(data):
    near_pairs = [(0, 1), (1, 0), (2, 3), (3, 2)]
    far = lax.ppermute(data, "src", [(0, 3), (1, 2), (2, 1), (3, 0)])
    near = lax.ppermute(data, "src", near_pairs)
    windows = []
    for v in range(data.shape[0]):
        across = lax.ppermute(far[v : v + 1], "src", near_pairs)
        windows.append([(data, v), (near, v), (across, 0), (far, v)])
    return windows


def hop_window(data):
    reach = min(HW, lax.axis_size("src") - 1)
    window = {0: data}
    for hop in range(1, reach + 1):
        window[-hop] = from_behind(window[1 - hop], "src", 1)
        window[hop] = from_behind(window[hop - 1], "src", -1)
    return [[(window[distance], v) for distance in range(-reach, reach + 1)] for v in range(data.shape[0])]


def gather_panels(primaries):
    bit = lax.axis_size("rcv") // 2
    panels = [primaries]
    for lower in range(1, bit):
        panels.append(swap(panels[lower & (lower - 1)], "rcv", lower & -lower))
    return panels, swap(primaries, "rcv", bit)


def hand_on(panel, token):
    bit = lax.axis_size("rcv") // 2
    panels = [after(panel, token)]
    for lower in range(1, bit):
        panels.append(swap(panels[lower & (lower - 1)], "rcv", lower & -lower))
    return panels[1:]


def fill_window(window, pieces):
    width = window.shape[-1] // 2
    for k, piece in pieces.items():
        window[k, :, :width] = piece[0]
        window[k, :, width:] = piece[1]


def slot_entries(aperture_ref, m, per_shard, depth):
    src = lax.axis_index("src")
    first_slot = lax.bitwise_xor(lax.axis_index("rcv"), m) * per_shard
    blocks = aperture_ref[...]
    at_row = lax.broadcasted_iota(jnp.int32, blocks.shape, 0) == src
    at_slot = lax.broadcasted_iota(jnp.int32, blocks.shape, 1)
    wanted = [jnp.sum(jnp.where(at_row & (at_slot == first_slot + q), blocks, 0)) for q in range(per_shard)]
    if lax.axis_size("src") == 4:
        return [lax.bitwise_xor(src, block) for block in wanted]
    return [block - src + depth // 2 for block in wanted]


def times(values, blocks):
    both = jnp.dot(values, blocks, preferred_element_type=jnp.float32)
    rows, width = both.shape[0] // 2, both.shape[1] // 2
    return both[:rows, :width] - both[rows:, width:], both[:rows, width:] + both[rows:, :width]


def rows_of(panel):
    return panel[...].reshape(2 * panel.shape[1], panel.shape[2])


def product(window, aperture_ref, panels, late_in_two=None, late=None):
    blocks = []
    for m, panel in panels.items():
        entries = slot_entries(aperture_ref, m, panel.shape[-1] // BLK, window.shape[0])
        blocks += [window[k] for k in entries]
    values = [rows_of(panel) for panel in panels.values()]
    if late_in_two is not None:
        values.append(late_in_two)
        blocks += [window[late]] * 2
    return times(jnp.concatenate(values, axis=1), jnp.concatenate(blocks, axis=0))


def sum_of_late(aperture_ref, panels, late, depth):
    total = None
    for m, panel in panels.items():
        values = rows_of(panel)
        for q, k in enumerate(slot_entries(aperture_ref, m, panel.shape[-1] // BLK, depth)):
            term = values[:, q * BLK : (q + 1) * BLK].astype(jnp.float32) * jnp.where(k == late, 1.0, 0.0)
            total = term if total is None else total + term
    return total


def in_two(total):
    high = total.astype(jnp.bfloat16)
    low = (total - high.astype(jnp.float32)).astype(jnp.bfloat16)
    return jnp.concatenate([high, low], axis=1)


def kernel_a(ats, late, aperture_ref, own_ref, *refs):
    piece_refs = list(refs[:-6])
    windows, sums, parts = refs[-6:-4], refs[-4:-2], refs[-2:]
    for v, (window, at) in enumerate(zip(windows, ats)):
        window[late] = jnp.zeros(window.shape[1:], window.dtype)
        fill_window(window, {k: piece_refs.pop(0).at[index] for k, index in at.items()})
        panels = {0: own_ref.at[v]}
        parts[v][0], parts[v][1] = product(window, aperture_ref, panels)
        sums[v][...] = sum_of_late(aperture_ref, panels, late, window.shape[0])


def kernel_b(late, aperture_ref, late_ref, _, last_window, first_sum, last_sum, first_in, last_in, *refs):
    *panel_refs, window, two, first_part, last_part = refs
    fill_window(window, {late: late_ref.at[0]})
    panels = [{1 + m: ref.at[v] for m, ref in enumerate(panel_refs)} for v in range(2)]
    real, imag = product(window, aperture_ref, panels[0], in_two(first_sum[...]), late)
    first_part[0] = first_in[0] + real
    first_part[1] = first_in[1] + imag
    real, imag = product(last_window, aperture_ref, panels[1])
    last_part[0] = last_in[0] + real
    last_part[1] = last_in[1] + imag
    two[...] = in_two(last_sum[...] + sum_of_late(aperture_ref, panels[1], late, last_window.shape[0]))


def last_kernel(far_half, late, aperture_ref, late_ref, first_window, _, two, first_part, last_part, *refs):
    *panel_refs, out_ref, window, result, sems = refs

    def finish(v, part, real, imag):
        copies = []
        for p, value in enumerate((real, imag)):
            result[v, p] = part[p] + value
            for chunk in range(PIECES):
                rows = pl.ds(chunk * (BLK // PIECES), BLK // PIECES)
                copies.append(
                    pltpu.make_async_copy(result.at[v, p, rows], out_ref.at[v, p, rows], sems.at[v, p, chunk])
                )
                copies[-1].start()
        return copies

    panels = [{far_half + m: ref.at[v] for m, ref in enumerate(panel_refs)} for v in range(2)]
    copies = finish(0, first_part, *product(first_window, aperture_ref, panels[0]))
    fill_window(window, {late: late_ref.at[0]})
    copies += finish(1, last_part, *product(window, aperture_ref, panels[1], two[...], late))
    for copy in copies:
        copy.wait()


def spec(space):
    return pl.BlockSpec(memory_space=space)


def cost(share):
    return pl.CostEstimate(flops=int(share * (8 * BLK * BLK * APER * BLK)), bytes_accessed=1 << 20, transcendentals=0)


def limit(megabytes):
    return pltpu.CompilerParams(vmem_limit_bytes=megabytes << 20)


def held(piece, token):
    return pl.pallas_call(
        lambda piece_ref, token_ref, out_ref: None,
        out_shape=jax.ShapeDtypeStruct(piece.shape, piece.dtype),
        in_specs=[spec(pl.ANY)] * 2,
        out_specs=spec(pl.ANY),
        input_output_aliases={0: 0},
        compiler_params=limit(1),
        cost_estimate=cost(12),
    )(piece, token)


def body(primaries, data, aperture):
    width = data.shape[3]
    line = lax.axis_size("src") == 4
    windows = (line_window if line else hop_window)(data)
    panels, far_panel = gather_panels(primaries)
    half = len(panels)
    late = 2 if line else len(windows[0]) - 1
    late_pieces = [piece[at : at + 1] for piece, at in (window[late] for window in windows)]
    early = [{k: piece for k, piece in enumerate(window) if k != late} for window in windows]
    vmem, anywhere = spec(pltpu.VMEM), spec(pl.ANY)
    window = jax.ShapeDtypeStruct((len(windows[0]), BLK, 2 * width), jnp.bfloat16)
    total = jax.ShapeDtypeStruct((2 * BLK, BLK), jnp.float32)
    part = jax.ShapeDtypeStruct((2, BLK, width), jnp.float32)

    pieces = [piece for window_pieces in early for piece, _ in window_pieces.values()]
    first, last, first_sum, last_sum, first_part, last_part = pl.pallas_call(
        functools.partial(kernel_a, [{k: at for k, (_, at) in pieces.items()} for pieces in early], late),
        out_shape=[window] * 2 + [total] * 2 + [part] * 2,
        in_specs=[vmem] * (2 + len(pieces)),
        out_specs=[vmem] * 6,
        compiler_params=limit(16),
        cost_estimate=cost(0.1),
    )(aperture, primaries, *pieces)

    handed_on = hand_on(far_panel, first_part)
    first, two, first_part, last_part = pl.pallas_call(
        functools.partial(kernel_b, late),
        out_shape=[window, jax.ShapeDtypeStruct((2 * BLK, 2 * BLK), jnp.bfloat16), part, part],
        in_specs=[vmem] * (8 + half),
        out_specs=[vmem] * 4,
        input_output_aliases={2: 0, 6: 2, 7: 3},
        compiler_params=limit(16),
        cost_estimate=cost(0.1),
    )(aperture, late_pieces[0], first, last, first_sum, last_sum, first_part, last_part, *panels[1:], far_panel)

    return pl.pallas_call(
        functools.partial(last_kernel, half + 1, late),
        out_shape=[jax.ShapeDtypeStruct((2, 2, BLK, width), jnp.float32), window],
        in_specs=[vmem] + [vmem] * (6 + len(handed_on)),
        out_specs=[anywhere, vmem],
        scratch_shapes=[pltpu.VMEM((2, 2, BLK, width), jnp.float32), pltpu.SemaphoreType.DMA((2, 2, PIECES))],
        input_output_aliases={3: 1},
        compiler_params=limit(16),
        cost_estimate=cost(1),
    )(aperture, held(late_pieces[1], two), first, last, two, first_part, last_part, *handed_on)[0]


def solution(mesh):
    placed = (P("freq", None, "src", "rcv"), P("freq", None, "src", "rcv"), P())
    return jax.shard_map(
        body, mesh=mesh, in_specs=placed, out_specs=P("freq", None, "src", "rcv"), check_vma=False
    )
```

```python
import functools

import jax
import jax.numpy as jnp
from jax import lax
from jax.experimental import pallas as pl
from jax.experimental.pallas import tpu as pltpu
from jax.sharding import PartitionSpec as P

BLK = 256
APER = 12
HW = 6
PIECES = 1


def after(value, *earlier):
    return lax.optimization_barrier((value, *earlier))[0]


def from_behind(x, axis, by):
    peers = lax.axis_size(axis)
    pairs = [(i, i + by) for i in range(peers) if 0 <= i + by < peers]
    return lax.ppermute(x, axis, pairs)


def swap(x, axis, bit):
    peers = lax.axis_size(axis)
    return lax.ppermute(x, axis, [(i, i ^ bit) for i in range(peers)])


def at_end():
    return (lax.axis_index("src") + 1) % lax.axis_size("src") < 2


def line_window(data):
    near_pairs = [(0, 1), (1, 0), (2, 3), (3, 2)]
    far = held(lax.ppermute(data, "src", [(0, 3), (1, 2), (2, 1), (3, 0)]), 5)
    near = lax.ppermute(data, "src", near_pairs)
    windows = []
    for v in range(data.shape[0]):
        across = lax.ppermute(far[v : v + 1], "src", near_pairs)
        windows.append([(data, v), (near, v), (across, 0), (far, v)])
    return windows


def hop_window(data):
    reach = min(HW, lax.axis_size("src") - 1)
    window = {0: data}
    for hop in range(1, reach + 1):
        window[-hop] = from_behind(window[1 - hop], "src", 1)
        window[hop] = from_behind(window[hop - 1], "src", -1)
    return [[(window[distance], v) for distance in range(-reach, reach + 1)] for v in range(data.shape[0])]


def gather_panels(primaries):
    bit = lax.axis_size("rcv") // 2
    panels = [primaries]
    for lower in range(1, bit):
        panels.append(swap(panels[lower & (lower - 1)], "rcv", lower & -lower))
    return panels, swap(primaries, "rcv", bit)


def hand_on(panel, token):
    bit = lax.axis_size("rcv") // 2
    panels = [after(panel, token)]
    for lower in range(1, bit):
        panels.append(swap(panels[lower & (lower - 1)], "rcv", lower & -lower))
    return panels[1:]


def fill_window(window, pieces):
    width = window.shape[-1] // 2
    for k, piece in pieces.items():
        window[k, :, :width] = piece[0]
        window[k, :, width:] = piece[1]


def slot_entries(aperture_ref, m, per_shard, depth):
    src = lax.axis_index("src")
    first_slot = lax.bitwise_xor(lax.axis_index("rcv"), m) * per_shard
    blocks = aperture_ref[...]
    at_row = lax.broadcasted_iota(jnp.int32, blocks.shape, 0) == src
    at_slot = lax.broadcasted_iota(jnp.int32, blocks.shape, 1)
    wanted = [jnp.sum(jnp.where(at_row & (at_slot == first_slot + q), blocks, 0)) for q in range(per_shard)]
    if lax.axis_size("src") == 4:
        return [lax.bitwise_xor(src, block) for block in wanted]
    return [block - src + depth // 2 for block in wanted]


def times(values, blocks):
    both = jnp.dot(values, blocks, preferred_element_type=jnp.float32)
    rows, width = both.shape[0] // 2, both.shape[1] // 2
    return both[:rows, :width] - both[rows:, width:], both[:rows, width:] + both[rows:, :width]


def rows_of(panel):
    return panel[...].reshape(2 * panel.shape[1], panel.shape[2])


def product(window, aperture_ref, panels, late_in_two=None, late=None):
    blocks = []
    for m, panel in panels.items():
        entries = slot_entries(aperture_ref, m, panel.shape[-1] // BLK, window.shape[0])
        blocks += [window[k] for k in entries]
    values = [rows_of(panel) for panel in panels.values()]
    if late_in_two is not None:
        values.append(late_in_two)
        blocks += [window[late]] * 2
    return times(jnp.concatenate(values, axis=1), jnp.concatenate(blocks, axis=0))


def sum_of_late(aperture_ref, panels, late, depth):
    total = None
    for m, panel in panels.items():
        values = rows_of(panel)
        for q, k in enumerate(slot_entries(aperture_ref, m, panel.shape[-1] // BLK, depth)):
            term = values[:, q * BLK : (q + 1) * BLK].astype(jnp.float32) * jnp.where(k == late, 1.0, 0.0)
            total = term if total is None else total + term
    return total


def in_two(total):
    high = total.astype(jnp.bfloat16)
    low = (total - high.astype(jnp.float32)).astype(jnp.bfloat16)
    return jnp.concatenate([high, low], axis=1)


def kernel_a(ats, late, aperture_ref, own_ref, *refs):
    piece_refs = list(refs[:-6])
    windows, sums, parts = refs[-6:-4], refs[-4:-2], refs[-2:]
    for v, (window, at) in enumerate(zip(windows, ats)):
        window[late] = jnp.zeros(window.shape[1:], window.dtype)
        fill_window(window, {k: piece_refs.pop(0).at[index] for k, index in at.items()})
        panels = {0: own_ref.at[v]}
        parts[v][0], parts[v][1] = product(window, aperture_ref, panels)
        sums[v][...] = sum_of_late(aperture_ref, panels, late, window.shape[0])


def kernel_b(late, aperture_ref, late_ref, _, last_window, first_sum, last_sum, first_in, last_in, *refs):
    *panel_refs, window, two, first_part, last_part = refs
    fill_window(window, {late: late_ref.at[0]})
    panels = [{1 + m: ref.at[v] for m, ref in enumerate(panel_refs)} for v in range(2)]
    real, imag = product(window, aperture_ref, panels[0], in_two(first_sum[...]), late)
    first_part[0] = first_in[0] + real
    first_part[1] = first_in[1] + imag
    real, imag = product(last_window, aperture_ref, panels[1])
    last_part[0] = last_in[0] + real
    last_part[1] = last_in[1] + imag
    two[...] = in_two(last_sum[...] + sum_of_late(aperture_ref, panels[1], late, last_window.shape[0]))


def last_kernel(far_half, late, aperture_ref, late_ref, first_window, _, two, first_part, last_part, *refs):
    *panel_refs, out_ref, window, result, sems = refs

    def finish(v, part, real, imag):
        copies = []
        for p, value in enumerate((real, imag)):
            result[v, p] = part[p] + value
            for chunk in range(PIECES):
                rows = pl.ds(chunk * (BLK // PIECES), BLK // PIECES)
                copies.append(
                    pltpu.make_async_copy(result.at[v, p, rows], out_ref.at[v, p, rows], sems.at[v, p, chunk])
                )
                copies[-1].start()
        return copies

    panels = [{far_half + m: ref.at[v] for m, ref in enumerate(panel_refs)} for v in range(2)]
    copies = finish(0, first_part, *product(first_window, aperture_ref, panels[0]))
    fill_window(window, {late: late_ref.at[0]})
    copies += finish(1, last_part, *product(window, aperture_ref, panels[1], two[...], late))
    for copy in copies:
        copy.wait()


def spec(space):
    return pl.BlockSpec(memory_space=space)


def cost(share):
    return pl.CostEstimate(flops=int(share * (8 * BLK * BLK * APER * BLK)), bytes_accessed=1 << 20, transcendentals=0)


def limit(megabytes):
    return pltpu.CompilerParams(vmem_limit_bytes=megabytes << 20)


def held(piece, share, *tokens):
    return pl.pallas_call(
        lambda *refs: None,
        out_shape=jax.ShapeDtypeStruct(piece.shape, piece.dtype),
        in_specs=[spec(pl.ANY)] * (1 + len(tokens)),
        out_specs=spec(pl.ANY),
        input_output_aliases={0: 0},
        compiler_params=limit(1),
        cost_estimate=cost(share),
    )(piece, *tokens)


def body(primaries, data, aperture):
    width = data.shape[3]
    line = lax.axis_size("src") == 4
    windows = (line_window if line else hop_window)(data)
    panels, far_panel = gather_panels(primaries)
    half = len(panels)
    late = 2 if line else len(windows[0]) - 1
    late_pieces = [piece[at : at + 1] for piece, at in (window[late] for window in windows)]
    early = [{k: piece for k, piece in enumerate(window) if k != late} for window in windows]
    vmem, anywhere = spec(pltpu.VMEM), spec(pl.ANY)
    window = jax.ShapeDtypeStruct((len(windows[0]), BLK, 2 * width), jnp.bfloat16)
    total = jax.ShapeDtypeStruct((2 * BLK, BLK), jnp.float32)
    part = jax.ShapeDtypeStruct((2, BLK, width), jnp.float32)

    pieces = [piece for window_pieces in early for piece, _ in window_pieces.values()]
    first, last, first_sum, last_sum, first_part, last_part = pl.pallas_call(
        functools.partial(kernel_a, [{k: at for k, (_, at) in pieces.items()} for pieces in early], late),
        out_shape=[window] * 2 + [total] * 2 + [part] * 2,
        in_specs=[vmem] * (2 + len(pieces)),
        out_specs=[vmem] * 6,
        compiler_params=limit(16),
        cost_estimate=cost(0.1),
    )(aperture, primaries, *pieces)

    far_panel = held(far_panel, 8, first_part)
    handed_on = hand_on(far_panel, first_part)
    first, two, first_part, last_part = pl.pallas_call(
        functools.partial(kernel_b, late),
        out_shape=[window, jax.ShapeDtypeStruct((2 * BLK, 2 * BLK), jnp.bfloat16), part, part],
        in_specs=[vmem] * (8 + half),
        out_specs=[vmem] * 4,
        input_output_aliases={2: 0, 6: 2, 7: 3},
        compiler_params=limit(16),
        cost_estimate=cost(0.1),
    )(aperture, late_pieces[0], first, last, first_sum, last_sum, first_part, last_part, *panels[1:], far_panel)

    return pl.pallas_call(
        functools.partial(last_kernel, half + 1, late),
        out_shape=[jax.ShapeDtypeStruct((2, 2, BLK, width), jnp.float32), window],
        in_specs=[vmem] + [vmem] * (6 + len(handed_on)),
        out_specs=[anywhere, vmem],
        scratch_shapes=[pltpu.VMEM((2, 2, BLK, width), jnp.float32), pltpu.SemaphoreType.DMA((2, 2, PIECES))],
        input_output_aliases={3: 1},
        compiler_params=limit(16),
        cost_estimate=cost(1),
    )(aperture, held(late_pieces[1], 12, two), first, last, two, first_part, last_part, *handed_on)[0]


def solution(mesh):
    placed = (P("freq", None, "src", "rcv"), P("freq", None, "src", "rcv"), P())
    return jax.shard_map(
        body, mesh=mesh, in_specs=placed, out_specs=P("freq", None, "src", "rcv"), check_vma=False
    )
```

```python
import functools

import jax
import jax.numpy as jnp
from jax import lax
from jax.experimental import pallas as pl
from jax.experimental.pallas import tpu as pltpu
from jax.sharding import PartitionSpec as P

BLK = 256
APER = 12
HW = 6
PIECES = 1


def after(value, *earlier):
    return lax.optimization_barrier((value, *earlier))[0]


def from_behind(x, axis, by):
    peers = lax.axis_size(axis)
    pairs = [(i, i + by) for i in range(peers) if 0 <= i + by < peers]
    return lax.ppermute(x, axis, pairs)


def swap(x, axis, bit):
    peers = lax.axis_size(axis)
    return lax.ppermute(x, axis, [(i, i ^ bit) for i in range(peers)])


def at_end():
    return (lax.axis_index("src") + 1) % lax.axis_size("src") < 2


def line_window(data):
    near_pairs = [(0, 1), (1, 0), (2, 3), (3, 2)]
    far = held(lax.ppermute(data, "src", [(0, 3), (1, 2), (2, 1), (3, 0)]), 5)
    near = lax.ppermute(data, "src", near_pairs)
    windows = []
    for v in range(data.shape[0]):
        across = lax.ppermute(far[v : v + 1], "src", near_pairs)
        windows.append([(data, v), (near, v), (across, 0), (far, v)])
    return windows


def hop_window(data):
    reach = min(HW, lax.axis_size("src") - 1)
    window = {0: data}
    for hop in range(1, reach + 1):
        window[-hop] = from_behind(window[1 - hop], "src", 1)
        window[hop] = from_behind(window[hop - 1], "src", -1)
    return [[(window[distance], v) for distance in range(-reach, reach + 1)] for v in range(data.shape[0])]


def gather_panels(primaries, first):
    bit = lax.axis_size("rcv") // 2
    panels = [after(primaries, first)]
    for lower in range(1, bit):
        panels.append(swap(panels[lower & (lower - 1)], "rcv", lower & -lower))
    return panels, swap(primaries, "rcv", bit)


def hand_on(panel, token):
    bit = lax.axis_size("rcv") // 2
    panels = [after(panel, token)]
    for lower in range(1, bit):
        panels.append(swap(panels[lower & (lower - 1)], "rcv", lower & -lower))
    return panels[1:]


def fill_window(window, pieces):
    width = window.shape[-1] // 2
    for k, piece in pieces.items():
        window[k, :, :width] = piece[0]
        window[k, :, width:] = piece[1]


def slot_entries(aperture_ref, m, per_shard, depth):
    src = lax.axis_index("src")
    first_slot = lax.bitwise_xor(lax.axis_index("rcv"), m) * per_shard
    blocks = aperture_ref[...]
    at_row = lax.broadcasted_iota(jnp.int32, blocks.shape, 0) == src
    at_slot = lax.broadcasted_iota(jnp.int32, blocks.shape, 1)
    wanted = [jnp.sum(jnp.where(at_row & (at_slot == first_slot + q), blocks, 0)) for q in range(per_shard)]
    if lax.axis_size("src") == 4:
        return [lax.bitwise_xor(src, block) for block in wanted]
    return [block - src + depth // 2 for block in wanted]


def times(values, blocks):
    both = jnp.dot(values, blocks, preferred_element_type=jnp.float32)
    rows, width = both.shape[0] // 2, both.shape[1] // 2
    return both[:rows, :width] - both[rows:, width:], both[:rows, width:] + both[rows:, :width]


def rows_of(panel):
    return panel[...].reshape(2 * panel.shape[1], panel.shape[2])


def product(window, aperture_ref, panels, late_in_two=None, late=None):
    blocks = []
    for m, panel in panels.items():
        entries = slot_entries(aperture_ref, m, panel.shape[-1] // BLK, window.shape[0])
        blocks += [window[k] for k in entries]
    values = [rows_of(panel) for panel in panels.values()]
    if late_in_two is not None:
        values.append(late_in_two)
        blocks += [window[late]] * 2
    return times(jnp.concatenate(values, axis=1), jnp.concatenate(blocks, axis=0))


def sum_of_late(aperture_ref, panels, late, depth):
    total = None
    for m, panel in panels.items():
        values = rows_of(panel)
        for q, k in enumerate(slot_entries(aperture_ref, m, panel.shape[-1] // BLK, depth)):
            term = values[:, q * BLK : (q + 1) * BLK].astype(jnp.float32) * jnp.where(k == late, 1.0, 0.0)
            total = term if total is None else total + term
    return total


def in_two(total):
    high = total.astype(jnp.bfloat16)
    low = (total - high.astype(jnp.float32)).astype(jnp.bfloat16)
    return jnp.concatenate([high, low], axis=1)


def kernel_a(ats, late, aperture_ref, own_ref, *refs):
    piece_refs = list(refs[:-6])
    windows, sums, parts = refs[-6:-4], refs[-4:-2], refs[-2:]
    for v, (window, at) in enumerate(zip(windows, ats)):
        window[late] = jnp.zeros(window.shape[1:], window.dtype)
        fill_window(window, {k: piece_refs.pop(0).at[index] for k, index in at.items()})
        panels = {0: own_ref.at[v]}
        parts[v][0], parts[v][1] = product(window, aperture_ref, panels)
        sums[v][...] = sum_of_late(aperture_ref, panels, late, window.shape[0])


def kernel_b(late, aperture_ref, late_ref, _, last_window, first_sum, last_sum, first_in, last_in, *refs):
    *panel_refs, window, two, first_part, last_part = refs
    fill_window(window, {late: late_ref.at[0]})
    panels = [{1 + m: ref.at[v] for m, ref in enumerate(panel_refs)} for v in range(2)]
    real, imag = product(window, aperture_ref, panels[0], in_two(first_sum[...]), late)
    first_part[0] = first_in[0] + real
    first_part[1] = first_in[1] + imag
    real, imag = product(last_window, aperture_ref, panels[1])
    last_part[0] = last_in[0] + real
    last_part[1] = last_in[1] + imag
    two[...] = in_two(last_sum[...] + sum_of_late(aperture_ref, panels[1], late, last_window.shape[0]))


def last_kernel(far_half, late, aperture_ref, late_ref, first_window, _, two, first_part, last_part, *refs):
    *panel_refs, out_ref, window, result, sems = refs

    def finish(v, part, real, imag):
        copies = []
        for p, value in enumerate((real, imag)):
            result[v, p] = part[p] + value
            for chunk in range(PIECES):
                rows = pl.ds(chunk * (BLK // PIECES), BLK // PIECES)
                copies.append(
                    pltpu.make_async_copy(result.at[v, p, rows], out_ref.at[v, p, rows], sems.at[v, p, chunk])
                )
                copies[-1].start()
        return copies

    panels = [{far_half + m: ref.at[v] for m, ref in enumerate(panel_refs)} for v in range(2)]
    copies = finish(0, first_part, *product(first_window, aperture_ref, panels[0]))
    fill_window(window, {late: late_ref.at[0]})
    copies += finish(1, last_part, *product(window, aperture_ref, panels[1], two[...], late))
    for copy in copies:
        copy.wait()


def spec(space):
    return pl.BlockSpec(memory_space=space)


def cost(share):
    return pl.CostEstimate(flops=int(share * (8 * BLK * BLK * APER * BLK)), bytes_accessed=1 << 20, transcendentals=0)


def limit(megabytes):
    return pltpu.CompilerParams(vmem_limit_bytes=megabytes << 20)


def held(piece, share, *tokens):
    return pl.pallas_call(
        lambda *refs: None,
        out_shape=jax.ShapeDtypeStruct(piece.shape, piece.dtype),
        in_specs=[spec(pl.ANY)] * (1 + len(tokens)),
        out_specs=spec(pl.ANY),
        input_output_aliases={0: 0},
        compiler_params=limit(1),
        cost_estimate=cost(share),
    )(piece, *tokens)


def body(primaries, data, aperture):
    width = data.shape[3]
    line = lax.axis_size("src") == 4
    windows = (line_window if line else hop_window)(data)
    panels, far_panel = gather_panels(primaries, windows[0][-1][0])
    half = len(panels)
    late = 2 if line else len(windows[0]) - 1
    late_pieces = [piece[at : at + 1] for piece, at in (window[late] for window in windows)]
    early = [{k: piece for k, piece in enumerate(window) if k != late} for window in windows]
    vmem, anywhere = spec(pltpu.VMEM), spec(pl.ANY)
    window = jax.ShapeDtypeStruct((len(windows[0]), BLK, 2 * width), jnp.bfloat16)
    total = jax.ShapeDtypeStruct((2 * BLK, BLK), jnp.float32)
    part = jax.ShapeDtypeStruct((2, BLK, width), jnp.float32)

    pieces = [piece for window_pieces in early for piece, _ in window_pieces.values()]
    first, last, first_sum, last_sum, first_part, last_part = pl.pallas_call(
        functools.partial(kernel_a, [{k: at for k, (_, at) in pieces.items()} for pieces in early], late),
        out_shape=[window] * 2 + [total] * 2 + [part] * 2,
        in_specs=[vmem] * (2 + len(pieces)),
        out_specs=[vmem] * 6,
        compiler_params=limit(16),
        cost_estimate=cost(0.1),
    )(aperture, primaries, *pieces)

    far_panel = held(far_panel, 12, first_part)
    handed_on = hand_on(far_panel, first_part)
    first, two, first_part, last_part = pl.pallas_call(
        functools.partial(kernel_b, late),
        out_shape=[window, jax.ShapeDtypeStruct((2 * BLK, 2 * BLK), jnp.bfloat16), part, part],
        in_specs=[vmem] * (8 + half),
        out_specs=[vmem] * 4,
        input_output_aliases={2: 0, 6: 2, 7: 3},
        compiler_params=limit(16),
        cost_estimate=cost(0.1),
    )(aperture, late_pieces[0], first, last, first_sum, last_sum, first_part, last_part, *panels[1:], far_panel)

    return pl.pallas_call(
        functools.partial(last_kernel, half + 1, late),
        out_shape=[jax.ShapeDtypeStruct((2, 2, BLK, width), jnp.float32), window],
        in_specs=[vmem] + [vmem] * (6 + len(handed_on)),
        out_specs=[anywhere, vmem],
        scratch_shapes=[pltpu.VMEM((2, 2, BLK, width), jnp.float32), pltpu.SemaphoreType.DMA((2, 2, PIECES))],
        input_output_aliases={3: 1},
        compiler_params=limit(16),
        cost_estimate=cost(1),
    )(aperture, held(late_pieces[1], 12, two), first, last, two, first_part, last_part, *handed_on)[0]


def solution(mesh):
    placed = (P("freq", None, "src", "rcv"), P("freq", None, "src", "rcv"), P())
    return jax.shard_map(
        body, mesh=mesh, in_specs=placed, out_specs=P("freq", None, "src", "rcv"), check_vma=False
    )
```

```python
import functools

import jax
import jax.numpy as jnp
from jax import lax
from jax.experimental import pallas as pl
from jax.experimental.pallas import tpu as pltpu
from jax.sharding import PartitionSpec as P

BLK = 256
APER = 12
HW = 6
HALVES = 2


def after(value, *earlier):
    return lax.optimization_barrier((value, *earlier))[0]


def from_behind(x, axis, by):
    peers = lax.axis_size(axis)
    pairs = [(i, i + by) for i in range(peers) if 0 <= i + by < peers]
    return lax.ppermute(x, axis, pairs)


def swap(x, axis, bit):
    peers = lax.axis_size(axis)
    return lax.ppermute(x, axis, [(i, i ^ bit) for i in range(peers)])


def at_end():
    return (lax.axis_index("src") + 1) % lax.axis_size("src") < 2


def line_window(data):
    near_pairs = [(0, 1), (1, 0), (2, 3), (3, 2)]
    far = held(lax.ppermute(data, "src", [(0, 3), (1, 2), (2, 1), (3, 0)]), 5)
    near = lax.ppermute(data, "src", near_pairs)
    windows = []
    for v in range(data.shape[0]):
        across = lax.ppermute(far[v : v + 1], "src", near_pairs)
        windows.append([(data, v), (near, v), (across, 0), (far, v)])
    return windows


def hop_window(data):
    reach = min(HW, lax.axis_size("src") - 1)
    window = {0: data}
    for hop in range(1, reach + 1):
        window[-hop] = from_behind(window[1 - hop], "src", 1)
        window[hop] = from_behind(window[hop - 1], "src", -1)
    return [[(window[distance], v) for distance in range(-reach, reach + 1)] for v in range(data.shape[0])]


def gather_panels(primaries, first):
    bit = lax.axis_size("rcv") // 2
    panels = [after(primaries, first)]
    for lower in range(1, bit):
        panels.append(swap(panels[lower & (lower - 1)], "rcv", lower & -lower))
    return panels, swap(primaries, "rcv", bit)


def hand_on(panel, token):
    bit = lax.axis_size("rcv") // 2
    panels = [after(panel, token)]
    for lower in range(1, bit):
        panels.append(swap(panels[lower & (lower - 1)], "rcv", lower & -lower))
    return panels[1:]


def fill_window(window, pieces):
    width = window.shape[-1] // 2
    for k, piece in pieces.items():
        window[k, :, :width] = piece[0]
        window[k, :, width:] = piece[1]


def slot_entries(aperture_ref, m, per_shard, depth):
    src = lax.axis_index("src")
    first_slot = lax.bitwise_xor(lax.axis_index("rcv"), m) * per_shard
    blocks = aperture_ref[...]
    at_row = lax.broadcasted_iota(jnp.int32, blocks.shape, 0) == src
    at_slot = lax.broadcasted_iota(jnp.int32, blocks.shape, 1)
    wanted = [jnp.sum(jnp.where(at_row & (at_slot == first_slot + q), blocks, 0)) for q in range(per_shard)]
    if lax.axis_size("src") == 4:
        return [lax.bitwise_xor(src, block) for block in wanted]
    return [block - src + depth // 2 for block in wanted]


def times(values, blocks):
    both = jnp.dot(values, blocks, preferred_element_type=jnp.float32)
    rows, width = both.shape[0] // 2, both.shape[1] // 2
    return both[:rows, :width] - both[rows:, width:], both[:rows, width:] + both[rows:, :width]


def rows_of(panel, rows=pl.ds(0, BLK)):
    return panel[:, rows].reshape(2 * rows.size, panel.shape[2])


def product(window, aperture_ref, panels, late_in_two=None, late=None, rows=pl.ds(0, BLK)):
    blocks = []
    for m, panel in panels.items():
        entries = slot_entries(aperture_ref, m, panel.shape[-1] // BLK, window.shape[0])
        blocks += [window[k] for k in entries]
    values = [rows_of(panel, rows) for panel in panels.values()]
    if late_in_two is not None:
        values.append(late_in_two)
        blocks += [window[late]] * 2
    return times(jnp.concatenate(values, axis=1), jnp.concatenate(blocks, axis=0))


def sum_of_late(aperture_ref, panels, late, depth):
    total = None
    for m, panel in panels.items():
        values = rows_of(panel)
        for q, k in enumerate(slot_entries(aperture_ref, m, panel.shape[-1] // BLK, depth)):
            term = values[:, q * BLK : (q + 1) * BLK].astype(jnp.float32) * jnp.where(k == late, 1.0, 0.0)
            total = term if total is None else total + term
    return total


def in_two(total):
    high = total.astype(jnp.bfloat16)
    low = (total - high.astype(jnp.float32)).astype(jnp.bfloat16)
    return jnp.concatenate([high, low], axis=1)


def kernel_a(ats, late, aperture_ref, own_ref, *refs):
    piece_refs = list(refs[:-6])
    windows, sums, parts = refs[-6:-4], refs[-4:-2], refs[-2:]
    for v, (window, at) in enumerate(zip(windows, ats)):
        window[late] = jnp.zeros(window.shape[1:], window.dtype)
        fill_window(window, {k: piece_refs.pop(0).at[index] for k, index in at.items()})
        panels = {0: own_ref.at[v]}
        parts[v][0], parts[v][1] = product(window, aperture_ref, panels)
        sums[v][...] = sum_of_late(aperture_ref, panels, late, window.shape[0])


def kernel_b(late, aperture_ref, late_ref, _, last_window, first_sum, last_sum, first_in, last_in, *refs):
    *panel_refs, window, two, first_part, last_part = refs
    fill_window(window, {late: late_ref.at[0]})
    panels = [{1 + m: ref.at[v] for m, ref in enumerate(panel_refs)} for v in range(2)]
    real, imag = product(window, aperture_ref, panels[0], in_two(first_sum[...]), late)
    first_part[0] = first_in[0] + real
    first_part[1] = first_in[1] + imag
    real, imag = product(last_window, aperture_ref, panels[1])
    last_part[0] = last_in[0] + real
    last_part[1] = last_in[1] + imag
    two[...] = in_two(last_sum[...] + sum_of_late(aperture_ref, panels[1], late, last_window.shape[0]))


def last_kernel(far_half, late, aperture_ref, late_ref, first_window, _, two, first_part, last_part, *refs):
    *panel_refs, out_ref, window, result, sems = refs

    def finish(v, rows, part, real, imag):
        copies = []
        for p, value in enumerate((real, imag)):
            result[v, p, rows] = part[p, rows] + value
            sem = sems.at[v, p, rows.start // (BLK // HALVES)]
            copies.append(pltpu.make_async_copy(result.at[v, p, rows], out_ref.at[v, p, rows], sem))
            copies[-1].start()
        return copies

    panels = [{far_half + m: ref.at[v] for m, ref in enumerate(panel_refs)} for v in range(2)]
    copies = finish(0, pl.ds(0, BLK), first_part, *product(first_window, aperture_ref, panels[0]))
    fill_window(window, {late: late_ref.at[0]})
    for half in range(HALVES):
        rows = pl.ds(half * (BLK // HALVES), BLK // HALVES)
        sums = jnp.concatenate([two[pl.ds(p * BLK + rows.start, rows.size)] for p in range(2)], axis=0)
        copies += finish(1, rows, last_part, *product(window, aperture_ref, panels[1], sums, late, rows))
    for copy in copies:
        copy.wait()


def spec(space):
    return pl.BlockSpec(memory_space=space)


def cost(share):
    return pl.CostEstimate(flops=int(share * (8 * BLK * BLK * APER * BLK)), bytes_accessed=1 << 20, transcendentals=0)


def limit(megabytes):
    return pltpu.CompilerParams(vmem_limit_bytes=megabytes << 20)


def held(piece, share, *tokens):
    return pl.pallas_call(
        lambda *refs: None,
        out_shape=jax.ShapeDtypeStruct(piece.shape, piece.dtype),
        in_specs=[spec(pl.ANY)] * (1 + len(tokens)),
        out_specs=spec(pl.ANY),
        input_output_aliases={0: 0},
        compiler_params=limit(1),
        cost_estimate=cost(share),
    )(piece, *tokens)


def body(primaries, data, aperture):
    width = data.shape[3]
    line = lax.axis_size("src") == 4
    windows = (line_window if line else hop_window)(data)
    panels, far_panel = gather_panels(primaries, windows[0][-1][0])
    half = len(panels)
    late = 2 if line else len(windows[0]) - 1
    late_pieces = [piece[at : at + 1] for piece, at in (window[late] for window in windows)]
    early = [{k: piece for k, piece in enumerate(window) if k != late} for window in windows]
    vmem, anywhere = spec(pltpu.VMEM), spec(pl.ANY)
    window = jax.ShapeDtypeStruct((len(windows[0]), BLK, 2 * width), jnp.bfloat16)
    total = jax.ShapeDtypeStruct((2 * BLK, BLK), jnp.float32)
    part = jax.ShapeDtypeStruct((2, BLK, width), jnp.float32)

    pieces = [piece for window_pieces in early for piece, _ in window_pieces.values()]
    first, last, first_sum, last_sum, first_part, last_part = pl.pallas_call(
        functools.partial(kernel_a, [{k: at for k, (_, at) in pieces.items()} for pieces in early], late),
        out_shape=[window] * 2 + [total] * 2 + [part] * 2,
        in_specs=[vmem] * (2 + len(pieces)),
        out_specs=[vmem] * 6,
        compiler_params=limit(16),
        cost_estimate=cost(0.1),
    )(aperture, primaries, *pieces)

    far_panel = held(far_panel, 12, first_part)
    handed_on = hand_on(far_panel, first_part)
    first, two, first_part, last_part = pl.pallas_call(
        functools.partial(kernel_b, late),
        out_shape=[window, jax.ShapeDtypeStruct((2 * BLK, 2 * BLK), jnp.bfloat16), part, part],
        in_specs=[vmem] * (8 + half),
        out_specs=[vmem] * 4,
        input_output_aliases={2: 0, 6: 2, 7: 3},
        compiler_params=limit(16),
        cost_estimate=cost(0.1),
    )(aperture, late_pieces[0], first, last, first_sum, last_sum, first_part, last_part, *panels[1:], far_panel)

    return pl.pallas_call(
        functools.partial(last_kernel, half + 1, late),
        out_shape=[jax.ShapeDtypeStruct((2, 2, BLK, width), jnp.float32), window],
        in_specs=[vmem] + [vmem] * (6 + len(handed_on)),
        out_specs=[anywhere, vmem],
        scratch_shapes=[pltpu.VMEM((2, 2, BLK, width), jnp.float32), pltpu.SemaphoreType.DMA((2, 2, HALVES))],
        input_output_aliases={3: 1},
        compiler_params=limit(16),
        cost_estimate=cost(1),
    )(aperture, held(late_pieces[1], 12, two), first, last, two, first_part, last_part, *handed_on)[0]


def solution(mesh):
    placed = (P("freq", None, "src", "rcv"), P("freq", None, "src", "rcv"), P())
    return jax.shard_map(
        body, mesh=mesh, in_specs=placed, out_specs=P("freq", None, "src", "rcv"), check_vma=False
    )
```

```python
import functools

import jax
import jax.numpy as jnp
from jax import lax
from jax.experimental import pallas as pl
from jax.experimental.pallas import tpu as pltpu
from jax.sharding import PartitionSpec as P

BLK = 256
APER = 12
HW = 6
PIECES = 1


def after(value, *earlier):
    return lax.optimization_barrier((value, *earlier))[0]


def from_behind(x, axis, by):
    peers = lax.axis_size(axis)
    pairs = [(i, i + by) for i in range(peers) if 0 <= i + by < peers]
    return lax.ppermute(x, axis, pairs)


def swap(x, axis, bit):
    peers = lax.axis_size(axis)
    return lax.ppermute(x, axis, [(i, i ^ bit) for i in range(peers)])


def at_end():
    return (lax.axis_index("src") + 1) % lax.axis_size("src") < 2


def line_window(data):
    near_pairs = [(0, 1), (1, 0), (2, 3), (3, 2)]
    far = held(lax.ppermute(data, "src", [(0, 3), (1, 2), (2, 1), (3, 0)]), 5)
    near = lax.ppermute(data, "src", near_pairs)
    windows = []
    for v in range(data.shape[0]):
        across = lax.ppermute(far[v : v + 1], "src", near_pairs)
        windows.append([(data, v), (near, v), (across, 0), (far, v)])
    return windows


def hop_window(data):
    reach = min(HW, lax.axis_size("src") - 1)
    window = {0: data}
    for hop in range(1, reach + 1):
        window[-hop] = from_behind(window[1 - hop], "src", 1)
        window[hop] = from_behind(window[hop - 1], "src", -1)
    return [[(window[distance], v) for distance in range(-reach, reach + 1)] for v in range(data.shape[0])]


def gather_panels(primaries, first):
    bit = lax.axis_size("rcv") // 2
    panels = [after(primaries, first)]
    for lower in range(1, bit):
        panels.append(swap(panels[lower & (lower - 1)], "rcv", lower & -lower))
    return panels, swap(primaries, "rcv", bit)


def hand_on(panel, token):
    bit = lax.axis_size("rcv") // 2
    panels = [after(panel, token)]
    for lower in range(1, bit):
        panels.append(swap(panels[lower & (lower - 1)], "rcv", lower & -lower))
    return panels[1:]


def fill_window(window, pieces):
    width = window.shape[-1] // 2
    for k, piece in pieces.items():
        window[k, :, :width] = piece[0]
        window[k, :, width:] = piece[1]


def slot_entries(aperture_ref, m, per_shard, depth):
    src = lax.axis_index("src")
    first_slot = lax.bitwise_xor(lax.axis_index("rcv"), m) * per_shard
    blocks = aperture_ref[...]
    at_row = lax.broadcasted_iota(jnp.int32, blocks.shape, 0) == src
    at_slot = lax.broadcasted_iota(jnp.int32, blocks.shape, 1)
    wanted = [jnp.sum(jnp.where(at_row & (at_slot == first_slot + q), blocks, 0)) for q in range(per_shard)]
    if lax.axis_size("src") == 4:
        return [lax.bitwise_xor(src, block) for block in wanted]
    return [block - src + depth // 2 for block in wanted]


def times(values, blocks):
    both = jnp.dot(values, blocks, preferred_element_type=jnp.float32)
    rows, width = both.shape[0] // 2, both.shape[1] // 2
    return both[:rows, :width] - both[rows:, width:], both[:rows, width:] + both[rows:, :width]


def rows_of(panel):
    return panel[...].reshape(2 * panel.shape[1], panel.shape[2])


def product(window, aperture_ref, panels, late_in_two=None, late=None):
    blocks = []
    for m, panel in panels.items():
        entries = slot_entries(aperture_ref, m, panel.shape[-1] // BLK, window.shape[0])
        blocks += [window[k] for k in entries]
    values = [rows_of(panel) for panel in panels.values()]
    if late_in_two is not None:
        values.append(late_in_two)
        blocks += [window[late]] * 2
    return times(jnp.concatenate(values, axis=1), jnp.concatenate(blocks, axis=0))


def sum_of_late(aperture_ref, panels, late, depth):
    total = None
    for m, panel in panels.items():
        values = rows_of(panel)
        for q, k in enumerate(slot_entries(aperture_ref, m, panel.shape[-1] // BLK, depth)):
            term = values[:, q * BLK : (q + 1) * BLK].astype(jnp.float32) * jnp.where(k == late, 1.0, 0.0)
            total = term if total is None else total + term
    return total


def in_two(total):
    high = total.astype(jnp.bfloat16)
    low = (total - high.astype(jnp.float32)).astype(jnp.bfloat16)
    return jnp.concatenate([high, low], axis=1)


def kernel_a(ats, late, aperture_ref, own_ref, *refs):
    piece_refs = list(refs[:-6])
    windows, sums, parts = refs[-6:-4], refs[-4:-2], refs[-2:]
    for v, (window, at) in enumerate(zip(windows, ats)):
        window[late] = jnp.zeros(window.shape[1:], window.dtype)
        fill_window(window, {k: piece_refs.pop(0).at[index] for k, index in at.items()})
        panels = {0: own_ref.at[v]}
        parts[v][0], parts[v][1] = product(window, aperture_ref, panels)
        sums[v][...] = sum_of_late(aperture_ref, panels, late, window.shape[0])


def kernel_b(late, aperture_ref, late_ref, _, last_window, first_sum, last_sum, first_in, last_in, *refs):
    *panel_refs, window, two, first_part, last_part = refs
    fill_window(window, {late: late_ref.at[0]})
    panels = [{1 + m: ref.at[v] for m, ref in enumerate(panel_refs)} for v in range(2)]
    real, imag = product(window, aperture_ref, panels[0], in_two(first_sum[...]), late)
    first_part[0] = first_in[0] + real
    first_part[1] = first_in[1] + imag
    real, imag = product(last_window, aperture_ref, panels[1])
    last_part[0] = last_in[0] + real
    last_part[1] = last_in[1] + imag
    two[...] = in_two(last_sum[...] + sum_of_late(aperture_ref, panels[1], late, last_window.shape[0]))


def last_kernel(far_half, late, aperture_ref, late_ref, first_window, _, two, first_part, last_part, *refs):
    *panel_refs, out_ref, window, result, sems = refs

    def finish(v, part, real, imag):
        copies = []
        for p, value in enumerate((real, imag)):
            result[v, p] = part[p] + value
            for chunk in range(PIECES):
                rows = pl.ds(chunk * (BLK // PIECES), BLK // PIECES)
                copies.append(
                    pltpu.make_async_copy(result.at[v, p, rows], out_ref.at[v, p, rows], sems.at[v, p, chunk])
                )
                copies[-1].start(priority=v)
        return copies

    panels = [{far_half + m: ref.at[v] for m, ref in enumerate(panel_refs)} for v in range(2)]
    copies = finish(0, first_part, *product(first_window, aperture_ref, panels[0]))
    fill_window(window, {late: late_ref.at[0]})
    copies += finish(1, last_part, *product(window, aperture_ref, panels[1], two[...], late))
    for copy in copies:
        copy.wait()


def spec(space):
    return pl.BlockSpec(memory_space=space)


def cost(share):
    return pl.CostEstimate(flops=int(share * (8 * BLK * BLK * APER * BLK)), bytes_accessed=1 << 20, transcendentals=0)


def limit(megabytes):
    return pltpu.CompilerParams(vmem_limit_bytes=megabytes << 20)


def held(piece, share, *tokens):
    return pl.pallas_call(
        lambda *refs: None,
        out_shape=jax.ShapeDtypeStruct(piece.shape, piece.dtype),
        in_specs=[spec(pl.ANY)] * (1 + len(tokens)),
        out_specs=spec(pl.ANY),
        input_output_aliases={0: 0},
        compiler_params=limit(1),
        cost_estimate=cost(share),
    )(piece, *tokens)


def body(primaries, data, aperture):
    width = data.shape[3]
    line = lax.axis_size("src") == 4
    windows = (line_window if line else hop_window)(data)
    panels, far_panel = gather_panels(primaries, windows[0][-1][0])
    half = len(panels)
    late = 2 if line else len(windows[0]) - 1
    late_pieces = [piece[at : at + 1] for piece, at in (window[late] for window in windows)]
    early = [{k: piece for k, piece in enumerate(window) if k != late} for window in windows]
    vmem, anywhere = spec(pltpu.VMEM), spec(pl.ANY)
    window = jax.ShapeDtypeStruct((len(windows[0]), BLK, 2 * width), jnp.bfloat16)
    total = jax.ShapeDtypeStruct((2 * BLK, BLK), jnp.float32)
    part = jax.ShapeDtypeStruct((2, BLK, width), jnp.float32)

    pieces = [piece for window_pieces in early for piece, _ in window_pieces.values()]
    first, last, first_sum, last_sum, first_part, last_part = pl.pallas_call(
        functools.partial(kernel_a, [{k: at for k, (_, at) in pieces.items()} for pieces in early], late),
        out_shape=[window] * 2 + [total] * 2 + [part] * 2,
        in_specs=[vmem] * (2 + len(pieces)),
        out_specs=[vmem] * 6,
        compiler_params=limit(16),
        cost_estimate=cost(0.1),
    )(aperture, primaries, *pieces)

    far_panel = held(far_panel, 12, first_part)
    handed_on = hand_on(far_panel, first_part)
    first, two, first_part, last_part = pl.pallas_call(
        functools.partial(kernel_b, late),
        out_shape=[window, jax.ShapeDtypeStruct((2 * BLK, 2 * BLK), jnp.bfloat16), part, part],
        in_specs=[vmem] * (8 + half),
        out_specs=[vmem] * 4,
        input_output_aliases={2: 0, 6: 2, 7: 3},
        compiler_params=limit(16),
        cost_estimate=cost(0.1),
    )(aperture, late_pieces[0], first, last, first_sum, last_sum, first_part, last_part, *panels[1:], far_panel)

    return pl.pallas_call(
        functools.partial(last_kernel, half + 1, late),
        out_shape=[jax.ShapeDtypeStruct((2, 2, BLK, width), jnp.float32), window],
        in_specs=[vmem] + [vmem] * (6 + len(handed_on)),
        out_specs=[anywhere, vmem],
        scratch_shapes=[pltpu.VMEM((2, 2, BLK, width), jnp.float32), pltpu.SemaphoreType.DMA((2, 2, PIECES))],
        input_output_aliases={3: 1},
        compiler_params=limit(16),
        cost_estimate=cost(1),
    )(aperture, held(late_pieces[1], 12, two), first, last, two, first_part, last_part, *handed_on)[0]


def solution(mesh):
    placed = (P("freq", None, "src", "rcv"), P("freq", None, "src", "rcv"), P())
    return jax.shard_map(
        body, mesh=mesh, in_specs=placed, out_specs=P("freq", None, "src", "rcv"), check_vma=False
    )
```

```python
import functools

import jax
import jax.numpy as jnp
from jax import lax
from jax.experimental import pallas as pl
from jax.experimental.pallas import tpu as pltpu
from jax.sharding import PartitionSpec as P

BLK = 256
APER = 12
HW = 6
PIECES = 1


def after(value, *earlier):
    return lax.optimization_barrier((value, *earlier))[0]


def from_behind(x, axis, by):
    peers = lax.axis_size(axis)
    pairs = [(i, i + by) for i in range(peers) if 0 <= i + by < peers]
    return lax.ppermute(x, axis, pairs)


def swap(x, axis, bit):
    peers = lax.axis_size(axis)
    return lax.ppermute(x, axis, [(i, i ^ bit) for i in range(peers)])


def at_end():
    return (lax.axis_index("src") + 1) % lax.axis_size("src") < 2


def line_window(data):
    near_pairs = [(0, 1), (1, 0), (2, 3), (3, 2)]
    far = held(lax.ppermute(data, "src", [(0, 2), (1, 3), (2, 0), (3, 1)]), 5)
    near = lax.ppermute(data, "src", near_pairs)
    windows = []
    for v in range(data.shape[0]):
        across = lax.ppermute(far[v : v + 1], "src", near_pairs)
        windows.append([(data, v), (near, v), (far, v), (across, 0)])
    return windows


def hop_window(data):
    reach = min(HW, lax.axis_size("src") - 1)
    window = {0: data}
    for hop in range(1, reach + 1):
        window[-hop] = from_behind(window[1 - hop], "src", 1)
        window[hop] = from_behind(window[hop - 1], "src", -1)
    return [[(window[distance], v) for distance in range(-reach, reach + 1)] for v in range(data.shape[0])]


def gather_panels(primaries, first):
    bit = lax.axis_size("rcv") // 2
    panels = [after(primaries, first)]
    for lower in range(1, bit):
        panels.append(swap(panels[lower & (lower - 1)], "rcv", lower & -lower))
    return panels, swap(primaries, "rcv", bit)


def hand_on(panel, token):
    bit = lax.axis_size("rcv") // 2
    panels = [after(panel, token)]
    for lower in range(1, bit):
        panels.append(swap(panels[lower & (lower - 1)], "rcv", lower & -lower))
    return panels[1:]


def fill_window(window, pieces):
    width = window.shape[-1] // 2
    for k, piece in pieces.items():
        window[k, :, :width] = piece[0]
        window[k, :, width:] = piece[1]


def slot_entries(aperture_ref, m, per_shard, depth):
    src = lax.axis_index("src")
    first_slot = lax.bitwise_xor(lax.axis_index("rcv"), m) * per_shard
    blocks = aperture_ref[...]
    at_row = lax.broadcasted_iota(jnp.int32, blocks.shape, 0) == src
    at_slot = lax.broadcasted_iota(jnp.int32, blocks.shape, 1)
    wanted = [jnp.sum(jnp.where(at_row & (at_slot == first_slot + q), blocks, 0)) for q in range(per_shard)]
    if lax.axis_size("src") == 4:
        return [lax.bitwise_xor(src, block) for block in wanted]
    return [block - src + depth // 2 for block in wanted]


def times(values, blocks):
    both = jnp.dot(values, blocks, preferred_element_type=jnp.float32)
    rows, width = both.shape[0] // 2, both.shape[1] // 2
    return both[:rows, :width] - both[rows:, width:], both[:rows, width:] + both[rows:, :width]


def rows_of(panel):
    return panel[...].reshape(2 * panel.shape[1], panel.shape[2])


def product(window, aperture_ref, panels, late_in_two=None, late=None):
    blocks = []
    for m, panel in panels.items():
        entries = slot_entries(aperture_ref, m, panel.shape[-1] // BLK, window.shape[0])
        blocks += [window[k] for k in entries]
    values = [rows_of(panel) for panel in panels.values()]
    if late_in_two is not None:
        values.append(late_in_two)
        blocks += [window[late]] * 2
    return times(jnp.concatenate(values, axis=1), jnp.concatenate(blocks, axis=0))


def sum_of_late(aperture_ref, panels, late, depth):
    total = None
    for m, panel in panels.items():
        values = rows_of(panel)
        for q, k in enumerate(slot_entries(aperture_ref, m, panel.shape[-1] // BLK, depth)):
            term = values[:, q * BLK : (q + 1) * BLK].astype(jnp.float32) * jnp.where(k == late, 1.0, 0.0)
            total = term if total is None else total + term
    return total


def in_two(total):
    high = total.astype(jnp.bfloat16)
    low = (total - high.astype(jnp.float32)).astype(jnp.bfloat16)
    return jnp.concatenate([high, low], axis=1)


def kernel_a(ats, late, aperture_ref, own_ref, *refs):
    piece_refs = list(refs[:-6])
    windows, sums, parts = refs[-6:-4], refs[-4:-2], refs[-2:]
    for v, (window, at) in enumerate(zip(windows, ats)):
        window[late] = jnp.zeros(window.shape[1:], window.dtype)
        fill_window(window, {k: piece_refs.pop(0).at[index] for k, index in at.items()})
        panels = {0: own_ref.at[v]}
        parts[v][0], parts[v][1] = product(window, aperture_ref, panels)
        sums[v][...] = sum_of_late(aperture_ref, panels, late, window.shape[0])


def kernel_b(late, aperture_ref, late_ref, _, last_window, first_sum, last_sum, first_in, last_in, *refs):
    *panel_refs, window, two, first_part, last_part = refs
    fill_window(window, {late: late_ref.at[0]})
    panels = [{1 + m: ref.at[v] for m, ref in enumerate(panel_refs)} for v in range(2)]
    real, imag = product(window, aperture_ref, panels[0], in_two(first_sum[...]), late)
    first_part[0] = first_in[0] + real
    first_part[1] = first_in[1] + imag
    real, imag = product(last_window, aperture_ref, panels[1])
    last_part[0] = last_in[0] + real
    last_part[1] = last_in[1] + imag
    two[...] = in_two(last_sum[...] + sum_of_late(aperture_ref, panels[1], late, last_window.shape[0]))


def last_kernel(far_half, late, aperture_ref, late_ref, first_window, _, two, first_part, last_part, *refs):
    *panel_refs, out_ref, window, result, sems = refs

    def finish(v, part, real, imag):
        copies = []
        for p, value in enumerate((real, imag)):
            result[v, p] = part[p] + value
            for chunk in range(PIECES):
                rows = pl.ds(chunk * (BLK // PIECES), BLK // PIECES)
                copies.append(
                    pltpu.make_async_copy(result.at[v, p, rows], out_ref.at[v, p, rows], sems.at[v, p, chunk])
                )
                copies[-1].start()
        return copies

    panels = [{far_half + m: ref.at[v] for m, ref in enumerate(panel_refs)} for v in range(2)]
    copies = finish(0, first_part, *product(first_window, aperture_ref, panels[0]))
    fill_window(window, {late: late_ref.at[0]})
    copies += finish(1, last_part, *product(window, aperture_ref, panels[1], two[...], late))
    for copy in copies:
        copy.wait()


def spec(space):
    return pl.BlockSpec(memory_space=space)


def cost(share):
    return pl.CostEstimate(flops=int(share * (8 * BLK * BLK * APER * BLK)), bytes_accessed=1 << 20, transcendentals=0)


def limit(megabytes):
    return pltpu.CompilerParams(vmem_limit_bytes=megabytes << 20)


def held(piece, share, *tokens):
    return pl.pallas_call(
        lambda *refs: None,
        out_shape=jax.ShapeDtypeStruct(piece.shape, piece.dtype),
        in_specs=[spec(pl.ANY)] * (1 + len(tokens)),
        out_specs=spec(pl.ANY),
        input_output_aliases={0: 0},
        compiler_params=limit(1),
        cost_estimate=cost(share),
    )(piece, *tokens)


def body(primaries, data, aperture):
    width = data.shape[3]
    line = lax.axis_size("src") == 4
    windows = (line_window if line else hop_window)(data)
    panels, far_panel = gather_panels(primaries, windows[0][-2][0])
    half = len(panels)
    late = len(windows[0]) - 1
    late_pieces = [piece[at : at + 1] for piece, at in (window[late] for window in windows)]
    early = [{k: piece for k, piece in enumerate(window) if k != late} for window in windows]
    vmem, anywhere = spec(pltpu.VMEM), spec(pl.ANY)
    window = jax.ShapeDtypeStruct((len(windows[0]), BLK, 2 * width), jnp.bfloat16)
    total = jax.ShapeDtypeStruct((2 * BLK, BLK), jnp.float32)
    part = jax.ShapeDtypeStruct((2, BLK, width), jnp.float32)

    pieces = [piece for window_pieces in early for piece, _ in window_pieces.values()]
    first, last, first_sum, last_sum, first_part, last_part = pl.pallas_call(
        functools.partial(kernel_a, [{k: at for k, (_, at) in pieces.items()} for pieces in early], late),
        out_shape=[window] * 2 + [total] * 2 + [part] * 2,
        in_specs=[vmem] * (2 + len(pieces)),
        out_specs=[vmem] * 6,
        compiler_params=limit(16),
        cost_estimate=cost(0.1),
    )(aperture, primaries, *pieces)

    far_panel = held(far_panel, 12, first_part)
    handed_on = hand_on(far_panel, first_part)
    first, two, first_part, last_part = pl.pallas_call(
        functools.partial(kernel_b, late),
        out_shape=[window, jax.ShapeDtypeStruct((2 * BLK, 2 * BLK), jnp.bfloat16), part, part],
        in_specs=[vmem] * (8 + half),
        out_specs=[vmem] * 4,
        input_output_aliases={2: 0, 6: 2, 7: 3},
        compiler_params=limit(16),
        cost_estimate=cost(0.1),
    )(aperture, late_pieces[0], first, last, first_sum, last_sum, first_part, last_part, *panels[1:], far_panel)

    return pl.pallas_call(
        functools.partial(last_kernel, half + 1, late),
        out_shape=[jax.ShapeDtypeStruct((2, 2, BLK, width), jnp.float32), window],
        in_specs=[vmem] + [vmem] * (6 + len(handed_on)),
        out_specs=[anywhere, vmem],
        scratch_shapes=[pltpu.VMEM((2, 2, BLK, width), jnp.float32), pltpu.SemaphoreType.DMA((2, 2, PIECES))],
        input_output_aliases={3: 1},
        compiler_params=limit(16),
        cost_estimate=cost(1),
    )(aperture, held(late_pieces[1], 12, two), first, last, two, first_part, last_part, *handed_on)[0]


def solution(mesh):
    placed = (P("freq", None, "src", "rcv"), P("freq", None, "src", "rcv"), P())
    return jax.shard_map(
        body, mesh=mesh, in_specs=placed, out_specs=P("freq", None, "src", "rcv"), check_vma=False
    )
```

```python
import functools

import jax
import jax.numpy as jnp
from jax import lax
from jax.experimental import pallas as pl
from jax.experimental.pallas import tpu as pltpu
from jax.sharding import PartitionSpec as P

BLK = 256
APER = 12
HW = 6
PIECES = 1


def after(value, *earlier):
    return lax.optimization_barrier((value, *earlier))[0]


def from_behind(x, axis, by):
    peers = lax.axis_size(axis)
    pairs = [(i, i + by) for i in range(peers) if 0 <= i + by < peers]
    return lax.ppermute(x, axis, pairs)


def swap(x, axis, bit):
    peers = lax.axis_size(axis)
    return lax.ppermute(x, axis, [(i, i ^ bit) for i in range(peers)])


def at_end():
    return (lax.axis_index("src") + 1) % lax.axis_size("src") < 2


def line_window(data):
    near_pairs = [(0, 1), (1, 0), (2, 3), (3, 2)]
    near = lax.ppermute(data, "src", near_pairs)
    far = lax.ppermute(data, "src", [(0, 2), (1, 3), (2, 0), (3, 1)])
    near, far = lax.optimization_barrier((near, far))
    far = held(far, 5)
    windows = []
    for v in range(data.shape[0]):
        across = lax.ppermute(far[v : v + 1], "src", near_pairs)
        windows.append([(data, v), (near, v), (far, v), (across, 0)])
    return windows


def hop_window(data):
    reach = min(HW, lax.axis_size("src") - 1)
    window = {0: data}
    for hop in range(1, reach + 1):
        window[-hop] = from_behind(window[1 - hop], "src", 1)
        window[hop] = from_behind(window[hop - 1], "src", -1)
    return [[(window[distance], v) for distance in range(-reach, reach + 1)] for v in range(data.shape[0])]


def gather_panels(primaries, first):
    bit = lax.axis_size("rcv") // 2
    panels = [after(primaries, first)]
    for lower in range(1, bit):
        panels.append(swap(panels[lower & (lower - 1)], "rcv", lower & -lower))
    return panels, swap(primaries, "rcv", bit)


def hand_on(panel, token):
    bit = lax.axis_size("rcv") // 2
    panels = [after(panel, token)]
    for lower in range(1, bit):
        panels.append(swap(panels[lower & (lower - 1)], "rcv", lower & -lower))
    return panels[1:]


def fill_window(window, pieces):
    width = window.shape[-1] // 2
    for k, piece in pieces.items():
        window[k, :, :width] = piece[0]
        window[k, :, width:] = piece[1]


def slot_entries(aperture_ref, m, per_shard, depth):
    src = lax.axis_index("src")
    first_slot = lax.bitwise_xor(lax.axis_index("rcv"), m) * per_shard
    blocks = aperture_ref[...]
    at_row = lax.broadcasted_iota(jnp.int32, blocks.shape, 0) == src
    at_slot = lax.broadcasted_iota(jnp.int32, blocks.shape, 1)
    wanted = [jnp.sum(jnp.where(at_row & (at_slot == first_slot + q), blocks, 0)) for q in range(per_shard)]
    if lax.axis_size("src") == 4:
        return [lax.bitwise_xor(src, block) for block in wanted]
    return [block - src + depth // 2 for block in wanted]


def times(values, blocks):
    both = jnp.dot(values, blocks, preferred_element_type=jnp.float32)
    rows, width = both.shape[0] // 2, both.shape[1] // 2
    return both[:rows, :width] - both[rows:, width:], both[:rows, width:] + both[rows:, :width]


def rows_of(panel):
    return panel[...].reshape(2 * panel.shape[1], panel.shape[2])


def product(window, aperture_ref, panels, late_in_two=None, late=None):
    blocks = []
    for m, panel in panels.items():
        entries = slot_entries(aperture_ref, m, panel.shape[-1] // BLK, window.shape[0])
        blocks += [window[k] for k in entries]
    values = [rows_of(panel) for panel in panels.values()]
    if late_in_two is not None:
        values.append(late_in_two)
        blocks += [window[late]] * 2
    return times(jnp.concatenate(values, axis=1), jnp.concatenate(blocks, axis=0))


def sum_of_late(aperture_ref, panels, late, depth):
    total = None
    for m, panel in panels.items():
        values = rows_of(panel)
        for q, k in enumerate(slot_entries(aperture_ref, m, panel.shape[-1] // BLK, depth)):
            term = values[:, q * BLK : (q + 1) * BLK].astype(jnp.float32) * jnp.where(k == late, 1.0, 0.0)
            total = term if total is None else total + term
    return total


def in_two(total):
    high = total.astype(jnp.bfloat16)
    low = (total - high.astype(jnp.float32)).astype(jnp.bfloat16)
    return jnp.concatenate([high, low], axis=1)


def kernel_a(ats, late, aperture_ref, own_ref, *refs):
    piece_refs = list(refs[:-6])
    windows, sums, parts = refs[-6:-4], refs[-4:-2], refs[-2:]
    for v, (window, at) in enumerate(zip(windows, ats)):
        window[late] = jnp.zeros(window.shape[1:], window.dtype)
        fill_window(window, {k: piece_refs.pop(0).at[index] for k, index in at.items()})
        panels = {0: own_ref.at[v]}
        parts[v][0], parts[v][1] = product(window, aperture_ref, panels)
        sums[v][...] = sum_of_late(aperture_ref, panels, late, window.shape[0])


def kernel_b(late, aperture_ref, late_ref, _, last_window, first_sum, last_sum, first_in, last_in, *refs):
    *panel_refs, window, two, first_part, last_part = refs
    fill_window(window, {late: late_ref.at[0]})
    panels = [{1 + m: ref.at[v] for m, ref in enumerate(panel_refs)} for v in range(2)]
    real, imag = product(window, aperture_ref, panels[0], in_two(first_sum[...]), late)
    first_part[0] = first_in[0] + real
    first_part[1] = first_in[1] + imag
    real, imag = product(last_window, aperture_ref, panels[1])
    last_part[0] = last_in[0] + real
    last_part[1] = last_in[1] + imag
    two[...] = in_two(last_sum[...] + sum_of_late(aperture_ref, panels[1], late, last_window.shape[0]))


def last_kernel(far_half, late, aperture_ref, late_ref, first_window, _, two, first_part, last_part, *refs):
    *panel_refs, out_ref, window, result, sems = refs

    def finish(v, part, real, imag):
        copies = []
        for p, value in enumerate((real, imag)):
            result[v, p] = part[p] + value
            for chunk in range(PIECES):
                rows = pl.ds(chunk * (BLK // PIECES), BLK // PIECES)
                copies.append(
                    pltpu.make_async_copy(result.at[v, p, rows], out_ref.at[v, p, rows], sems.at[v, p, chunk])
                )
                copies[-1].start()
        return copies

    panels = [{far_half + m: ref.at[v] for m, ref in enumerate(panel_refs)} for v in range(2)]
    copies = finish(0, first_part, *product(first_window, aperture_ref, panels[0]))
    fill_window(window, {late: late_ref.at[0]})
    copies += finish(1, last_part, *product(window, aperture_ref, panels[1], two[...], late))
    for copy in copies:
        copy.wait()


def spec(space):
    return pl.BlockSpec(memory_space=space)


def cost(share):
    return pl.CostEstimate(flops=int(share * (8 * BLK * BLK * APER * BLK)), bytes_accessed=1 << 20, transcendentals=0)


def limit(megabytes):
    return pltpu.CompilerParams(vmem_limit_bytes=megabytes << 20)


def held(piece, share, *tokens):
    return pl.pallas_call(
        lambda *refs: None,
        out_shape=jax.ShapeDtypeStruct(piece.shape, piece.dtype),
        in_specs=[spec(pl.ANY)] * (1 + len(tokens)),
        out_specs=spec(pl.ANY),
        input_output_aliases={0: 0},
        compiler_params=limit(1),
        cost_estimate=cost(share),
    )(piece, *tokens)


def body(primaries, data, aperture):
    width = data.shape[3]
    line = lax.axis_size("src") == 4
    windows = (line_window if line else hop_window)(data)
    panels, far_panel = gather_panels(primaries, windows[0][-2][0])
    half = len(panels)
    late = len(windows[0]) - 1
    late_pieces = [piece[at : at + 1] for piece, at in (window[late] for window in windows)]
    early = [{k: piece for k, piece in enumerate(window) if k != late} for window in windows]
    vmem, anywhere = spec(pltpu.VMEM), spec(pl.ANY)
    window = jax.ShapeDtypeStruct((len(windows[0]), BLK, 2 * width), jnp.bfloat16)
    total = jax.ShapeDtypeStruct((2 * BLK, BLK), jnp.float32)
    part = jax.ShapeDtypeStruct((2, BLK, width), jnp.float32)

    pieces = [piece for window_pieces in early for piece, _ in window_pieces.values()]
    first, last, first_sum, last_sum, first_part, last_part = pl.pallas_call(
        functools.partial(kernel_a, [{k: at for k, (_, at) in pieces.items()} for pieces in early], late),
        out_shape=[window] * 2 + [total] * 2 + [part] * 2,
        in_specs=[vmem] * (2 + len(pieces)),
        out_specs=[vmem] * 6,
        compiler_params=limit(16),
        cost_estimate=cost(0.1),
    )(aperture, primaries, *pieces)

    far_panel = held(far_panel, 12, first_part)
    handed_on = hand_on(far_panel, first_part)
    first, two, first_part, last_part = pl.pallas_call(
        functools.partial(kernel_b, late),
        out_shape=[window, jax.ShapeDtypeStruct((2 * BLK, 2 * BLK), jnp.bfloat16), part, part],
        in_specs=[vmem] * (8 + half),
        out_specs=[vmem] * 4,
        input_output_aliases={2: 0, 6: 2, 7: 3},
        compiler_params=limit(16),
        cost_estimate=cost(0.1),
    )(aperture, late_pieces[0], first, last, first_sum, last_sum, first_part, last_part, *panels[1:], far_panel)

    return pl.pallas_call(
        functools.partial(last_kernel, half + 1, late),
        out_shape=[jax.ShapeDtypeStruct((2, 2, BLK, width), jnp.float32), window],
        in_specs=[vmem] + [vmem] * (6 + len(handed_on)),
        out_specs=[anywhere, vmem],
        scratch_shapes=[pltpu.VMEM((2, 2, BLK, width), jnp.float32), pltpu.SemaphoreType.DMA((2, 2, PIECES))],
        input_output_aliases={3: 1},
        compiler_params=limit(16),
        cost_estimate=cost(1),
    )(aperture, held(late_pieces[1], 12, two), first, last, two, first_part, last_part, *handed_on)[0]


def solution(mesh):
    placed = (P("freq", None, "src", "rcv"), P("freq", None, "src", "rcv"), P())
    return jax.shard_map(
        body, mesh=mesh, in_specs=placed, out_specs=P("freq", None, "src", "rcv"), check_vma=False
    )
```

```python
import functools

import jax
import jax.numpy as jnp
from jax import lax
from jax.experimental import pallas as pl
from jax.experimental.pallas import tpu as pltpu
from jax.sharding import PartitionSpec as P

BLK = 256
APER = 12
HW = 6
PIECES = 1


def after(value, *earlier):
    return lax.optimization_barrier((value, *earlier))[0]


def from_behind(x, axis, by):
    peers = lax.axis_size(axis)
    pairs = [(i, i + by) for i in range(peers) if 0 <= i + by < peers]
    return lax.ppermute(x, axis, pairs)


def swap(x, axis, bit):
    peers = lax.axis_size(axis)
    return lax.ppermute(x, axis, [(i, i ^ bit) for i in range(peers)])


def at_end():
    return (lax.axis_index("src") + 1) % lax.axis_size("src") < 2


def line_window(data):
    near_pairs = [(0, 1), (1, 0), (2, 3), (3, 2)]
    near = lax.ppermute(data, "src", near_pairs)
    far = lax.ppermute(data, "src", [(0, 2), (1, 3), (2, 0), (3, 1)])
    near, far = lax.optimization_barrier((near, far))
    far = held(far, 5)
    windows = []
    for v in range(data.shape[0]):
        across = lax.ppermute(far[v : v + 1], "src", near_pairs)
        windows.append([(data, v), (near, v), (far, v), (across, 0)])
    return windows


def hop_window(data):
    reach = min(HW, lax.axis_size("src") - 1)
    window = {0: data}
    for hop in range(1, reach + 1):
        window[-hop] = from_behind(window[1 - hop], "src", 1)
        window[hop] = from_behind(window[hop - 1], "src", -1)
    return [[(window[distance], v) for distance in range(-reach, reach + 1)] for v in range(data.shape[0])]


def gather_panels(primaries, first):
    bit = lax.axis_size("rcv") // 2
    panels = [after(primaries, first)]
    for lower in range(1, bit):
        panels.append(swap(panels[lower & (lower - 1)], "rcv", lower & -lower))
    return panels, swap(primaries, "rcv", bit)


def hand_on(panel, token):
    bit = lax.axis_size("rcv") // 2
    panels = [after(panel, token)]
    for lower in range(1, bit):
        panels.append(swap(panels[lower & (lower - 1)], "rcv", lower & -lower))
    return panels[1:]


def fill_window(window, pieces):
    width = window.shape[-1] // 2
    for k, piece in pieces.items():
        window[k, :, :width] = piece[0]
        window[k, :, width:] = piece[1]


def slot_entries(aperture_ref, m, per_shard, depth):
    src = lax.axis_index("src")
    first_slot = lax.bitwise_xor(lax.axis_index("rcv"), m) * per_shard
    blocks = aperture_ref[...]
    at_row = lax.broadcasted_iota(jnp.int32, blocks.shape, 0) == src
    at_slot = lax.broadcasted_iota(jnp.int32, blocks.shape, 1)
    wanted = [jnp.sum(jnp.where(at_row & (at_slot == first_slot + q), blocks, 0)) for q in range(per_shard)]
    if lax.axis_size("src") == 4:
        return [lax.bitwise_xor(src, block) for block in wanted]
    return [block - src + depth // 2 for block in wanted]


def times(values, blocks):
    both = jnp.dot(values, blocks, preferred_element_type=jnp.float32)
    rows, width = both.shape[0] // 2, both.shape[1] // 2
    return both[:rows, :width] - both[rows:, width:], both[:rows, width:] + both[rows:, :width]


def rows_of(panel):
    return panel[...].reshape(2 * panel.shape[1], panel.shape[2])


def product(window, aperture_ref, panels, late_in_two=None, late=None):
    blocks = []
    for m, panel in panels.items():
        entries = slot_entries(aperture_ref, m, panel.shape[-1] // BLK, window.shape[0])
        blocks += [window[k] for k in entries]
    values = [rows_of(panel) for panel in panels.values()]
    if late_in_two is not None:
        values.append(late_in_two)
        blocks += [window[late]] * 2
    return times(jnp.concatenate(values, axis=1), jnp.concatenate(blocks, axis=0))


def sum_of_late(aperture_ref, panels, late, depth):
    total = None
    for m, panel in panels.items():
        values = rows_of(panel)
        for q, k in enumerate(slot_entries(aperture_ref, m, panel.shape[-1] // BLK, depth)):
            term = values[:, q * BLK : (q + 1) * BLK].astype(jnp.float32) * jnp.where(k == late, 1.0, 0.0)
            total = term if total is None else total + term
    return total


def in_two(total):
    high = total.astype(jnp.bfloat16)
    low = (total - high.astype(jnp.float32)).astype(jnp.bfloat16)
    return jnp.concatenate([high, low], axis=1)


def kernel_a(ats, late, aperture_ref, own_ref, *refs):
    piece_refs = list(refs[:-6])
    windows, sums, parts = refs[-6:-4], refs[-4:-2], refs[-2:]
    for v, (window, at) in enumerate(zip(windows, ats)):
        window[late] = jnp.zeros(window.shape[1:], window.dtype)
        fill_window(window, {k: piece_refs.pop(0).at[index] for k, index in at.items()})
        panels = {0: own_ref.at[v]}
        parts[v][0], parts[v][1] = product(window, aperture_ref, panels)
        sums[v][...] = sum_of_late(aperture_ref, panels, late, window.shape[0])


def kernel_b(late, aperture_ref, last_window, last_sum, last_in, *refs):
    *panel_refs, two, last_part = refs
    panels = {1 + m: ref.at[1] for m, ref in enumerate(panel_refs)}
    real, imag = product(last_window, aperture_ref, panels)
    last_part[0] = last_in[0] + real
    last_part[1] = last_in[1] + imag
    two[...] = in_two(last_sum[...] + sum_of_late(aperture_ref, panels, late, last_window.shape[0]))


def kernel_c(late, aperture_ref, late_ref, _, first_sum, first_in, *refs):
    *panel_refs, window, first_part = refs
    fill_window(window, {late: late_ref.at[0]})
    panels = {1 + m: ref.at[0] for m, ref in enumerate(panel_refs)}
    real, imag = product(window, aperture_ref, panels, in_two(first_sum[...]), late)
    first_part[0] = first_in[0] + real
    first_part[1] = first_in[1] + imag


def last_kernel(far_half, late, aperture_ref, late_ref, first_window, _, two, first_part, last_part, *refs):
    *panel_refs, out_ref, window, result, sems = refs

    def finish(v, part, real, imag):
        copies = []
        for p, value in enumerate((real, imag)):
            result[v, p] = part[p] + value
            for chunk in range(PIECES):
                rows = pl.ds(chunk * (BLK // PIECES), BLK // PIECES)
                copies.append(
                    pltpu.make_async_copy(result.at[v, p, rows], out_ref.at[v, p, rows], sems.at[v, p, chunk])
                )
                copies[-1].start()
        return copies

    panels = [{far_half + m: ref.at[v] for m, ref in enumerate(panel_refs)} for v in range(2)]
    copies = finish(0, first_part, *product(first_window, aperture_ref, panels[0]))
    fill_window(window, {late: late_ref.at[0]})
    copies += finish(1, last_part, *product(window, aperture_ref, panels[1], two[...], late))
    for copy in copies:
        copy.wait()


def spec(space):
    return pl.BlockSpec(memory_space=space)


def cost(share):
    return pl.CostEstimate(flops=int(share * (8 * BLK * BLK * APER * BLK)), bytes_accessed=1 << 20, transcendentals=0)


def limit(megabytes):
    return pltpu.CompilerParams(vmem_limit_bytes=megabytes << 20)


def held(piece, share, *tokens):
    return pl.pallas_call(
        lambda *refs: None,
        out_shape=jax.ShapeDtypeStruct(piece.shape, piece.dtype),
        in_specs=[spec(pl.ANY)] * (1 + len(tokens)),
        out_specs=spec(pl.ANY),
        input_output_aliases={0: 0},
        compiler_params=limit(1),
        cost_estimate=cost(share),
    )(piece, *tokens)


def body(primaries, data, aperture):
    width = data.shape[3]
    line = lax.axis_size("src") == 4
    windows = (line_window if line else hop_window)(data)
    panels, far_panel = gather_panels(primaries, windows[0][-2][0])
    half = len(panels)
    late = len(windows[0]) - 1
    late_pieces = [piece[at : at + 1] for piece, at in (window[late] for window in windows)]
    early = [{k: piece for k, piece in enumerate(window) if k != late} for window in windows]
    vmem, anywhere = spec(pltpu.VMEM), spec(pl.ANY)
    window = jax.ShapeDtypeStruct((len(windows[0]), BLK, 2 * width), jnp.bfloat16)
    total = jax.ShapeDtypeStruct((2 * BLK, BLK), jnp.float32)
    part = jax.ShapeDtypeStruct((2, BLK, width), jnp.float32)

    pieces = [piece for window_pieces in early for piece, _ in window_pieces.values()]
    first, last, first_sum, last_sum, first_part, last_part = pl.pallas_call(
        functools.partial(kernel_a, [{k: at for k, (_, at) in pieces.items()} for pieces in early], late),
        out_shape=[window] * 2 + [total] * 2 + [part] * 2,
        in_specs=[vmem] * (2 + len(pieces)),
        out_specs=[vmem] * 6,
        compiler_params=limit(16),
        cost_estimate=cost(0.1),
    )(aperture, primaries, *pieces)

    far_panel = held(far_panel, 12, first_part)
    handed_on = hand_on(far_panel, first_part)
    two, last_part = pl.pallas_call(
        functools.partial(kernel_b, late),
        out_shape=[jax.ShapeDtypeStruct((2 * BLK, 2 * BLK), jnp.bfloat16), part],
        in_specs=[vmem] * (4 + half),
        out_specs=[vmem] * 2,
        input_output_aliases={3: 1},
        compiler_params=limit(16),
        cost_estimate=cost(0.05),
    )(aperture, last, last_sum, last_part, *panels[1:], far_panel)

    first, first_part = pl.pallas_call(
        functools.partial(kernel_c, late),
        out_shape=[window, part],
        in_specs=[vmem] * (5 + half),
        out_specs=[vmem] * 2,
        input_output_aliases={2: 0, 4: 1},
        compiler_params=limit(16),
        cost_estimate=cost(0.05),
    )(aperture, after(late_pieces[0], two), first, first_sum, first_part, *panels[1:], far_panel)

    return pl.pallas_call(
        functools.partial(last_kernel, half + 1, late),
        out_shape=[jax.ShapeDtypeStruct((2, 2, BLK, width), jnp.float32), window],
        in_specs=[vmem] + [vmem] * (6 + len(handed_on)),
        out_specs=[anywhere, vmem],
        scratch_shapes=[pltpu.VMEM((2, 2, BLK, width), jnp.float32), pltpu.SemaphoreType.DMA((2, 2, PIECES))],
        input_output_aliases={3: 1},
        compiler_params=limit(16),
        cost_estimate=cost(1),
    )(aperture, held(late_pieces[1], 12, first_part), first, last, two, first_part, last_part, *handed_on)[0]


def solution(mesh):
    placed = (P("freq", None, "src", "rcv"), P("freq", None, "src", "rcv"), P())
    return jax.shard_map(
        body, mesh=mesh, in_specs=placed, out_specs=P("freq", None, "src", "rcv"), check_vma=False
    )
```

```python
import functools

import jax
import jax.numpy as jnp
from jax import lax
from jax.experimental import pallas as pl
from jax.experimental.pallas import tpu as pltpu
from jax.sharding import PartitionSpec as P

BLK = 256
APER = 12
HW = 6
PIECES = 1


def after(value, *earlier):
    return lax.optimization_barrier((value, *earlier))[0]


def from_behind(x, axis, by):
    peers = lax.axis_size(axis)
    pairs = [(i, i + by) for i in range(peers) if 0 <= i + by < peers]
    return lax.ppermute(x, axis, pairs)


def swap(x, axis, bit):
    peers = lax.axis_size(axis)
    return lax.ppermute(x, axis, [(i, i ^ bit) for i in range(peers)])


def at_end():
    return (lax.axis_index("src") + 1) % lax.axis_size("src") < 2


def line_window(data):
    near_pairs = [(0, 1), (1, 0), (2, 3), (3, 2)]
    near = lax.ppermute(data, "src", near_pairs)
    far = lax.ppermute(data, "src", [(0, 2), (1, 3), (2, 0), (3, 1)])
    near, far = lax.optimization_barrier((near, far))
    far = held(far, 5)
    windows = []
    for v in range(data.shape[0]):
        across = lax.ppermute(far[v : v + 1], "src", near_pairs)
        windows.append([(data, v), (near, v), (far, v), (across, 0)])
    return windows


def hop_window(data):
    reach = min(HW, lax.axis_size("src") - 1)
    window = {0: data}
    for hop in range(1, reach + 1):
        window[-hop] = from_behind(window[1 - hop], "src", 1)
        window[hop] = from_behind(window[hop - 1], "src", -1)
    return [[(window[distance], v) for distance in range(-reach, reach + 1)] for v in range(data.shape[0])]


def gather_panels(primaries):
    bit = lax.axis_size("rcv") // 2
    panels = [primaries]
    for lower in range(1, bit):
        panels.append(swap(panels[lower & (lower - 1)], "rcv", lower & -lower))
    return panels, swap(primaries, "rcv", bit)


def hand_on(panel, token):
    bit = lax.axis_size("rcv") // 2
    panels = [after(panel, token)]
    for lower in range(1, bit):
        panels.append(swap(panels[lower & (lower - 1)], "rcv", lower & -lower))
    return panels[1:]


def fill_window(window, pieces):
    width = window.shape[-1] // 2
    for k, piece in pieces.items():
        window[k, :, :width] = piece[0]
        window[k, :, width:] = piece[1]


def slot_entries(aperture_ref, m, per_shard, depth):
    src = lax.axis_index("src")
    first_slot = lax.bitwise_xor(lax.axis_index("rcv"), m) * per_shard
    blocks = aperture_ref[...]
    at_row = lax.broadcasted_iota(jnp.int32, blocks.shape, 0) == src
    at_slot = lax.broadcasted_iota(jnp.int32, blocks.shape, 1)
    wanted = [jnp.sum(jnp.where(at_row & (at_slot == first_slot + q), blocks, 0)) for q in range(per_shard)]
    if lax.axis_size("src") == 4:
        return [lax.bitwise_xor(src, block) for block in wanted]
    return [block - src + depth // 2 for block in wanted]


def times(values, blocks):
    both = jnp.dot(values, blocks, preferred_element_type=jnp.float32)
    rows, width = both.shape[0] // 2, both.shape[1] // 2
    return both[:rows, :width] - both[rows:, width:], both[:rows, width:] + both[rows:, :width]


def rows_of(panel):
    return panel[...].reshape(2 * panel.shape[1], panel.shape[2])


def product(window, aperture_ref, panels, late_in_two=None, late=None):
    blocks = []
    for m, panel in panels.items():
        entries = slot_entries(aperture_ref, m, panel.shape[-1] // BLK, window.shape[0])
        blocks += [window[k] for k in entries]
    values = [rows_of(panel) for panel in panels.values()]
    if late_in_two is not None:
        values.append(late_in_two)
        blocks += [window[late]] * 2
    return times(jnp.concatenate(values, axis=1), jnp.concatenate(blocks, axis=0))


def sum_of_late(aperture_ref, panels, late, depth):
    total = None
    for m, panel in panels.items():
        values = rows_of(panel)
        for q, k in enumerate(slot_entries(aperture_ref, m, panel.shape[-1] // BLK, depth)):
            term = values[:, q * BLK : (q + 1) * BLK].astype(jnp.float32) * jnp.where(k == late, 1.0, 0.0)
            total = term if total is None else total + term
    return total


def in_two(total):
    high = total.astype(jnp.bfloat16)
    low = (total - high.astype(jnp.float32)).astype(jnp.bfloat16)
    return jnp.concatenate([high, low], axis=1)


def kernel_a(ats, late, aperture_ref, own_ref, *refs):
    piece_refs = list(refs[:-6])
    windows, sums, parts = refs[-6:-4], refs[-4:-2], refs[-2:]
    for v, (window, at) in enumerate(zip(windows, ats)):
        window[late] = jnp.zeros(window.shape[1:], window.dtype)
        fill_window(window, {k: piece_refs.pop(0).at[index] for k, index in at.items()})
        panels = {0: own_ref.at[v]}
        parts[v][0], parts[v][1] = product(window, aperture_ref, panels)
        sums[v][...] = sum_of_late(aperture_ref, panels, late, window.shape[0])


def kernel_b(late, aperture_ref, last_window, last_sum, last_in, *refs):
    *panel_refs, two, last_part = refs
    panels = {1 + m: ref.at[1] for m, ref in enumerate(panel_refs)}
    real, imag = product(last_window, aperture_ref, panels)
    last_part[0] = last_in[0] + real
    last_part[1] = last_in[1] + imag
    two[...] = in_two(last_sum[...] + sum_of_late(aperture_ref, panels, late, last_window.shape[0]))


def kernel_c(late, aperture_ref, late_ref, _, first_sum, first_in, *refs):
    *panel_refs, window, first_part = refs
    fill_window(window, {late: late_ref.at[0]})
    panels = {1 + m: ref.at[0] for m, ref in enumerate(panel_refs)}
    real, imag = product(window, aperture_ref, panels, in_two(first_sum[...]), late)
    first_part[0] = first_in[0] + real
    first_part[1] = first_in[1] + imag


def last_kernel(far_half, late, aperture_ref, late_ref, first_window, _, two, first_part, last_part, *refs):
    *panel_refs, out_ref, window, result, sems = refs

    def finish(v, part, real, imag):
        copies = []
        for p, value in enumerate((real, imag)):
            result[v, p] = part[p] + value
            for chunk in range(PIECES):
                rows = pl.ds(chunk * (BLK // PIECES), BLK // PIECES)
                copies.append(
                    pltpu.make_async_copy(result.at[v, p, rows], out_ref.at[v, p, rows], sems.at[v, p, chunk])
                )
                copies[-1].start()
        return copies

    panels = [{far_half + m: ref.at[v] for m, ref in enumerate(panel_refs)} for v in range(2)]
    copies = finish(0, first_part, *product(first_window, aperture_ref, panels[0]))
    fill_window(window, {late: late_ref.at[0]})
    copies += finish(1, last_part, *product(window, aperture_ref, panels[1], two[...], late))
    for copy in copies:
        copy.wait()


def spec(space):
    return pl.BlockSpec(memory_space=space)


def cost(share):
    return pl.CostEstimate(flops=int(share * (8 * BLK * BLK * APER * BLK)), bytes_accessed=1 << 20, transcendentals=0)


def limit(megabytes):
    return pltpu.CompilerParams(vmem_limit_bytes=megabytes << 20)


def held(piece, share, *tokens):
    return pl.pallas_call(
        lambda *refs: None,
        out_shape=jax.ShapeDtypeStruct(piece.shape, piece.dtype),
        in_specs=[spec(pl.ANY)] * (1 + len(tokens)),
        out_specs=spec(pl.ANY),
        input_output_aliases={0: 0},
        compiler_params=limit(1),
        cost_estimate=cost(share),
    )(piece, *tokens)


def body(primaries, data, aperture):
    width = data.shape[3]
    line = lax.axis_size("src") == 4
    windows = (line_window if line else hop_window)(data)
    panels, far_panel = gather_panels(primaries)
    half = len(panels)
    late = len(windows[0]) - 1
    late_pieces = [piece[at : at + 1] for piece, at in (window[late] for window in windows)]
    early = [{k: piece for k, piece in enumerate(window) if k != late} for window in windows]
    vmem, anywhere = spec(pltpu.VMEM), spec(pl.ANY)
    window = jax.ShapeDtypeStruct((len(windows[0]), BLK, 2 * width), jnp.bfloat16)
    total = jax.ShapeDtypeStruct((2 * BLK, BLK), jnp.float32)
    part = jax.ShapeDtypeStruct((2, BLK, width), jnp.float32)

    pieces = [piece for window_pieces in early for piece, _ in window_pieces.values()]
    first, last, first_sum, last_sum, first_part, last_part = pl.pallas_call(
        functools.partial(kernel_a, [{k: at for k, (_, at) in pieces.items()} for pieces in early], late),
        out_shape=[window] * 2 + [total] * 2 + [part] * 2,
        in_specs=[vmem] * (2 + len(pieces)),
        out_specs=[vmem] * 6,
        compiler_params=limit(16),
        cost_estimate=cost(0.1),
    )(aperture, primaries, *pieces)

    far_panel = held(far_panel, 12, first_part)
    handed_on = hand_on(far_panel, first_part)
    two, last_part = pl.pallas_call(
        functools.partial(kernel_b, late),
        out_shape=[jax.ShapeDtypeStruct((2 * BLK, 2 * BLK), jnp.bfloat16), part],
        in_specs=[vmem] * (4 + half),
        out_specs=[vmem] * 2,
        input_output_aliases={3: 1},
        compiler_params=limit(16),
        cost_estimate=cost(0.05),
    )(aperture, last, last_sum, last_part, *panels[1:], far_panel)

    first, first_part = pl.pallas_call(
        functools.partial(kernel_c, late),
        out_shape=[window, part],
        in_specs=[vmem] * (5 + half),
        out_specs=[vmem] * 2,
        input_output_aliases={2: 0, 4: 1},
        compiler_params=limit(16),
        cost_estimate=cost(0.05),
    )(aperture, after(late_pieces[0], two), first, first_sum, first_part, *panels[1:], far_panel)

    return pl.pallas_call(
        functools.partial(last_kernel, half + 1, late),
        out_shape=[jax.ShapeDtypeStruct((2, 2, BLK, width), jnp.float32), window],
        in_specs=[vmem] + [vmem] * (6 + len(handed_on)),
        out_specs=[anywhere, vmem],
        scratch_shapes=[pltpu.VMEM((2, 2, BLK, width), jnp.float32), pltpu.SemaphoreType.DMA((2, 2, PIECES))],
        input_output_aliases={3: 1},
        compiler_params=limit(16),
        cost_estimate=cost(1),
    )(aperture, held(late_pieces[1], 12, first_part), first, last, two, first_part, last_part, *handed_on)[0]


def solution(mesh):
    placed = (P("freq", None, "src", "rcv"), P("freq", None, "src", "rcv"), P())
    return jax.shard_map(
        body, mesh=mesh, in_specs=placed, out_specs=P("freq", None, "src", "rcv"), check_vma=False
    )
```

```python
import functools

import jax
import jax.numpy as jnp
from jax import lax
from jax.experimental import pallas as pl
from jax.experimental.pallas import tpu as pltpu
from jax.sharding import PartitionSpec as P

BLK = 256
APER = 12
HW = 6
PIECES = 1


def after(value, *earlier):
    return lax.optimization_barrier((value, *earlier))[0]


def from_behind(x, axis, by):
    peers = lax.axis_size(axis)
    pairs = [(i, i + by) for i in range(peers) if 0 <= i + by < peers]
    return lax.ppermute(x, axis, pairs)


def swap(x, axis, bit):
    peers = lax.axis_size(axis)
    return lax.ppermute(x, axis, [(i, i ^ bit) for i in range(peers)])


def at_end():
    return (lax.axis_index("src") + 1) % lax.axis_size("src") < 2


def line_window(data):
    near_pairs = [(0, 1), (1, 0), (2, 3), (3, 2)]
    far = held(lax.ppermute(data, "src", [(0, 3), (1, 2), (2, 1), (3, 0)]), 5)
    near = lax.ppermute(data, "src", near_pairs)
    windows = []
    for v in range(data.shape[0]):
        across = lax.ppermute(far[v : v + 1], "src", near_pairs)
        windows.append([(data, v), (near, v), (across, 0), (far, v)])
    return windows


def hop_window(data):
    reach = min(HW, lax.axis_size("src") - 1)
    window = {0: data}
    for hop in range(1, reach + 1):
        window[-hop] = from_behind(window[1 - hop], "src", 1)
        window[hop] = from_behind(window[hop - 1], "src", -1)
    return [[(window[distance], v) for distance in range(-reach, reach + 1)] for v in range(data.shape[0])]


def gather_panels(primaries, first):
    bit = lax.axis_size("rcv") // 2
    panels = [after(primaries, first)]
    for lower in range(1, bit):
        panels.append(swap(panels[lower & (lower - 1)], "rcv", lower & -lower))
    return panels, swap(primaries, "rcv", bit)


def hand_on(panel, token):
    bit = lax.axis_size("rcv") // 2
    panels = [after(panel, token)]
    for lower in range(1, bit):
        panels.append(swap(panels[lower & (lower - 1)], "rcv", lower & -lower))
    return panels[1:]


def fill_window(window, pieces):
    width = window.shape[-1] // 2
    for k, piece in pieces.items():
        window[k, :, :width] = piece[0]
        window[k, :, width:] = piece[1]


def slot_entries(aperture_ref, m, per_shard, depth):
    src = lax.axis_index("src")
    first_slot = lax.bitwise_xor(lax.axis_index("rcv"), m) * per_shard
    blocks = aperture_ref[...]
    at_row = lax.broadcasted_iota(jnp.int32, blocks.shape, 0) == src
    at_slot = lax.broadcasted_iota(jnp.int32, blocks.shape, 1)
    wanted = [jnp.sum(jnp.where(at_row & (at_slot == first_slot + q), blocks, 0)) for q in range(per_shard)]
    if lax.axis_size("src") == 4:
        return [lax.bitwise_xor(src, block) for block in wanted]
    return [block - src + depth // 2 for block in wanted]


def times(values, blocks):
    both = jnp.dot(values, blocks, preferred_element_type=jnp.float32)
    rows, width = both.shape[0] // 2, both.shape[1] // 2
    return both[:rows, :width] - both[rows:, width:], both[:rows, width:] + both[rows:, :width]


def rows_of(panel):
    return panel[...].reshape(2 * panel.shape[1], panel.shape[2])


def product(window, aperture_ref, panels, late_in_two=None, late=None):
    blocks = []
    for m, panel in panels.items():
        entries = slot_entries(aperture_ref, m, panel.shape[-1] // BLK, window.shape[0])
        blocks += [window[k] for k in entries]
    values = [rows_of(panel) for panel in panels.values()]
    if late_in_two is not None:
        values.append(late_in_two)
        blocks += [window[late]] * 2
    return times(jnp.concatenate(values, axis=1), jnp.concatenate(blocks, axis=0))


def sum_of_late(aperture_ref, panels, late, depth):
    total = None
    for m, panel in panels.items():
        values = rows_of(panel)
        for q, k in enumerate(slot_entries(aperture_ref, m, panel.shape[-1] // BLK, depth)):
            term = values[:, q * BLK : (q + 1) * BLK].astype(jnp.float32) * jnp.where(k == late, 1.0, 0.0)
            total = term if total is None else total + term
    return total


def in_two(total):
    high = total.astype(jnp.bfloat16)
    low = (total - high.astype(jnp.float32)).astype(jnp.bfloat16)
    return jnp.concatenate([high, low], axis=1)


def kernel_a(ats, late, aperture_ref, own_ref, *refs):
    piece_refs = list(refs[:-6])
    windows, sums, parts = refs[-6:-4], refs[-4:-2], refs[-2:]
    for v, (window, at) in enumerate(zip(windows, ats)):
        window[late] = jnp.zeros(window.shape[1:], window.dtype)
        fill_window(window, {k: piece_refs.pop(0).at[index] for k, index in at.items()})
        panels = {0: own_ref.at[v]}
        parts[v][0], parts[v][1] = product(window, aperture_ref, panels)
        sums[v][...] = sum_of_late(aperture_ref, panels, late, window.shape[0])


def kernel_b(late, aperture_ref, late_ref, _, last_window, first_sum, last_sum, first_in, last_in, *refs):
    *panel_refs, window, two, first_part, last_part = refs
    fill_window(window, {late: late_ref.at[0]})
    panels = [{1 + m: ref.at[v] for m, ref in enumerate(panel_refs)} for v in range(2)]
    real, imag = product(window, aperture_ref, panels[0], in_two(first_sum[...]), late)
    first_part[0] = first_in[0] + real
    first_part[1] = first_in[1] + imag
    real, imag = product(last_window, aperture_ref, panels[1])
    last_part[0] = last_in[0] + real
    last_part[1] = last_in[1] + imag
    two[...] = in_two(last_sum[...] + sum_of_late(aperture_ref, panels[1], late, last_window.shape[0]))


def last_kernel(far_half, late, aperture_ref, late_ref, first_window, _, two, first_part, last_part, *refs):
    *panel_refs, out_ref, window, result, sems = refs

    def finish(v, part, real, imag):
        copies = []
        for p, value in enumerate((real, imag)):
            result[v, p] = part[p] + value
            for chunk in range(PIECES):
                rows = pl.ds(chunk * (BLK // PIECES), BLK // PIECES)
                copies.append(
                    pltpu.make_async_copy(result.at[v, p, rows], out_ref.at[v, p, rows], sems.at[v, p, chunk])
                )
                copies[-1].start()
        return copies

    panels = [{far_half + m: ref.at[v] for m, ref in enumerate(panel_refs)} for v in range(2)]
    fill_window(window, {late: late_ref.at[0]})
    copies = finish(1, last_part, *product(window, aperture_ref, panels[1], two[...], late))
    copies += finish(0, first_part, *product(first_window, aperture_ref, panels[0]))
    for copy in copies:
        copy.wait()


def spec(space):
    return pl.BlockSpec(memory_space=space)


def cost(share):
    return pl.CostEstimate(flops=int(share * (8 * BLK * BLK * APER * BLK)), bytes_accessed=1 << 20, transcendentals=0)


def limit(megabytes):
    return pltpu.CompilerParams(vmem_limit_bytes=megabytes << 20)


def held(piece, share, *tokens):
    return pl.pallas_call(
        lambda *refs: None,
        out_shape=jax.ShapeDtypeStruct(piece.shape, piece.dtype),
        in_specs=[spec(pl.ANY)] * (1 + len(tokens)),
        out_specs=spec(pl.ANY),
        input_output_aliases={0: 0},
        compiler_params=limit(1),
        cost_estimate=cost(share),
    )(piece, *tokens)


def body(primaries, data, aperture):
    width = data.shape[3]
    line = lax.axis_size("src") == 4
    windows = (line_window if line else hop_window)(data)
    panels, far_panel = gather_panels(primaries, windows[0][-1][0])
    half = len(panels)
    late = 2 if line else len(windows[0]) - 1
    late_pieces = [piece[at : at + 1] for piece, at in (window[late] for window in windows)]
    early = [{k: piece for k, piece in enumerate(window) if k != late} for window in windows]
    vmem, anywhere = spec(pltpu.VMEM), spec(pl.ANY)
    window = jax.ShapeDtypeStruct((len(windows[0]), BLK, 2 * width), jnp.bfloat16)
    total = jax.ShapeDtypeStruct((2 * BLK, BLK), jnp.float32)
    part = jax.ShapeDtypeStruct((2, BLK, width), jnp.float32)

    pieces = [piece for window_pieces in early for piece, _ in window_pieces.values()]
    first, last, first_sum, last_sum, first_part, last_part = pl.pallas_call(
        functools.partial(kernel_a, [{k: at for k, (_, at) in pieces.items()} for pieces in early], late),
        out_shape=[window] * 2 + [total] * 2 + [part] * 2,
        in_specs=[vmem] * (2 + len(pieces)),
        out_specs=[vmem] * 6,
        compiler_params=limit(16),
        cost_estimate=cost(0.1),
    )(aperture, primaries, *pieces)

    far_panel = held(far_panel, 12, first_part)
    handed_on = hand_on(far_panel, first_part)
    first, two, first_part, last_part = pl.pallas_call(
        functools.partial(kernel_b, late),
        out_shape=[window, jax.ShapeDtypeStruct((2 * BLK, 2 * BLK), jnp.bfloat16), part, part],
        in_specs=[vmem] * (8 + half),
        out_specs=[vmem] * 4,
        input_output_aliases={2: 0, 6: 2, 7: 3},
        compiler_params=limit(16),
        cost_estimate=cost(0.1),
    )(aperture, late_pieces[0], first, last, first_sum, last_sum, first_part, last_part, *panels[1:], far_panel)

    return pl.pallas_call(
        functools.partial(last_kernel, half + 1, late),
        out_shape=[jax.ShapeDtypeStruct((2, 2, BLK, width), jnp.float32), window],
        in_specs=[vmem] + [vmem] * (6 + len(handed_on)),
        out_specs=[anywhere, vmem],
        scratch_shapes=[pltpu.VMEM((2, 2, BLK, width), jnp.float32), pltpu.SemaphoreType.DMA((2, 2, PIECES))],
        input_output_aliases={3: 1},
        compiler_params=limit(16),
        cost_estimate=cost(1),
    )(aperture, held(late_pieces[1], 12, two), first, last, two, first_part, last_part, *handed_on)[0]


def solution(mesh):
    placed = (P("freq", None, "src", "rcv"), P("freq", None, "src", "rcv"), P())
    return jax.shard_map(
        body, mesh=mesh, in_specs=placed, out_specs=P("freq", None, "src", "rcv"), check_vma=False
    )
```

```python
import functools

import jax
import jax.numpy as jnp
from jax import lax
from jax.experimental import pallas as pl
from jax.experimental.pallas import tpu as pltpu
from jax.sharding import PartitionSpec as P

BLK = 256
APER = 12
HW = 6
PIECES = 1


def after(value, *earlier):
    return lax.optimization_barrier((value, *earlier))[0]


def from_behind(x, axis, by):
    peers = lax.axis_size(axis)
    pairs = [(i, i + by) for i in range(peers) if 0 <= i + by < peers]
    return lax.ppermute(x, axis, pairs)


def swap(x, axis, bit):
    peers = lax.axis_size(axis)
    return lax.ppermute(x, axis, [(i, i ^ bit) for i in range(peers)])


def at_end():
    return (lax.axis_index("src") + 1) % lax.axis_size("src") < 2


def line_window(data):
    near_pairs = [(0, 1), (1, 0), (2, 3), (3, 2)]
    far = held(lax.ppermute(data, "src", [(0, 3), (1, 2), (2, 1), (3, 0)]), 5)
    near = lax.ppermute(data, "src", near_pairs)
    windows = []
    for v in range(data.shape[0]):
        across = lax.ppermute(far[v : v + 1], "src", near_pairs)
        windows.append([(data, v), (near, v), (across, 0), (far, v)])
    return windows


def hop_window(data):
    reach = min(HW, lax.axis_size("src") - 1)
    window = {0: data}
    for hop in range(1, reach + 1):
        window[-hop] = from_behind(window[1 - hop], "src", 1)
        window[hop] = from_behind(window[hop - 1], "src", -1)
    return [[(window[distance], v) for distance in range(-reach, reach + 1)] for v in range(data.shape[0])]


def gather_panels(primaries, first):
    bit = lax.axis_size("rcv") // 2
    panels = [after(primaries, first)]
    for lower in range(1, bit):
        panels.append(swap(panels[lower & (lower - 1)], "rcv", lower & -lower))
    return panels, swap(primaries, "rcv", bit)


def hand_on(panel, token):
    bit = lax.axis_size("rcv") // 2
    panels = [after(panel, token)]
    for lower in range(1, bit):
        panels.append(swap(panels[lower & (lower - 1)], "rcv", lower & -lower))
    return panels[1:]


def fill_window(window, pieces):
    width = window.shape[-1] // 2
    for k, piece in pieces.items():
        window[k, :, :width] = piece[0]
        window[k, :, width:] = piece[1]


def slot_entries(aperture_ref, m, per_shard, depth):
    src = lax.axis_index("src")
    first_slot = lax.bitwise_xor(lax.axis_index("rcv"), m) * per_shard
    blocks = aperture_ref[...]
    at_row = lax.broadcasted_iota(jnp.int32, blocks.shape, 0) == src
    at_slot = lax.broadcasted_iota(jnp.int32, blocks.shape, 1)
    wanted = [jnp.sum(jnp.where(at_row & (at_slot == first_slot + q), blocks, 0)) for q in range(per_shard)]
    if lax.axis_size("src") == 4:
        return [lax.bitwise_xor(src, block) for block in wanted]
    return [block - src + depth // 2 for block in wanted]


def times(values, blocks):
    both = jnp.dot(values, blocks, preferred_element_type=jnp.float32)
    rows, width = both.shape[0] // 2, both.shape[1] // 2
    return both[:rows, :width] - both[rows:, width:], both[:rows, width:] + both[rows:, :width]


def rows_of(panel):
    return panel[...].reshape(2 * panel.shape[1], panel.shape[2])


def product(window, aperture_ref, panels, late_in_two=None, late=None):
    blocks = []
    for m, panel in panels.items():
        entries = slot_entries(aperture_ref, m, panel.shape[-1] // BLK, window.shape[0])
        blocks += [window[k] for k in entries]
    values = [rows_of(panel) for panel in panels.values()]
    if late_in_two is not None:
        values.append(late_in_two)
        blocks += [window[late]] * 2
    return times(jnp.concatenate(values, axis=1), jnp.concatenate(blocks, axis=0))


def sum_of_late(aperture_ref, panels, late, depth):
    total = None
    for m, panel in panels.items():
        values = rows_of(panel)
        for q, k in enumerate(slot_entries(aperture_ref, m, panel.shape[-1] // BLK, depth)):
            term = values[:, q * BLK : (q + 1) * BLK].astype(jnp.float32) * jnp.where(k == late, 1.0, 0.0)
            total = term if total is None else total + term
    return total


def in_two(total):
    high = total.astype(jnp.bfloat16)
    low = (total - high.astype(jnp.float32)).astype(jnp.bfloat16)
    return jnp.concatenate([high, low], axis=1)


def kernel_a(ats, late, aperture_ref, own_ref, *refs):
    piece_refs = list(refs[:-6])
    windows, sums, parts = refs[-6:-4], refs[-4:-2], refs[-2:]
    for v, (window, at) in enumerate(zip(windows, ats)):
        window[late] = jnp.zeros(window.shape[1:], window.dtype)
        fill_window(window, {k: piece_refs.pop(0).at[index] for k, index in at.items()})
        panels = {0: own_ref.at[v]}
        parts[v][0], parts[v][1] = product(window, aperture_ref, panels)
        sums[v][...] = sum_of_late(aperture_ref, panels, late, window.shape[0])


def kernel_b(late, aperture_ref, late_ref, _, last_window, first_sum, last_sum, first_in, last_in, *refs):
    *panel_refs, window, two, first_part, last_part = refs
    fill_window(window, {late: late_ref.at[0]})
    panels = [{1 + m: ref.at[v] for m, ref in enumerate(panel_refs)} for v in range(2)]
    real, imag = product(window, aperture_ref, panels[0], in_two(first_sum[...]), late)
    first_part[0] = first_in[0] + real
    first_part[1] = first_in[1] + imag
    real, imag = product(last_window, aperture_ref, panels[1])
    last_part[0] = last_in[0] + real
    last_part[1] = last_in[1] + imag
    two[...] = in_two(last_sum[...] + sum_of_late(aperture_ref, panels[1], late, last_window.shape[0]))


def last_kernel(far_half, late, aperture_ref, late_ref, first_window, _, two, first_part, last_part, *refs):
    *panel_refs, out_ref, window, result, sems = refs

    def finish(v, part, real, imag):
        copies = []
        for p, value in enumerate((real, imag)):
            result[v, p] = part[p] + value
            for chunk in range(PIECES):
                rows = pl.ds(chunk * (BLK // PIECES), BLK // PIECES)
                copies.append(
                    pltpu.make_async_copy(result.at[v, p, rows], out_ref.at[v, p, rows], sems.at[v, p, chunk])
                )
                copies[-1].start(priority=1 - v)
        return copies

    panels = [{far_half + m: ref.at[v] for m, ref in enumerate(panel_refs)} for v in range(2)]
    fill_window(window, {late: late_ref.at[0]})
    copies = finish(1, last_part, *product(window, aperture_ref, panels[1], two[...], late))
    copies += finish(0, first_part, *product(first_window, aperture_ref, panels[0]))
    for copy in copies:
        copy.wait()


def spec(space):
    return pl.BlockSpec(memory_space=space)


def cost(share):
    return pl.CostEstimate(flops=int(share * (8 * BLK * BLK * APER * BLK)), bytes_accessed=1 << 20, transcendentals=0)


def limit(megabytes):
    return pltpu.CompilerParams(vmem_limit_bytes=megabytes << 20)


def held(piece, share, *tokens):
    return pl.pallas_call(
        lambda *refs: None,
        out_shape=jax.ShapeDtypeStruct(piece.shape, piece.dtype),
        in_specs=[spec(pl.ANY)] * (1 + len(tokens)),
        out_specs=spec(pl.ANY),
        input_output_aliases={0: 0},
        compiler_params=limit(1),
        cost_estimate=cost(share),
    )(piece, *tokens)


def body(primaries, data, aperture):
    width = data.shape[3]
    line = lax.axis_size("src") == 4
    windows = (line_window if line else hop_window)(data)
    panels, far_panel = gather_panels(primaries, windows[0][-1][0])
    half = len(panels)
    late = 2 if line else len(windows[0]) - 1
    late_pieces = [piece[at : at + 1] for piece, at in (window[late] for window in windows)]
    early = [{k: piece for k, piece in enumerate(window) if k != late} for window in windows]
    vmem, anywhere = spec(pltpu.VMEM), spec(pl.ANY)
    window = jax.ShapeDtypeStruct((len(windows[0]), BLK, 2 * width), jnp.bfloat16)
    total = jax.ShapeDtypeStruct((2 * BLK, BLK), jnp.float32)
    part = jax.ShapeDtypeStruct((2, BLK, width), jnp.float32)

    pieces = [piece for window_pieces in early for piece, _ in window_pieces.values()]
    first, last, first_sum, last_sum, first_part, last_part = pl.pallas_call(
        functools.partial(kernel_a, [{k: at for k, (_, at) in pieces.items()} for pieces in early], late),
        out_shape=[window] * 2 + [total] * 2 + [part] * 2,
        in_specs=[vmem] * (2 + len(pieces)),
        out_specs=[vmem] * 6,
        compiler_params=limit(16),
        cost_estimate=cost(0.1),
    )(aperture, primaries, *pieces)

    far_panel = held(far_panel, 12, first_part)
    handed_on = hand_on(far_panel, first_part)
    first, two, first_part, last_part = pl.pallas_call(
        functools.partial(kernel_b, late),
        out_shape=[window, jax.ShapeDtypeStruct((2 * BLK, 2 * BLK), jnp.bfloat16), part, part],
        in_specs=[vmem] * (8 + half),
        out_specs=[vmem] * 4,
        input_output_aliases={2: 0, 6: 2, 7: 3},
        compiler_params=limit(16),
        cost_estimate=cost(0.1),
    )(aperture, late_pieces[0], first, last, first_sum, last_sum, first_part, last_part, *panels[1:], far_panel)

    return pl.pallas_call(
        functools.partial(last_kernel, half + 1, late),
        out_shape=[jax.ShapeDtypeStruct((2, 2, BLK, width), jnp.float32), window],
        in_specs=[vmem] + [vmem] * (6 + len(handed_on)),
        out_specs=[anywhere, vmem],
        scratch_shapes=[pltpu.VMEM((2, 2, BLK, width), jnp.float32), pltpu.SemaphoreType.DMA((2, 2, PIECES))],
        input_output_aliases={3: 1},
        compiler_params=limit(16),
        cost_estimate=cost(1),
    )(aperture, held(late_pieces[1], 12, two), first, last, two, first_part, last_part, *handed_on)[0]


def solution(mesh):
    placed = (P("freq", None, "src", "rcv"), P("freq", None, "src", "rcv"), P())
    return jax.shard_map(
        body, mesh=mesh, in_specs=placed, out_specs=P("freq", None, "src", "rcv"), check_vma=False
    )
```
